32 devices in a mesh: pu: 4 (over y, core), pv: 8 (over z, x).
Axes of the slice: x: 2, y: 2, z: 4, core: 2. Of those that a mesh axis runs over, the one named last changes fastest.
Arguments:
- density: bfloat16 [24, 48, 128, 768], P('pu', 'pv'), may hold values from -6 to 6
- near_blocks: bfloat16 [24, 48, 6, 128, 128], P('pu', 'pv'), may hold values from -0.21875 to 0.21875
- neighbours: int32 [24, 48, 6], P('pu', 'pv'), may hold values from 0 to 9
- far_right: bfloat16 [24, 48, 128, 128], P('pu', 'pv'), may hold values from -0.09375 to 0.09375
- far_left: float32 [4, 8, 1024, 128], P('pu', 'pv'), may hold values from -0.1875 to 0.1875
- sketch: float32 [256, 128], replicated, may hold values from -0.375 to 0.375
- patch_order: int32 [32], replicated, may hold values from 0 to 31, each once
Outputs:
- corrected: bfloat16 [24, 48, 128, 768], P('pu', 'pv')
- far_field: float32 [1024, 768], P('pu', 'pv')
The draws below stay inside these ranges and needn't reach their ends.
Inputs may be any that keep to these rules, and one draw needn't show every extreme that they name: `neighbours`: entry e < 9 names the block displaced by e // 3 - 1 patch rows and e % 3 - 1 patch columns (e = 4 is the block itself); 9 marks an empty slot. `patch_order`: A permutation of the patches.
All inputs are finite; a program needn't handle non-finite values.
Results may differ from the reference program's by a relative error of at most 0.0028.
Values may be sent and summed in bfloat16 or wider, within the bound.
No kernel may reach another device: no remote copies, remote signals or barrier semaphores. Data moves between devices by JAX's collectives and lax.ppermute only.
A program may use at most 256 MiB of HBM per device.

```python
import jax
import jax.numpy as jnp
from jax import lax

BLK = 64
SLOTS = 6
GU = 6
GV = 6
RHS = 768
OBS = 1024
RANK = 128
NBU = 24
NBV = 48
N_PU = 4
N_PV = 8
DEVICES = 32


def plant(drawn, rng, least, high):
    longest = drawn.shape.index(max(drawn.shape))
    spots = []
    for shift in (0, 1):
        where = [jax.random.randint(jax.random.fold_in(rng, axis), (), 0, length) for axis, length in enumerate(drawn.shape)]
        where[longest] = (where[longest] + shift) % drawn.shape[longest]
        spots.append(tuple(where))
    return drawn.at[spots[0]].set(least).at[spots[1]].set(high)


def levels(own_key, dims, split, least, top_value):
    factor_of = 1.0
    for axis_at, parts in split:
        draws = jax.random.uniform(jax.random.fold_in(jax.random.fold_in(own_key, 6), axis_at), (parts,), jnp.float32, least / len(split), top_value / len(split))
        factor_of = factor_of * jnp.repeat(jnp.exp(draws), dims[axis_at] // parts).reshape((-1,) + (1,) * (len(dims) - 1 - axis_at))
    return factor_of


def scatter_about(key, extent, spread, bound, pieces=(), held_as=jnp.bfloat16):
    drawn = spread * jax.random.normal(key, extent, jnp.float32)
    if pieces:
        drawn = drawn * levels(key, extent, pieces, -0.22, 0.18)
    return jnp.clip(drawn, -bound, bound).astype(held_as)


def setup_inputs(seed: int = 0) -> dict:
    seeds = jax.random.split(jax.random.key(seed), 8)
    density = scatter_about(seeds[0], (NBU, NBV, 2 * BLK, RHS), 1.0, 6.0, ((0, 4), (1, 8)))
    near_blocks = scatter_about(seeds[1], (NBU, NBV, SLOTS, 2 * BLK, 2 * BLK), (2 * BLK * SLOTS) ** -0.5, 0.21875, ((0, 4), (1, 8)))
    neighbours = plant(jax.random.randint(seeds[2], (NBU, NBV, SLOTS), 0, 10), jax.random.fold_in(seeds[2], 1), 0, 9).astype(jnp.int32)
    far_right = scatter_about(seeds[3], (NBU, NBV, 2 * BLK, RANK), (GU * GV * 2 * BLK) ** -0.5, 0.09375, ((0, 4), (1, 8)))
    far_left = scatter_about(seeds[4], (N_PU, N_PV, OBS, RANK), OBS ** -0.5, 0.1875, ((0, 4), (1, 8)), jnp.float32)
    sketch = scatter_about(seeds[5], (2 * RANK, RANK), (2 * RANK) ** -0.5, 0.375, (), jnp.float32)
    patch_order = jax.random.permutation(seeds[6], DEVICES).astype(jnp.int32)
    return dict(density=density, near_blocks=near_blocks, neighbours=neighbours, far_right=far_right, far_left=far_left, sketch=sketch, patch_order=patch_order)


highest = lax.Precision.HIGHEST
empty_slot = 9

def merge_pair(first_left, first_coef, second_left, second_coef, sketch):
    stacked = jnp.concatenate([first_left, second_left], axis=1)
    coeff_pairs = jnp.concatenate([first_coef, second_coef], axis=0)
    gram_matrix = jnp.dot(stacked.T, stacked, precision=highest)
    reduced = jnp.dot(sketch.T, gram_matrix, precision=highest)
    inner_gram = jnp.dot(reduced, sketch, precision=highest)
    inner_gram = 0.5 * (inner_gram + inner_gram.T)
    factor = jnp.linalg.cholesky(inner_gram)
    sketched = jnp.dot(stacked, sketch, precision=highest)
    new_left = lax.linalg.triangular_solve(factor, sketched.T, left_side=True, lower=True).T
    new_coef = lax.linalg.triangular_solve(factor, jnp.dot(reduced, coeff_pairs, precision=highest), left_side=True, lower=True)
    return (new_left, new_coef)

def local_tree(left_stack, coef_stack, group_keys, sketch):
    while left_stack.shape[0] > 1:
        half_count = left_stack.shape[0] // 2
        left_pairs = left_stack.reshape((half_count, 2) + left_stack.shape[1:])
        coef_pairs = coef_stack.reshape((half_count, 2) + coef_stack.shape[1:])
        key_pairs = group_keys.reshape(half_count, 2)
        first_mask = (key_pairs[:, 0] < key_pairs[:, 1])[:, None, None]
        first_left = jnp.where(first_mask, left_pairs[:, 0], left_pairs[:, 1])
        second_left = jnp.where(first_mask, left_pairs[:, 1], left_pairs[:, 0])
        first_coef = jnp.where(first_mask, coef_pairs[:, 0], coef_pairs[:, 1])
        second_coef = jnp.where(first_mask, coef_pairs[:, 1], coef_pairs[:, 0])
        left_stack, coef_stack = jax.vmap(merge_pair, in_axes=(0, 0, 0, 0, None))(first_left, first_coef, second_left, second_coef, sketch)
        group_keys = key_pairs.min(axis=1)
    return (left_stack[0], coef_stack[0])

def reference(density, near_blocks, neighbours, far_right, far_left, sketch, patch_order):
    padded = jnp.pad(density, ((1, 1), (1, 1), (0, 0), (0, 0)))
    col_base = jnp.arange(NBV).astype(jnp.int32)

    def one_row(row_index):
        slab = lax.dynamic_slice_in_dim(padded, row_index, 3, 0)
        blocks_row = lax.dynamic_index_in_dim(near_blocks, row_index, 0, keepdims=False)
        links_row = lax.dynamic_index_in_dim(neighbours, row_index, 0, keepdims=False)
        density_row = lax.dynamic_index_in_dim(density, row_index, 0, keepdims=False)
        summed = jnp.zeros(density_row.shape, jnp.float32)
        for position in range(SLOTS):
            slot_links = links_row[:, position]
            stencil = jnp.minimum(slot_links, 8)
            near_rows = slab[stencil // 3, col_base + stencil % 3]
            product = jnp.einsum('jab,jbr->jar', blocks_row[:, position].astype(jnp.float32), near_rows.astype(jnp.float32))
            summed = summed + jnp.where((slot_links < empty_slot)[:, None, None], product, 0.0)
        return (density_row.astype(jnp.float32) + summed).astype(jnp.bfloat16)
    corrected = lax.map(one_row, jnp.arange(NBU).astype(jnp.int32))

    def patch_coeffs(patch_row):
        rows_here = lax.dynamic_slice_in_dim(corrected, patch_row * GU, GU, 0).reshape(GU, N_PV, GV, 2 * BLK, RHS)
        right_here = lax.dynamic_slice_in_dim(far_right, patch_row * GU, GU, 0).reshape(GU, N_PV, GV, 2 * BLK, RANK)
        return jnp.einsum('ivjar,ivjak->vrk', right_here.astype(jnp.float32), rows_here.astype(jnp.float32))
    coeffs = lax.map(patch_coeffs, jnp.arange(N_PU).astype(jnp.int32))
    key_grid = patch_order.reshape(N_PU, N_PV)
    row_left, row_coef = jax.vmap(local_tree, in_axes=(0, 0, 0, None))(far_left, coeffs, key_grid, sketch)
    root_left, root_coef = local_tree(row_left, row_coef, key_grid.min(axis=1), sketch)
    far_field = jnp.dot(root_left, root_coef, precision=highest)
    return (corrected, far_field)
```

```python
import functools

import jax
import jax.numpy as jnp
from jax import lax
from jax.experimental import pallas as pl
from jax.experimental.pallas import tpu as pltpu
from jax.sharding import PartitionSpec as P

high = lax.Precision.HIGH
empty_slot = 9
vmem_bytes = 48 * 1024 * 1024


def dot_t(a, b, dims, precision=None):
    return lax.dot_general(
        a, b, (dims, ((), ())), precision=precision, preferred_element_type=jnp.float32
    )


def split_dot(a, b, dims):
    return dot_t(a, b, dims, high)


def near_kernel(spans, centre_base, centre_step, n_src, nb_ref, *refs):
    srcs = refs[:n_src]
    near_ref, right_ref = refs[n_src : n_src + 2]
    out_ref, coef_ref, ext_ref, sems = refs[-4:]
    i = pl.program_id(0)
    j = pl.program_id(1)
    rows = ext_ref.shape[0]

    def copies(row):
        found = []
        for index, (source, at, ext_row, ext_col, width) in enumerate(spans):
            if ext_row != row:
                continue
            view = srcs[source]
            for step in at:
                view = view.at[step]
            found.append(
                pltpu.make_async_copy(
                    view, ext_ref.at[ext_row, pl.ds(ext_col, width)], sems.at[index]
                )
            )
        return found

    first = jnp.logical_and(i == 0, j == 0)

    @pl.when(first)
    def _():
        for row in range(rows):
            for copy in copies(row):
                copy.start()
        coef_ref[...] = jnp.zeros_like(coef_ref)
        for row in range(2):
            for copy in copies(row):
                copy.wait()

    for row in range(2, rows):

        @pl.when(jnp.logical_and(j == 0, i == row - 2))
        def _():
            for copy in copies(row):
                copy.wait()

    centre = centre_base + centre_step * j
    total = ext_ref[i + 1, centre].astype(jnp.float32)
    slots = near_ref.shape[2]
    col = centre_base + centre_step * j if centre_step == 1 else j * (nb_ref.shape[1] - 1)
    for slot in range(0, slots, 2):
        weights = []
        values = []
        for part in range(slot, min(slot + 2, slots)):
            link = nb_ref[i, col, part]
            place = jnp.minimum(link, empty_slot - 1)
            weight = near_ref[0, 0, part]
            weights.append(jnp.where(link < empty_slot, weight, jnp.zeros_like(weight)))
            values.append(ext_ref[i + lax.div(place, 3), centre - 1 + lax.rem(place, 3)])
        total = total + jnp.dot(
            jnp.concatenate(weights, axis=1),
            jnp.concatenate(values, axis=0),
            preferred_element_type=jnp.float32,
        )
    corrected = total.astype(jnp.bfloat16)
    out_ref[0, 0] = corrected
    coef_ref[...] += dot_t(right_ref[0, 0], corrected, ((0,), (0,)))


def near_part(sources, spans, ext_cols, centre, column, n_cols, near_blocks, far_right, neighbours, prior):
    gu, gv, slots, size, _ = near_blocks.shape
    rhs = sources[0].shape[-1]
    rank = far_right.shape[-1]
    kernel = functools.partial(near_kernel, spans, centre[0], centre[1], len(sources))
    block = pl.BlockSpec((1, 1, size, rhs), lambda i, j, nb: (i, column(j), 0, 0))
    in_specs = [pl.BlockSpec(memory_space=pl.ANY)] * len(sources) + [
        pl.BlockSpec((1, 1, slots, size, size), lambda i, j, nb: (i, column(j), 0, 0, 0)),
        pl.BlockSpec((1, 1, size, rank), lambda i, j, nb: (i, column(j), 0, 0)),
    ]
    args = list(sources) + [near_blocks, far_right]
    aliases = {}
    if prior is not None:
        in_specs.append(pl.BlockSpec(memory_space=pl.ANY))
        args.append(prior)
        aliases = {len(args): 0}
    return pl.pallas_call(
        kernel,
        grid_spec=pltpu.PrefetchScalarGridSpec(
            num_scalar_prefetch=1,
            grid=(gu, n_cols),
            in_specs=in_specs,
            out_specs=[block, pl.BlockSpec((rank, rhs), lambda i, j, nb: (0, 0))],
            scratch_shapes=[
                pltpu.VMEM((gu + 2, ext_cols, size, rhs), jnp.bfloat16),
                pltpu.SemaphoreType.DMA((len(spans),)),
            ],
        ),
        out_shape=[
            jax.ShapeDtypeStruct((gu, gv, size, rhs), jnp.bfloat16),
            jax.ShapeDtypeStruct((rank, rhs), jnp.float32),
        ],
        input_output_aliases=aliases,
        compiler_params=pltpu.CompilerParams(
            dimension_semantics=("arbitrary", "arbitrary"), vmem_limit_bytes=vmem_bytes
        ),
    )(neighbours, *args)


def near_inner(density, top, bottom, near_blocks, far_right, neighbours):
    gu, gv = density.shape[:2]
    spans = [(1, (0,), 0, 0, gv)]
    spans += [(0, (row,), row + 1, 0, gv) for row in range(gu)]
    spans += [(2, (0,), gu + 1, 0, gv)]
    return near_part(
        (density, top, bottom), spans, gv, (1, 1), lambda j: j + 1, gv - 2, near_blocks, far_right, neighbours, None
    )


def near_outer(density, top, bottom, left, right, corner_top, corner_bottom, near_blocks, far_right, neighbours, prior):
    gu, gv = density.shape[:2]
    spans = []
    for ext_row, source, at in (
        [(0, 1, (0,))] + [(row + 1, 0, (row,)) for row in range(gu)] + [(gu + 1, 2, (0,))]
    ):
        spans.append((source, at + (pl.ds(0, 2),), ext_row, 1, 2))
        spans.append((source, at + (pl.ds(gv - 2, 2),), ext_row, 3, 2))
    for row in range(gu):
        spans.append((3, (row,), row + 1, 0, 1))
        spans.append((4, (row,), row + 1, 5, 1))
    for source, ext_row in ((5, 0), (6, gu + 1)):
        spans.append((source, (pl.ds(0, 1),), ext_row, 0, 1))
        spans.append((source, (pl.ds(1, 1),), ext_row, 5, 1))
    return near_part(
        (density, top, bottom, left, right, corner_top, corner_bottom),
        spans,
        6,
        (1, 3),
        lambda j: j * (gv - 1),
        2,
        near_blocks,
        far_right,
        neighbours,
        prior,
    )


def eliminate(w_k, w_e):
    size = w_k.shape[0]
    step = 32
    tile = 8
    sub = lax.broadcasted_iota(jnp.int32, (tile, size), 0)
    for base in range(0, size, step):
        count = step // tile
        k_rows = [w_k[base + tile * r : base + tile * (r + 1), :] for r in range(count)]
        e_rows = [w_e[base + tile * r : base + tile * (r + 1), :] for r in range(count)]
        for q in range(count):
            at = base + tile * q
            cols = {
                (r, k): jnp.broadcast_to(k_rows[r][:, at + k : at + k + 1], (tile, size))
                for r in range(q, count)
                for k in range(tile)
            }
            pivots = jnp.ones((tile, size), jnp.float32)
            for k in range(tile):
                pivot = jnp.broadcast_to(cols[q, k][k : k + 1, :], (tile, size))
                pivots = jnp.where(sub == k, pivot, pivots)
                inverse = 1.0 / pivot
                k_pivot = jnp.broadcast_to(k_rows[q][k : k + 1, :], (tile, size)) * inverse
                e_pivot = jnp.broadcast_to(e_rows[q][k : k + 1, :], (tile, size)) * inverse
                links = {
                    m: jnp.broadcast_to(cols[q, k][m : m + 1, :], (tile, size)) * inverse
                    for m in range(k + 1, tile)
                }
                for r in range(q, count):
                    factor = cols[r, k]
                    if r == q:
                        factor = jnp.where(sub > k, factor, 0.0)
                    for m in range(k + 1, tile):
                        cols[r, m] = cols[r, m] - factor * links[m]
                    k_rows[r] = k_rows[r] - factor * k_pivot
                    e_rows[r] = e_rows[r] - factor * e_pivot
            root = lax.rsqrt(pivots)
            k_rows[q] = k_rows[q] * root
            e_rows[q] = e_rows[q] * root
        e_now = jnp.concatenate(e_rows, axis=0)
        w_e[base : base + step, :] = e_now
        if base + step < size:
            k_now = jnp.concatenate(k_rows, axis=0)
            k_hi = k_now.astype(jnp.bfloat16)
            k_lo = (k_now - k_hi.astype(jnp.float32)).astype(jnp.bfloat16)
            e_hi = e_now.astype(jnp.bfloat16)
            e_lo = (e_now - e_hi.astype(jnp.float32)).astype(jnp.bfloat16)
            lhs = jnp.concatenate([k_hi, k_hi, k_lo], axis=0)
            k_rhs = jnp.concatenate([k_hi, k_lo, k_hi], axis=0)
            e_rhs = jnp.concatenate([e_hi, e_lo, e_hi], axis=0)
            k_fall = dot_t(lhs, k_rhs, ((0,), (0,)))
            e_fall = dot_t(lhs, e_rhs, ((0,), (0,)))
            w_k[base + step :, :] -= k_fall[base + step :, :]
            w_e[base + step :, :] -= e_fall[base + step :, :]


def merge_kernel(lead_ref, mine_ref, other_ref, sketch_ref, path_ref, left_ref, new_path_ref, w_k, w_e):
    rank = mine_ref.shape[1]
    lead = lead_ref[0] > 0
    first = sketch_ref[:rank, :]
    second = sketch_ref[rank:, :]
    mine = mine_ref[...]
    sketched = split_dot(mine, jnp.where(lead, first, second), ((1,), (0,))) + split_dot(
        other_ref[...], jnp.where(lead, second, first), ((1,), (0,))
    )
    w_k[...] = split_dot(sketched, sketched, ((0,), (0,)))
    rows = lax.broadcasted_iota(jnp.int32, (rank, rank), 0)
    cols = lax.broadcasted_iota(jnp.int32, (rank, rank), 1)
    w_e[...] = jnp.where(rows == cols, 1.0, 0.0)
    eliminate(w_k, w_e)
    inverse = w_e[...]
    left_ref[...] = split_dot(sketched, inverse, ((1,), (1,)))
    own = split_dot(sketched, mine, ((0,), (0,)))
    new_path_ref[...] = split_dot(inverse, split_dot(own, path_ref[...], ((1,), (0,))), ((1,), (0,)))


def merge(lead, mine, other, sketch, path):
    rows, rank = mine.shape
    whole = pl.BlockSpec(memory_space=pltpu.VMEM)
    return pl.pallas_call(
        merge_kernel,
        in_specs=[pl.BlockSpec(memory_space=pltpu.SMEM), whole, whole, whole, whole],
        out_specs=[whole, whole],
        out_shape=[
            jax.ShapeDtypeStruct((rows, rank), jnp.float32),
            jax.ShapeDtypeStruct((rank, rank), jnp.float32),
        ],
        scratch_shapes=[pltpu.VMEM((rank, rank), jnp.float32), pltpu.VMEM((rank, rank), jnp.float32)],
        compiler_params=pltpu.CompilerParams(vmem_limit_bytes=vmem_bytes),
    )(lead, mine, other, sketch, path)


def from_partner(value, axis, distance):
    mask = 2**distance
    pairs = [(source, source ^ mask) for source in range(lax.axis_size(axis))]
    return lax.ppermute(value, axis, pairs)


def mine_leads(group_keys, position, tree_level):
    block_min = group_keys.reshape(-1, 1 << tree_level).min(axis=1)
    mine_key = block_min[position >> tree_level]
    their_key = block_min[position >> tree_level ^ 1]
    return (mine_key < their_key).astype(jnp.int32).reshape(1)


def shifted(value, axis, by):
    count = lax.axis_size(axis)
    return lax.ppermute(value, axis, [(i, i + by) for i in range(count) if 0 <= i + by < count])


def per_device(density, near_blocks, neighbours, far_right, far_left, sketch, patch_order):
    pu_count = lax.axis_size("pu")
    pv_count = lax.axis_size("pv")
    pu_index = lax.axis_index("pu")
    pv_index = lax.axis_index("pv")
    key_grid = patch_order.reshape(pu_count, pv_count)
    row_keys = lax.dynamic_index_in_dim(key_grid, pu_index, 0, keepdims=False)
    column_keys = key_grid.min(axis=1)
    gu, gv, size, rhs = density.shape

    left_now = far_left[0, 0]
    rank = left_now.shape[1]
    path = jnp.eye(rank, dtype=jnp.float32)
    other = from_partner(left_now, "pv", 0)

    left = shifted(density[:, gv - 1 :], "pv", 1)
    right = shifted(density[:, :1], "pv", -1)
    top = shifted(density[gu - 1 :], "pu", 1)
    bottom = shifted(density[:1], "pu", -1)

    corrected, inner_coef = near_inner(density, top, bottom, near_blocks, far_right, neighbours)

    corner_top = shifted(jnp.concatenate([left[gu - 1], right[gu - 1]], axis=0), "pu", 1)
    corner_bottom = shifted(jnp.concatenate([left[0], right[0]], axis=0), "pu", -1)

    pv_levels = pv_count.bit_length() - 1
    pu_levels = pu_count.bit_length() - 1
    for level in range(pv_levels + pu_levels):
        if level < pv_levels:
            lead = mine_leads(row_keys, pv_index, level)
            if level:
                other = from_partner(left_now, "pv", level)
        else:
            lead = mine_leads(column_keys, pu_index, level - pv_levels)
            other = from_partner(left_now, "pu", level - pv_levels)
        left_now, path = merge(lead, left_now, other, sketch, path)

    corrected, outer_coef = near_outer(
        density, top, bottom, left, right, corner_top, corner_bottom, near_blocks, far_right, neighbours, corrected
    )
    coef = inner_coef + outer_coef
    share = lax.dot_general(coef, path, (((0,), (1,)), ((), ())), precision=high)
    chunks = lax.all_to_all(share.reshape(pv_count, rhs // pv_count, rank), "pv", 0, 0)
    root_coef = chunks.sum(axis=0)
    for level in range(pu_levels):
        root_coef = root_coef + from_partner(root_coef, "pu", level)
    obs_rows = left_now.shape[0] // pu_count
    left_rows = lax.dynamic_slice_in_dim(left_now, pu_index * obs_rows, obs_rows, 0)
    far_field = lax.dot_general(left_rows, root_coef, (((1,), (1,)), ((), ())), precision=high)
    return (corrected, far_field)


def solution(mesh):
    in_specs = (
        P("pu", "pv", None, None),
        P("pu", "pv", None, None, None),
        P("pu", "pv", None),
        P("pu", "pv", None, None),
        P("pu", "pv", None, None),
        P(),
        P(),
    )
    out_specs = (P("pu", "pv", None, None), P("pu", "pv"))
    return jax.shard_map(
        per_device, mesh=mesh, in_specs=in_specs, out_specs=out_specs, check_vma=False
    )
```

```python
import functools

import jax
import jax.numpy as jnp
from jax import lax
from jax.experimental import pallas as pl
from jax.experimental.pallas import tpu as pltpu
from jax.sharding import PartitionSpec as P

high = lax.Precision.HIGH
empty_slot = 9
near_vmem = 32 * 1024 * 1024
merge_vmem = 12 * 1024 * 1024


def dot_t(a, b, dims, precision=None):
    return lax.dot_general(
        a, b, (dims, ((), ())), precision=precision, preferred_element_type=jnp.float32
    )


def split_dot(a, b, dims):
    return dot_t(a, b, dims, high)


def near_kernel(plan, n_src, nb_ref, *refs):
    spans, wanted, block_rows, block_cols, centre_rows, centre_cols = plan
    count = len(block_cols)
    srcs = refs[:n_src]
    near_refs = refs[n_src : n_src + count]
    right_refs = refs[n_src + count : n_src + 2 * count]
    out_ref, coef_ref, ext_ref, stage_ref, sems, out_sems = refs[-6:]
    step = pl.program_id(0)
    steps = len(block_rows)

    def copies(row):
        found = []
        for index, (source, at, ext_row, ext_col, width) in enumerate(spans):
            if ext_row == row:
                view = srcs[source]
                for part in at:
                    view = view.at[part]
                target = ext_ref.at[ext_row, pl.ds(ext_col, width)]
                found.append(pltpu.make_async_copy(view, target, sems.at[index]))
        return found

    def send(place, at_step, part):
        row = block_rows[0] + at_step * (block_rows[1] - block_rows[0])
        return pltpu.make_async_copy(
            stage_ref.at[place, part], out_ref.at[row, block_cols[part]], out_sems.at[place, part]
        )

    @pl.when(step == 0)
    def _():
        for row in range(ext_ref.shape[0]):
            for copy in copies(row):
                copy.start()
        coef_ref[...] = jnp.zeros_like(coef_ref)

    for at_step, rows in enumerate(wanted):

        @pl.when(step == at_step)
        def _():
            for row in rows:
                for copy in copies(row):
                    copy.wait()

    place = lax.rem(step, 2)

    @pl.when(step >= 2)
    def _():
        for part in range(count):
            send(place, step - 2, part).wait()

    row = block_rows[0] + step * (block_rows[1] - block_rows[0])
    centre = centre_rows[0] + step * (centre_rows[1] - centre_rows[0])
    coef = coef_ref[...]
    for part in range(count):
        near_ref = near_refs[part]
        middle = centre_cols[part]
        weights = []
        values = []
        for slot in range(near_ref.shape[2]):
            link = nb_ref[row, block_cols[part], slot]
            there = jnp.minimum(link, empty_slot - 1)
            weight = near_ref[0, 0, slot]
            weights.append(jnp.where(link < empty_slot, weight, jnp.zeros_like(weight)))
            values.append(ext_ref[centre - 1 + lax.div(there, 3), middle - 1 + lax.rem(there, 3)])
        total = jnp.dot(
            jnp.concatenate(weights, axis=1),
            jnp.concatenate(values, axis=0),
            preferred_element_type=jnp.float32,
        )
        corrected = (ext_ref[centre, middle].astype(jnp.float32) + total).astype(jnp.bfloat16)
        stage_ref[place, part] = corrected
        send(place, step, part).start()
        coef = coef + dot_t(right_refs[part][0, 0], corrected, ((0,), (0,)))
    coef_ref[...] = coef

    @pl.when(step == steps - 1)
    def _():
        for at_step in range(max(steps - 2, 0), steps):
            for part in range(count):
                send(at_step % 2, at_step, part).wait()


def near_part(sources, plan, near_blocks, far_right, neighbours, prior):
    spans, _, block_rows, block_cols, _, _ = plan
    gu, gv, slots, size, _ = near_blocks.shape
    rhs = sources[0].shape[-1]
    rank = far_right.shape[-1]
    ext_rows = 1 + max(span[2] for span in spans)
    ext_cols = max(span[3] + span[4] for span in spans)
    at, by = block_rows[0], block_rows[1] - block_rows[0]
    in_specs = [pl.BlockSpec(memory_space=pl.ANY)] * len(sources)
    in_specs += [
        pl.BlockSpec((1, 1, slots, size, size), lambda i, nb, col=col: (at + i * by, col, 0, 0, 0))
        for col in block_cols
    ]
    in_specs += [
        pl.BlockSpec((1, 1, size, rank), lambda i, nb, col=col: (at + i * by, col, 0, 0))
        for col in block_cols
    ]
    args = list(sources) + [near_blocks] * len(block_cols) + [far_right] * len(block_cols)
    aliases = {}
    if prior is not None:
        in_specs.append(pl.BlockSpec(memory_space=pl.ANY))
        args.append(prior)
        aliases = {len(args): 0}
    return pl.pallas_call(
        functools.partial(near_kernel, plan, len(sources)),
        grid_spec=pltpu.PrefetchScalarGridSpec(
            num_scalar_prefetch=1,
            grid=(len(block_rows),),
            in_specs=in_specs,
            out_specs=[
                pl.BlockSpec(memory_space=pl.ANY),
                pl.BlockSpec((rank, rhs), lambda i, nb: (0, 0)),
            ],
            scratch_shapes=[
                pltpu.VMEM((ext_rows, ext_cols, size, rhs), jnp.bfloat16),
                pltpu.VMEM((2, len(block_cols), size, rhs), jnp.bfloat16),
                pltpu.SemaphoreType.DMA((len(spans),)),
                pltpu.SemaphoreType.DMA((2, len(block_cols))),
            ],
        ),
        out_shape=[
            jax.ShapeDtypeStruct((gu, gv, size, rhs), jnp.bfloat16),
            jax.ShapeDtypeStruct((rank, rhs), jnp.float32),
        ],
        input_output_aliases=aliases,
        compiler_params=pltpu.CompilerParams(
            dimension_semantics=("arbitrary",), vmem_limit_bytes=near_vmem
        ),
    )(neighbours, *args)


def near_middle(density, near_blocks, far_right, neighbours, prior):
    gu, gv = density.shape[:2]
    spans = [(0, (row,), row, 0, gv) for row in range(gu)]
    rows = list(range(1, gu - 1))
    wanted = [(0, 1, 2)] + [(row + 1,) for row in rows[1:]]
    cols = list(range(1, gv - 1))
    plan = (spans, wanted, rows, cols, rows, cols)
    return near_part((density,), plan, near_blocks, far_right, neighbours, prior)


def near_rows(density, top, bottom, near_blocks, far_right, neighbours, prior):
    gu, gv = density.shape[:2]
    spans = [(1, (), 0, 0, gv)]
    spans += [(0, (row,), at, 0, gv) for at, row in ((1, 0), (2, 1), (3, gu - 2), (4, gu - 1))]
    spans += [(2, (), 5, 0, gv)]
    cols = list(range(1, gv - 1))
    plan = (spans, [(0, 1, 2), (3, 4, 5)], [0, gu - 1], cols, [1, 4], cols)
    return near_part((density, top, bottom), plan, near_blocks, far_right, neighbours, prior)


def near_cols(density, top, bottom, ends, mids, corner_top, corner_bottom, near_blocks, far_right, neighbours, prior):
    gu, gv = density.shape[:2]
    spans = []
    for ext_row, source, at in (
        [(0, 1, ())] + [(row + 1, 0, (row,)) for row in range(gu)] + [(gu + 1, 2, ())]
    ):
        spans.append((source, at + (pl.ds(0, 2),), ext_row, 1, 2))
        spans.append((source, at + (pl.ds(gv - 2, 2),), ext_row, 3, 2))
    for side in range(2):
        col = 5 * side
        for row in range(gu):
            if row in (0, gu - 1):
                spans.append((3 + side, (pl.ds(0 if row == 0 else 1, 1),), row + 1, col, 1))
            else:
                spans.append((5 + side, (pl.ds(row - 1, 1),), row + 1, col, 1))
        spans.append((7, (pl.ds(side, 1),), 0, col, 1))
        spans.append((8, (pl.ds(side, 1),), gu + 1, col, 1))
    rows = list(range(gu))
    wanted = [(0, 1, 2)] + [(row + 2,) for row in rows[1:]]
    plan = (spans, wanted, rows, [0, gv - 1], [row + 1 for row in rows], [1, 4])
    sources = (density, top, bottom, *ends, *mids, corner_top, corner_bottom)
    return near_part(sources, plan, near_blocks, far_right, neighbours, prior)


def edges_kernel(density, *refs):
    *outs, sems = refs
    gu, gv = density.shape[:2]
    copies = []
    for side, col in ((0, gv - 1), (1, 0)):
        copies.append((density.at[0, pl.ds(col, 1)], outs[side].at[pl.ds(0, 1)]))
        copies.append((density.at[gu - 1, pl.ds(col, 1)], outs[side].at[pl.ds(1, 1)]))
        copies.append((density.at[pl.ds(1, gu - 2), col], outs[2 + side]))
    copies.append((density.at[gu - 1], outs[4]))
    copies.append((density.at[0], outs[5]))
    copies = [
        pltpu.make_async_copy(source, target, sems.at[index])
        for index, (source, target) in enumerate(copies)
    ]
    for copy in copies:
        copy.start()
    for copy in copies:
        copy.wait()


def patch_edges(density):
    gu, gv, size, rhs = density.shape
    counts = (2, 2, gu - 2, gu - 2, gv, gv)
    return pl.pallas_call(
        edges_kernel,
        in_specs=[pl.BlockSpec(memory_space=pl.ANY)],
        out_specs=[pl.BlockSpec(memory_space=pl.ANY)] * len(counts),
        out_shape=[jax.ShapeDtypeStruct((count, size, rhs), density.dtype) for count in counts],
        scratch_shapes=[pltpu.SemaphoreType.DMA((8,))],
    )(density)


def eliminate(w_k, w_e):
    size = w_k.shape[0]
    step = 32
    tile = 8
    sub = lax.broadcasted_iota(jnp.int32, (tile, size), 0)
    for base in range(0, size, step):
        count = step // tile
        k_rows = [w_k[base + tile * r : base + tile * (r + 1), :] for r in range(count)]
        e_rows = [w_e[base + tile * r : base + tile * (r + 1), :] for r in range(count)]
        for q in range(count):
            at = base + tile * q
            cols = {
                (r, k): jnp.broadcast_to(k_rows[r][:, at + k : at + k + 1], (tile, size))
                for r in range(q, count)
                for k in range(tile)
            }
            pivots = jnp.ones((tile, size), jnp.float32)
            for k in range(tile):
                pivot = jnp.broadcast_to(cols[q, k][k : k + 1, :], (tile, size))
                pivots = jnp.where(sub == k, pivot, pivots)
                inverse = 1.0 / pivot
                k_pivot = jnp.broadcast_to(k_rows[q][k : k + 1, :], (tile, size)) * inverse
                e_pivot = jnp.broadcast_to(e_rows[q][k : k + 1, :], (tile, size)) * inverse
                links = {
                    m: jnp.broadcast_to(cols[q, k][m : m + 1, :], (tile, size)) * inverse
                    for m in range(k + 1, tile)
                }
                for r in range(q, count):
                    factor = cols[r, k]
                    if r == q:
                        factor = jnp.where(sub > k, factor, 0.0)
                    for m in range(k + 1, tile):
                        cols[r, m] = cols[r, m] - factor * links[m]
                    k_rows[r] = k_rows[r] - factor * k_pivot
                    e_rows[r] = e_rows[r] - factor * e_pivot
            root = lax.rsqrt(pivots)
            k_rows[q] = k_rows[q] * root
            e_rows[q] = e_rows[q] * root
        e_now = jnp.concatenate(e_rows, axis=0)
        w_e[base : base + step, :] = e_now
        if base + step < size:
            k_now = jnp.concatenate(k_rows, axis=0)
            k_hi = k_now.astype(jnp.bfloat16)
            k_lo = (k_now - k_hi.astype(jnp.float32)).astype(jnp.bfloat16)
            e_hi = e_now.astype(jnp.bfloat16)
            e_lo = (e_now - e_hi.astype(jnp.float32)).astype(jnp.bfloat16)
            lhs = jnp.concatenate([k_hi, k_hi, k_lo], axis=0)
            k_rhs = jnp.concatenate([k_hi, k_lo, k_hi], axis=0)
            e_rhs = jnp.concatenate([e_hi, e_lo, e_hi], axis=0)
            k_fall = dot_t(lhs, k_rhs, ((0,), (0,)))
            e_fall = dot_t(lhs, e_rhs, ((0,), (0,)))
            w_k[base + step :, :] -= k_fall[base + step :, :]
            w_e[base + step :, :] -= e_fall[base + step :, :]


code_rows = 16


def encode(value, out_ref):
    rows = value.shape[0]
    top = jnp.max(jnp.abs(value), axis=0, keepdims=True)
    power = jnp.clip(jnp.floor(jnp.log2(32000.0 / jnp.maximum(top, 1e-30))), -60.0, 60.0)
    scaled = jnp.floor(value * jnp.exp2(power) + 0.5)
    out_ref[:rows, :] = scaled.astype(jnp.int32).astype(jnp.int16)
    powers = jnp.broadcast_to(power, (code_rows, value.shape[1]))
    out_ref[rows:, :] = powers.astype(jnp.int32).astype(jnp.int16)


def decode(ref):
    rows = ref.shape[0] - code_rows
    power = ref[rows:, :].astype(jnp.int32).astype(jnp.float32)[:1]
    return ref[:rows, :].astype(jnp.int32).astype(jnp.float32) * jnp.exp2(-power)


def encode_kernel(value_ref, out_ref):
    encode(value_ref[...], out_ref)


def encoded(value):
    rows, cols = value.shape
    return pl.pallas_call(
        encode_kernel,
        out_shape=jax.ShapeDtypeStruct((rows + code_rows, cols), jnp.int16),
        compiler_params=pltpu.CompilerParams(vmem_limit_bytes=merge_vmem),
    )(value)


def merge_kernel(has_path, last, info_ref, mine_ref, other_ref, sketch_ref, *refs):
    if has_path:
        path_ref, *refs = refs
    left_ref, new_path_ref, w_k, w_e, y_ref = refs
    rank = mine_ref.shape[1]
    lead = info_ref[0] > 0
    first = sketch_ref[:rank, :]
    second = sketch_ref[rank:, :]
    mine = decode(mine_ref)
    sketched = split_dot(mine, jnp.where(lead, first, second), ((1,), (0,))) + split_dot(
        decode(other_ref), jnp.where(lead, second, first), ((1,), (0,))
    )
    w_k[...] = split_dot(sketched, sketched, ((0,), (0,)))
    rows = lax.broadcasted_iota(jnp.int32, (rank, rank), 0)
    cols = lax.broadcasted_iota(jnp.int32, (rank, rank), 1)
    w_e[...] = jnp.where(rows == cols, 1.0, 0.0)
    eliminate(w_k, w_e)
    inverse = w_e[...]
    if last:
        y_ref[...] = sketched
        count = left_ref.shape[0]
        part = y_ref[pl.ds(pl.multiple_of(info_ref[1] * count, 8), count), :]
        left_ref[...] = split_dot(part, inverse, ((1,), (1,)))
    else:
        encode(split_dot(sketched, inverse, ((1,), (1,))), left_ref)
    own = split_dot(sketched, mine, ((0,), (0,)))
    if has_path:
        own = split_dot(own, path_ref[...], ((1,), (0,)))
    new_path_ref[...] = split_dot(inverse, own, ((1,), (0,)))


def merge(info, mine, other, sketch, path, last_rows):
    rows, rank = mine.shape
    whole = pl.BlockSpec(memory_space=pltpu.VMEM)
    paths = () if path is None else (path,)
    if last_rows:
        left = jax.ShapeDtypeStruct((last_rows, rank), jnp.float32)
    else:
        left = jax.ShapeDtypeStruct(mine.shape, jnp.int16)
    return pl.pallas_call(
        functools.partial(merge_kernel, bool(paths), bool(last_rows)),
        in_specs=[pl.BlockSpec(memory_space=pltpu.SMEM), whole, whole, whole] + [whole] * len(paths),
        out_specs=[whole, whole],
        out_shape=[left, jax.ShapeDtypeStruct((rank, rank), jnp.float32)],
        scratch_shapes=[
            pltpu.VMEM((rank, rank), jnp.float32),
            pltpu.VMEM((rank, rank), jnp.float32),
            pltpu.VMEM((rows - code_rows, rank), jnp.float32),
        ],
        compiler_params=pltpu.CompilerParams(vmem_limit_bytes=merge_vmem),
    )(info, mine, other, sketch, *paths)


def from_partner(value, axis, distance):
    mask = 2**distance
    pairs = [(source, source ^ mask) for source in range(lax.axis_size(axis))]
    return lax.ppermute(value, axis, pairs)


def mine_leads(group_keys, position, tree_level):
    block_min = group_keys.reshape(-1, 1 << tree_level).min(axis=1)
    mine_key = block_min[position >> tree_level]
    their_key = block_min[position >> tree_level ^ 1]
    return (mine_key < their_key).astype(jnp.int32).reshape(1)


def shifted(value, axis, by):
    count = lax.axis_size(axis)
    return lax.ppermute(value, axis, [(i, i + by) for i in range(count) if 0 <= i + by < count])


def tied(*values):
    return lax.optimization_barrier(values)


def per_device(density, near_blocks, neighbours, far_right, far_left, sketch, patch_order):
    pu_count = lax.axis_size("pu")
    pv_count = lax.axis_size("pv")
    pu_index = lax.axis_index("pu")
    pv_index = lax.axis_index("pv")
    key_grid = patch_order.reshape(pu_count, pv_count)
    row_keys = lax.dynamic_index_in_dim(key_grid, pu_index, 0, keepdims=False)
    column_keys = key_grid.min(axis=1)
    gu, gv, size, rhs = density.shape
    pv_levels = pv_count.bit_length() - 1
    pu_levels = pu_count.bit_length() - 1
    levels = pv_levels + pu_levels
    place = pu_index.astype(jnp.int32).reshape(1)

    def info(level):
        if level < pv_levels:
            lead = mine_leads(row_keys, pv_index, level)
        else:
            lead = mine_leads(column_keys, pu_index, level - pv_levels)
        return jnp.concatenate([lead, place])

    def partner(value, level):
        if level < pv_levels:
            return from_partner(value, "pv", level)
        return from_partner(value, "pu", level - pv_levels)

    rows = far_left.shape[2]
    left = encoded(far_left[0, 0])
    other = partner(left, 0)
    density, left = tied(density, left)
    *columns, last_row, first_row = patch_edges(density)
    top = shifted(last_row, "pu", 1)
    bottom = shifted(first_row, "pu", -1)
    columns, other = tied(columns, other)
    ends = [shifted(columns[0], "pv", 1), shifted(columns[1], "pv", -1)]
    mids = [shifted(columns[2], "pv", 1), shifted(columns[3], "pv", -1)]
    corner_top = shifted(jnp.concatenate([ends[0][1:], ends[1][1:]], axis=0), "pu", 1)
    corner_bottom = shifted(jnp.concatenate([ends[0][:1], ends[1][:1]], axis=0), "pu", -1)

    coefs = []
    corrected = None
    pv_path = pu_path = None
    for level in range(levels):
        if level:
            other = partner(left, level)
            if level in (1, 2, levels - 1):
                links, left = tied(neighbours, left)
                if level == 1:
                    corrected, coef = near_rows(density, top, bottom, near_blocks, far_right, links, corrected)
                elif level == 2:
                    corrected, coef = near_middle(density, near_blocks, far_right, links, corrected)
                else:
                    corrected, coef = near_cols(
                        density,
                        top,
                        bottom,
                        ends,
                        mids,
                        corner_top,
                        corner_bottom,
                        near_blocks,
                        far_right,
                        links,
                        corrected,
                    )
                other, coef = tied(other, coef)
                coefs.append(coef)
        path = pv_path if level < pv_levels else pu_path
        last_rows = rows // pu_count if level == levels - 1 else 0
        left, path = merge(info(level), left, other, sketch, path, last_rows)
        if level < pv_levels:
            pv_path = path
        else:
            pu_path = path

    coef = functools.reduce(lambda a, b: a + b, coefs)
    share = lax.dot_general(coef, pv_path, (((0,), (1,)), ((), ())), precision=high)
    share = share.reshape(pv_count, rhs // pv_count, -1)
    for level in range(pv_levels):
        bit = (pv_index >> level) & 1
        pairs = share.reshape(share.shape[0] // 2, 2, *share.shape[1:])
        keep = lax.dynamic_index_in_dim(pairs, bit, 1, keepdims=False)
        give = lax.dynamic_index_in_dim(pairs, 1 - bit, 1, keepdims=False)
        share = keep + from_partner(give, "pv", level)
    root_coef = lax.dot_general(share[0], pu_path, (((1,), (1,)), ((), ())), precision=high)
    for level in range(pu_levels):
        root_coef = root_coef + from_partner(root_coef, "pu", level)
    far_field = lax.dot_general(left, root_coef, (((1,), (1,)), ((), ())), precision=high)
    return (corrected, far_field)


def solution(mesh):
    in_specs = (
        P("pu", "pv", None, None),
        P("pu", "pv", None, None, None),
        P("pu", "pv", None),
        P("pu", "pv", None, None),
        P("pu", "pv", None, None),
        P(),
        P(),
    )
    out_specs = (P("pu", "pv", None, None), P("pu", "pv"))
    return jax.shard_map(
        per_device, mesh=mesh, in_specs=in_specs, out_specs=out_specs, check_vma=False
    )
```

```python
import functools

import jax
import jax.numpy as jnp
from jax import lax
from jax.experimental import pallas as pl
from jax.experimental.pallas import tpu as pltpu
from jax.sharding import PartitionSpec as P

high = lax.Precision.HIGH
empty_slot = 9
near_vmem = 26 * 1024 * 1024
merge_vmem = 12 * 1024 * 1024


def dot_t(a, b, dims, precision=None):
    return lax.dot_general(
        a, b, (dims, ((), ())), precision=precision, preferred_element_type=jnp.float32
    )


def split_dot(a, b, dims):
    return dot_t(a, b, dims, high)


def near_kernel(plan, nb_ref, *refs):
    spans, wanted, block_rows, block_cols, centre_rows, centre_cols = plan
    near_hbm, right_hbm, *srcs = refs[:-8]
    out_ref, coef_ref, ext_ref, near_ref, right_ref, stage_ref, sems, out_sems = refs[-8:]
    count = len(block_cols)
    steps = len(block_rows)
    step = pl.program_id(0)
    together = block_cols == list(range(block_cols[0], block_cols[0] + count))
    groups = [(block_cols[0], 0, count)] if together else [(c, k, 1) for k, c in enumerate(block_cols)]

    def fetch(at_step):
        found = []
        for index, (source, at, ext_row, ext_col, width) in enumerate(spans):
            if ext_row in wanted[at_step]:
                view = srcs[source]
                for part in at:
                    view = view.at[part]
                target = ext_ref.at[ext_row, pl.ds(ext_col, width)]
                found.append(pltpu.make_async_copy(view, target, sems.at[index]))
        base = len(spans) + 2 * at_step * len(groups)
        for index, (col, slot, width) in enumerate(groups):
            row = block_rows[at_step]
            for offset, source, target in ((0, near_hbm, near_ref), (1, right_hbm, right_ref)):
                found.append(
                    pltpu.make_async_copy(
                        source.at[row, pl.ds(col, width)],
                        target.at[at_step, pl.ds(slot, width)],
                        sems.at[base + 2 * index + offset],
                    )
                )
        return found

    def send(place, at_step, part):
        row = block_rows[0] + at_step * (block_rows[1] - block_rows[0])
        return pltpu.make_async_copy(
            stage_ref.at[place, part], out_ref.at[row, block_cols[part]], out_sems.at[place, part]
        )

    @pl.when(step == 0)
    def _():
        for at_step in range(steps):
            for copy in fetch(at_step):
                copy.start()

    for at_step in range(steps):

        @pl.when(step == at_step)
        def _():
            for copy in fetch(at_step):
                copy.wait()

    place = lax.rem(step, 2)

    @pl.when(step >= 2)
    def _():
        for part in range(count):
            send(place, step - 2, part).wait()

    row = block_rows[0] + step * (block_rows[1] - block_rows[0])
    centre = centre_rows[0] + step * (centre_rows[1] - centre_rows[0])
    rhs = ext_ref.shape[-1]
    tile = 256 if rhs % 256 == 0 else rhs
    for part in range(count):
        middle = centre_cols[part]
        weights = []
        places = []
        for slot in range(near_ref.shape[2]):
            link = nb_ref[row, block_cols[part], slot]
            there = jnp.minimum(link, empty_slot - 1)
            weight = near_ref[step, part, slot]
            weights.append(jnp.where(link < empty_slot, weight, jnp.zeros_like(weight)))
            places.append((centre - 1 + lax.div(there, 3), middle - 1 + lax.rem(there, 3)))
        weights = jnp.concatenate(weights, axis=1)
        for at in range(0, rhs, tile):
            values = [ext_ref[i, j, :, at : at + tile] for i, j in places]
            total = jnp.dot(weights, jnp.concatenate(values, axis=0), preferred_element_type=jnp.float32)
            own = ext_ref[centre, middle, :, at : at + tile].astype(jnp.float32)
            stage_ref[place, part, :, at : at + tile] = (own + total).astype(jnp.bfloat16)
        send(place, step, part).start()
    rights = jnp.concatenate([right_ref[step, part] for part in range(count)], axis=0)
    blocks = jnp.concatenate([stage_ref[place, part] for part in range(count)], axis=0)
    coef = dot_t(rights, blocks, ((0,), (0,)))

    @pl.when(step == 0)
    def _():
        coef_ref[...] = coef

    @pl.when(step > 0)
    def _():
        coef_ref[...] += coef

    @pl.when(step == steps - 1)
    def _():
        for at_step in range(max(steps - 2, 0), steps):
            for part in range(count):
                send(at_step % 2, at_step, part).wait()


def in_hbm(value):
    return pltpu.with_memory_space_constraint(value, pltpu.HBM)


def near_part(sources, plan, near_blocks, far_right, neighbours, prior):
    spans, _, block_rows, block_cols, _, _ = plan
    gu, gv, slots, size, _ = near_blocks.shape
    rhs = sources[0].shape[-1]
    rank = far_right.shape[-1]
    ext_rows = 1 + max(span[2] for span in spans)
    ext_cols = max(span[3] + span[4] for span in spans)
    steps, count = len(block_rows), len(block_cols)
    args = [near_blocks, far_right, *sources]
    args = [in_hbm(value) if value.ndim > 3 else value for value in args]
    aliases = {}
    if prior is not None:
        args.append(prior)
        aliases = {len(args): 0}
    held = pl.BlockSpec(memory_space=pltpu.HBM)
    return pl.pallas_call(
        functools.partial(near_kernel, plan),
        grid_spec=pltpu.PrefetchScalarGridSpec(
            num_scalar_prefetch=1,
            grid=(steps,),
            in_specs=[held, held]
            + [held if source.ndim == 4 else pl.BlockSpec(memory_space=pl.ANY) for source in sources]
            + [held] * len(aliases),
            out_specs=[held, pl.BlockSpec((rank, rhs), lambda i, nb: (0, 0))],
            scratch_shapes=[
                pltpu.VMEM((ext_rows, ext_cols, size, rhs), jnp.bfloat16),
                pltpu.VMEM((steps, count, slots, size, size), jnp.bfloat16),
                pltpu.VMEM((steps, count, size, rank), jnp.bfloat16),
                pltpu.VMEM((2, count, size, rhs), jnp.bfloat16),
                pltpu.SemaphoreType.DMA((len(spans) + 2 * steps * count,)),
                pltpu.SemaphoreType.DMA((2, count)),
            ],
        ),
        out_shape=[
            jax.ShapeDtypeStruct((gu, gv, size, rhs), jnp.bfloat16),
            jax.ShapeDtypeStruct((rank, rhs), jnp.float32),
        ],
        input_output_aliases=aliases,
        cost_estimate=pl.CostEstimate(flops=7000000000, bytes_accessed=10000000, transcendentals=0),
        compiler_params=pltpu.CompilerParams(
            dimension_semantics=("arbitrary",), vmem_limit_bytes=near_vmem
        ),
    )(neighbours, *args)


def near_middle(density, near_blocks, far_right, neighbours, prior):
    gu, gv = density.shape[:2]
    spans = [(0, (row,), row, 0, gv) for row in range(gu)]
    rows = list(range(1, gu - 1))
    wanted = [(0, 1, 2)] + [(row + 1,) for row in rows[1:]]
    cols = list(range(1, gv - 1))
    plan = (spans, wanted, rows, cols, rows, cols)
    return near_part((density,), plan, near_blocks, far_right, neighbours, prior)


def near_rows(density, top, bottom, near_blocks, far_right, neighbours, prior):
    gu, gv = density.shape[:2]
    spans = [(1, (), 0, 0, gv)]
    spans += [(0, (row,), at, 0, gv) for at, row in ((1, 0), (2, 1), (3, gu - 2), (4, gu - 1))]
    spans += [(2, (), 5, 0, gv)]
    cols = list(range(1, gv - 1))
    plan = (spans, [(0, 1, 2), (3, 4, 5)], [0, gu - 1], cols, [1, 4], cols)
    return near_part((density, top, bottom), plan, near_blocks, far_right, neighbours, prior)


def near_cols(density, top, bottom, ends, mids, corner_top, corner_bottom, near_blocks, far_right, neighbours, prior):
    gu, gv = density.shape[:2]
    spans = []
    for ext_row, source, at in (
        [(0, 1, ())] + [(row + 1, 0, (row,)) for row in range(gu)] + [(gu + 1, 2, ())]
    ):
        spans.append((source, at + (pl.ds(0, 2),), ext_row, 1, 2))
        spans.append((source, at + (pl.ds(gv - 2, 2),), ext_row, 3, 2))
    for side in range(2):
        col = 5 * side
        for row in range(gu):
            if row in (0, gu - 1):
                spans.append((3 + side, (pl.ds(0 if row == 0 else 1, 1),), row + 1, col, 1))
            else:
                spans.append((5 + side, (pl.ds(row - 1, 1),), row + 1, col, 1))
        spans.append((7, (pl.ds(side, 1),), 0, col, 1))
        spans.append((8, (pl.ds(side, 1),), gu + 1, col, 1))
    rows = list(range(gu))
    wanted = [(0, 1, 2)] + [(row + 2,) for row in rows[1:]]
    plan = (spans, wanted, rows, [0, gv - 1], [row + 1 for row in rows], [1, 4])
    sources = (density, top, bottom, *ends, *mids, corner_top, corner_bottom)
    return near_part(sources, plan, near_blocks, far_right, neighbours, prior)


def run_copies(pairs, sems):
    copies = [
        pltpu.make_async_copy(source, target, sems.at[index])
        for index, (source, target) in enumerate(pairs)
    ]
    for copy in copies:
        copy.start()
    for copy in copies:
        copy.wait()


def edges_kernel(density, *refs):
    *outs, sems = refs
    gu, gv = density.shape[:2]
    pairs = []
    for side, col in ((0, gv - 1), (1, 0)):
        pairs.append((density.at[0, pl.ds(col, 1)], outs[side].at[pl.ds(0, 1)]))
        pairs.append((density.at[gu - 1, pl.ds(col, 1)], outs[side].at[pl.ds(1, 1)]))
        pairs.append((density.at[pl.ds(1, gu - 2), col], outs[2 + side]))
    pairs.append((density.at[gu - 1], outs[4]))
    pairs.append((density.at[0], outs[5]))
    run_copies(pairs, sems)


def patch_edges(density):
    gu, gv, size, rhs = density.shape
    counts = (2, 2, gu - 2, gu - 2, gv, gv)
    return pl.pallas_call(
        edges_kernel,
        in_specs=[pl.BlockSpec(memory_space=pltpu.HBM)],
        out_specs=[pl.BlockSpec(memory_space=pltpu.VMEM)] * len(counts),
        out_shape=[jax.ShapeDtypeStruct((count, size, rhs), density.dtype) for count in counts],
        scratch_shapes=[pltpu.SemaphoreType.DMA((8,))],
        cost_estimate=pl.CostEstimate(flops=7000000000, bytes_accessed=10000000, transcendentals=0),
        compiler_params=pltpu.CompilerParams(vmem_limit_bytes=merge_vmem),
    )(in_hbm(density))


def corners_kernel(first, last, top, bottom):
    for side, ends in enumerate((first, last)):
        top[side] = ends[1]
        bottom[side] = ends[0]


def patch_corners(ends):
    whole = pl.BlockSpec(memory_space=pltpu.VMEM)
    return pl.pallas_call(
        corners_kernel,
        in_specs=[whole, whole],
        out_specs=[whole, whole],
        out_shape=[jax.ShapeDtypeStruct(ends[0].shape, ends[0].dtype)] * 2,
        cost_estimate=pl.CostEstimate(flops=7000000000, bytes_accessed=10000000, transcendentals=0),
        compiler_params=pltpu.CompilerParams(vmem_limit_bytes=merge_vmem),
    )(*ends)


def reciprocal(value):
    guess = pl.reciprocal(value, approx=True)
    return guess * (2.0 - value * guess)


def eliminate(w_k, w_e):
    size = w_k.shape[0]
    step = 32
    tile = 8
    sub = lax.broadcasted_iota(jnp.int32, (tile, size), 0)

    def spread(value, row):
        return jnp.broadcast_to(value[row : row + 1, :], (tile, size))

    for base in range(0, size, step):
        count = step // tile
        k_rows = [w_k[base + tile * r : base + tile * (r + 1), :] for r in range(count)]
        e_rows = [w_e[base + tile * r : base + tile * (r + 1), :] for r in range(count)]
        for q in range(count):
            at = base + tile * q
            cols = {
                (r, k): jnp.broadcast_to(k_rows[r][:, at + k : at + k + 1], (tile, size))
                for r in range(q, count)
                for k in range(tile)
            }
            k_done = k_rows[q]
            e_done = e_rows[q]
            for k in range(0, tile, 2):
                a = spread(cols[q, k], k)
                b = spread(cols[q, k], k + 1)
                c = spread(cols[q, k + 1], k + 1)
                det = a * c - b * b
                inverse = reciprocal(det)

                def solved(one, two):
                    return (c * one - b * two) * inverse, (a * two - b * one) * inverse

                k_one, k_two = spread(k_rows[q], k), spread(k_rows[q], k + 1)
                e_one, e_two = spread(e_rows[q], k), spread(e_rows[q], k + 1)
                k_solved = solved(k_one, k_two)
                e_solved = solved(e_one, e_two)
                links = {
                    m: solved(spread(cols[q, k], m), spread(cols[q, k + 1], m)) for m in range(k + 2, tile)
                }
                root = lax.rsqrt(a)
                second = lax.rsqrt(det) * a * root
                slope = b * root * root
                k_done = jnp.where(sub == k, k_one * root, k_done)
                e_done = jnp.where(sub == k, e_one * root, e_done)
                k_done = jnp.where(sub == k + 1, (k_two - slope * k_one) * second, k_done)
                e_done = jnp.where(sub == k + 1, (e_two - slope * e_one) * second, e_done)
                for r in range(q, count):
                    one, two = cols[r, k], cols[r, k + 1]
                    if r == q:
                        if k + 2 == tile:
                            continue
                        one = jnp.where(sub > k + 1, one, 0.0)
                        two = jnp.where(sub > k + 1, two, 0.0)
                    for m in range(k + 2, tile):
                        cols[r, m] = cols[r, m] - (one * links[m][0] + two * links[m][1])
                    k_rows[r] = k_rows[r] - (one * k_solved[0] + two * k_solved[1])
                    e_rows[r] = e_rows[r] - (one * e_solved[0] + two * e_solved[1])
            k_rows[q] = k_done
            e_rows[q] = e_done
        e_now = jnp.concatenate(e_rows, axis=0)
        w_e[base : base + step, :] = e_now
        if base + step < size:
            k_now = jnp.concatenate(k_rows, axis=0)
            k_hi = k_now.astype(jnp.bfloat16)
            k_lo = (k_now - k_hi.astype(jnp.float32)).astype(jnp.bfloat16)
            e_hi = e_now.astype(jnp.bfloat16)
            e_lo = (e_now - e_hi.astype(jnp.float32)).astype(jnp.bfloat16)
            lhs = jnp.concatenate([k_hi, k_hi, k_lo], axis=0)
            k_rhs = jnp.concatenate([k_hi, k_lo, k_hi], axis=0)
            e_rhs = jnp.concatenate([e_hi, e_lo, e_hi], axis=0)
            k_fall = dot_t(lhs, k_rhs, ((0,), (0,)))
            e_fall = dot_t(lhs, e_rhs, ((0,), (0,)))
            w_k[base + step :, :] -= k_fall[base + step :, :]
            w_e[base + step :, :] -= e_fall[base + step :, :]


code_rows = 16


def encode(value, out_ref):
    rows = value.shape[0]
    top = jnp.max(jnp.abs(value), axis=0, keepdims=True)
    power = jnp.clip(jnp.floor(jnp.log2(32000.0 / jnp.maximum(top, 1e-30))), -60.0, 60.0)
    scaled = jnp.floor(value * jnp.exp2(power) + 0.5)
    out_ref[:rows, :] = scaled.astype(jnp.int32).astype(jnp.int16)
    powers = jnp.broadcast_to(power, (code_rows, value.shape[1]))
    out_ref[rows:, :] = powers.astype(jnp.int32).astype(jnp.int16)


def decode(ref):
    rows = ref.shape[0] - code_rows
    power = ref[rows:, :].astype(jnp.int32).astype(jnp.float32)[:1]
    return ref[:rows, :].astype(jnp.int32).astype(jnp.float32) * jnp.exp2(-power)


def first_kernel(counts, order_ref, value_ref, code_ref, info_ref):
    pu_count, pv_count = counts
    pu_index = lax.axis_index("pu")
    pv_index = lax.axis_index("pv")

    def least(values):
        return functools.reduce(jnp.minimum, values)

    at = 0
    width = 1
    while width < pv_count:
        start = lax.div(pv_index, width) * width
        other = start + width - 2 * width * lax.rem(lax.div(pv_index, width), 2)
        mine = least([order_ref[pu_index * pv_count + start + k] for k in range(width)])
        theirs = least([order_ref[pu_index * pv_count + other + k] for k in range(width)])
        info_ref[at] = (mine < theirs).astype(jnp.int32)
        at += 1
        width *= 2
    width = 1
    while width < pu_count:
        start = lax.div(pu_index, width) * width
        other = start + width - 2 * width * lax.rem(lax.div(pu_index, width), 2)
        mine = least([order_ref[start * pv_count + k] for k in range(width * pv_count)])
        theirs = least([order_ref[other * pv_count + k] for k in range(width * pv_count)])
        info_ref[at] = (mine < theirs).astype(jnp.int32)
        at += 1
        width *= 2
    info_ref[at] = pu_index
    encode(value_ref[0, 0], code_ref)


def first_step(value, order, counts, levels):
    rows, cols = value.shape[2:]
    return pl.pallas_call(
        functools.partial(first_kernel, counts),
        in_specs=[pl.BlockSpec(memory_space=pltpu.SMEM), pl.BlockSpec(memory_space=pltpu.VMEM)],
        out_specs=[pl.BlockSpec(memory_space=pltpu.VMEM), pl.BlockSpec(memory_space=pltpu.SMEM)],
        out_shape=[
            jax.ShapeDtypeStruct((rows + code_rows, cols), jnp.int16),
            jax.ShapeDtypeStruct((levels + 1,), jnp.int32),
        ],
        cost_estimate=pl.CostEstimate(flops=7000000000, bytes_accessed=10000000, transcendentals=0),
        compiler_params=pltpu.CompilerParams(vmem_limit_bytes=merge_vmem),
    )(order, value)


def merge_kernel(level, has_path, last, info_ref, mine_ref, other_ref, sketch_ref, *refs):
    if has_path:
        path_ref, *refs = refs
    left_ref, new_path_ref, w_k, w_e, y_ref = refs
    rank = mine_ref.shape[1]
    lead = info_ref[level] > 0
    mine = decode(mine_ref)
    other = decode(other_ref)
    stacked = jnp.concatenate([jnp.where(lead, mine, other), jnp.where(lead, other, mine)], axis=1)
    sketched = split_dot(stacked, sketch_ref[...], ((1,), (0,)))
    w_k[...] = split_dot(sketched, sketched, ((0,), (0,)))
    rows = lax.broadcasted_iota(jnp.int32, (rank, rank), 0)
    cols = lax.broadcasted_iota(jnp.int32, (rank, rank), 1)
    w_e[...] = jnp.where(rows == cols, 1.0, 0.0)
    eliminate(w_k, w_e)
    inverse = w_e[...]
    if last:
        y_ref[...] = sketched
        count = left_ref.shape[0]
        part = y_ref[pl.ds(pl.multiple_of(info_ref[info_ref.shape[0] - 1] * count, 8), count), :]
        left_ref[...] = split_dot(part, inverse, ((1,), (1,)))
    else:
        encode(split_dot(sketched, inverse, ((1,), (1,))), left_ref)
    own = split_dot(sketched, mine, ((0,), (0,)))
    if has_path:
        own = split_dot(own, path_ref[...], ((1,), (0,)))
    new_path_ref[...] = split_dot(inverse, own, ((1,), (0,)))


def merge(level, info, mine, other, sketch, path, last_rows):
    rows, rank = mine.shape
    whole = pl.BlockSpec(memory_space=pltpu.VMEM)
    paths = () if path is None else (path,)
    if last_rows:
        left = jax.ShapeDtypeStruct((last_rows, rank), jnp.float32)
    else:
        left = jax.ShapeDtypeStruct(mine.shape, jnp.int16)
    return pl.pallas_call(
        functools.partial(merge_kernel, level, bool(paths), bool(last_rows)),
        in_specs=[pl.BlockSpec(memory_space=pltpu.SMEM), whole, whole, whole] + [whole] * len(paths),
        out_specs=[whole, whole],
        out_shape=[left, jax.ShapeDtypeStruct((rank, rank), jnp.float32)],
        scratch_shapes=[
            pltpu.VMEM((rank, rank), jnp.float32),
            pltpu.VMEM((rank, rank), jnp.float32),
            pltpu.VMEM((rows - code_rows, rank), jnp.float32),
        ],
        cost_estimate=pl.CostEstimate(flops=7000000000, bytes_accessed=10000000, transcendentals=0),
        compiler_params=pltpu.CompilerParams(vmem_limit_bytes=merge_vmem),
    )(info, mine, other, sketch, *paths)


def from_partner(value, axis, distance):
    mask = 2**distance
    pairs = [(source, source ^ mask) for source in range(lax.axis_size(axis))]
    return lax.ppermute(value, axis, pairs)


def shifted(value, axis, by):
    count = lax.axis_size(axis)
    return lax.ppermute(value, axis, [(i, i + by) for i in range(count) if 0 <= i + by < count])


def tied(*values):
    return lax.optimization_barrier(values)


def per_device(density, near_blocks, neighbours, far_right, far_left, sketch, patch_order):
    pu_count = lax.axis_size("pu")
    pv_count = lax.axis_size("pv")
    pv_index = lax.axis_index("pv")
    rhs = density.shape[3]
    pv_levels = pv_count.bit_length() - 1
    pu_levels = pu_count.bit_length() - 1
    levels = pv_levels + pu_levels

    def partner(value, level):
        if level < pv_levels:
            return from_partner(value, "pv", level)
        return from_partner(value, "pu", level - pv_levels)

    rows = far_left.shape[2]
    left, info = first_step(far_left, patch_order, (pu_count, pv_count), levels)
    other = partner(left, 0)
    density, left = tied(density, left)
    *columns, last_row, first_row = patch_edges(density)
    top = shifted(last_row, "pu", 1)
    bottom = shifted(first_row, "pu", -1)
    columns, other = tied(columns, other)
    ends = [shifted(columns[0], "pv", 1), shifted(columns[1], "pv", -1)]

    coefs = []
    corrected = None
    pv_path = pu_path = None
    for level in range(levels):
        if level:
            other = partner(left, level)
            links, left = tied(neighbours, left)
            if level == 1:
                columns, left = tied(columns, left)
                mids = [shifted(columns[2], "pv", 1), shifted(columns[3], "pv", -1)]
                corrected, coef = near_middle(density, near_blocks, far_right, links, corrected)
            elif level == 2:
                corner_top, corner_bottom = patch_corners(ends)
                corner_top = shifted(corner_top, "pu", 1)
                corner_bottom = shifted(corner_bottom, "pu", -1)
                corrected, coef = near_rows(density, top, bottom, near_blocks, far_right, links, corrected)
            elif level == levels - 1:
                corrected, coef = near_cols(
                    density,
                    top,
                    bottom,
                    ends,
                    mids,
                    corner_top,
                    corner_bottom,
                    near_blocks,
                    far_right,
                    links,
                    corrected,
                )
            else:
                coef = None
            if coef is not None:
                other, coef = tied(other, coef)
                coefs.append(coef)
        path = pv_path if level < pv_levels else pu_path
        last_rows = rows // pu_count if level == levels - 1 else 0
        left, path = merge(level, info, left, other, sketch, path, last_rows)
        if level < pv_levels:
            pv_path = path
        else:
            pu_path = path

    coef = functools.reduce(lambda a, b: a + b, coefs)
    share = lax.dot_general(coef, pv_path, (((0,), (1,)), ((), ())), precision=high)
    share = share.reshape(pv_count, rhs // pv_count, -1)
    for level in range(pv_levels):
        bit = (pv_index >> level) & 1
        pairs = share.reshape(share.shape[0] // 2, 2, *share.shape[1:])
        keep = lax.dynamic_index_in_dim(pairs, bit, 1, keepdims=False)
        give = lax.dynamic_index_in_dim(pairs, 1 - bit, 1, keepdims=False)
        share = keep + from_partner(give, "pv", level)
    root_coef = lax.dot_general(share[0], pu_path, (((1,), (1,)), ((), ())), precision=high)
    for level in range(pu_levels):
        root_coef = root_coef + from_partner(root_coef, "pu", level)
    far_field = lax.dot_general(left, root_coef, (((1,), (1,)), ((), ())), precision=high)
    return (corrected, far_field)


def solution(mesh):
    in_specs = (
        P("pu", "pv", None, None),
        P("pu", "pv", None, None, None),
        P("pu", "pv", None),
        P("pu", "pv", None, None),
        P("pu", "pv", None, None),
        P(),
        P(),
    )
    out_specs = (P("pu", "pv", None, None), P("pu", "pv"))
    return jax.shard_map(
        per_device, mesh=mesh, in_specs=in_specs, out_specs=out_specs, check_vma=False
    )
```

```python
import functools

import jax
import jax.numpy as jnp
from jax import lax
from jax.experimental import pallas as pl
from jax.experimental.pallas import tpu as pltpu
from jax.sharding import PartitionSpec as P

high = lax.Precision.HIGH
empty_slot = 9
near_vmem = 26 * 1024 * 1024
merge_vmem = 12 * 1024 * 1024


def dot_t(a, b, dims, precision=None):
    return lax.dot_general(
        a, b, (dims, ((), ())), precision=precision, preferred_element_type=jnp.float32
    )


def split_dot(a, b, dims):
    return dot_t(a, b, dims, high)


def in_hbm(value):
    return pltpu.with_memory_space_constraint(value, pltpu.HBM)


def cost(microseconds):
    return pl.CostEstimate(flops=int(microseconds * 1.1e9), bytes_accessed=0, transcendentals=0)


def near_kernel(plan, n_src, nb_ref, near_hbm, right_hbm, *refs):
    spans, block_rows, centre_rows, count, first_col, centre_col = plan
    srcs = refs[:n_src]
    out_ref, coef_ref, ext_ref, near_ref, right_ref, stage_ref, sems, out_sems = refs[-8:]
    steps = len(block_rows)
    step = pl.program_id(0)
    col = first_col()

    def fetch(at_step):
        found = []
        for index, (needed, views) in enumerate(spans):
            if needed == at_step:
                source, target = views(srcs, ext_ref)
                found.append(pltpu.make_async_copy(source, target, sems.at[index]))
        base = len(spans) + 2 * at_step
        for offset, source, target in ((0, near_hbm, near_ref), (1, right_hbm, right_ref)):
            found.append(
                pltpu.make_async_copy(
                    source.at[block_rows[at_step], pl.ds(col, count)], target.at[at_step], sems.at[base + offset]
                )
            )
        return found

    def send(place, at_step, part):
        row = block_rows[0] + at_step * (block_rows[1] - block_rows[0])
        return pltpu.make_async_copy(
            stage_ref.at[place, part], out_ref.at[row, col + part], out_sems.at[place, part]
        )

    @pl.when(step == 0)
    def _():
        for at_step in range(steps):
            for copy in fetch(at_step):
                copy.start()

    for at_step in range(steps):

        @pl.when(step == at_step)
        def _():
            for copy in fetch(at_step):
                copy.wait()

    place = lax.rem(step, 2)

    @pl.when(step >= 2)
    def _():
        for part in range(count):
            send(place, step - 2, part).wait()

    row = block_rows[0] + step * (block_rows[1] - block_rows[0])
    centre = centre_rows[0] + step * (centre_rows[1] - centre_rows[0])
    rhs = ext_ref.shape[-1]
    tile = 256 if rhs % 256 == 0 else rhs
    for part in range(count):
        middle = centre_col + part
        weights = []
        places = []
        for slot in range(near_ref.shape[2]):
            link = nb_ref[row, col + part, slot]
            there = jnp.minimum(link, empty_slot - 1)
            weight = near_ref[step, part, slot]
            weights.append(jnp.where(link < empty_slot, weight, jnp.zeros_like(weight)))
            places.append((centre - 1 + lax.div(there, 3), middle - 1 + lax.rem(there, 3)))
        weights = jnp.concatenate(weights, axis=1)
        for at in range(0, rhs, tile):
            values = [ext_ref[i, j, :, at : at + tile] for i, j in places]
            total = jnp.dot(weights, jnp.concatenate(values, axis=0), preferred_element_type=jnp.float32)
            own = ext_ref[centre, middle, :, at : at + tile].astype(jnp.float32)
            stage_ref[place, part, :, at : at + tile] = (own + total).astype(jnp.bfloat16)
        send(place, step, part).start()
    rights = jnp.concatenate([right_ref[step, part] for part in range(count)], axis=0)
    blocks = jnp.concatenate([stage_ref[place, part] for part in range(count)], axis=0)
    coef = dot_t(rights, blocks, ((0,), (0,)))

    @pl.when(step == 0)
    def _():
        coef_ref[...] = coef

    @pl.when(step > 0)
    def _():
        coef_ref[...] += coef

    @pl.when(step == steps - 1)
    def _():
        for at_step in range(max(steps - 2, 0), steps):
            for part in range(count):
                send(at_step % 2, at_step, part).wait()


def near_part(sources, plan, ext_shape, near_blocks, far_right, neighbours, prior, time):
    spans, block_rows, _, count, _, _ = plan
    gu, gv, slots, size, _ = near_blocks.shape
    rhs = sources[0].shape[-1]
    rank = far_right.shape[-1]
    steps = len(block_rows)
    args = [near_blocks, far_right, *sources]
    args = [in_hbm(value) if value.ndim > 3 else value for value in args]
    aliases = {}
    if prior is not None:
        args.append(prior)
        aliases = {len(args): 0}
    held = pl.BlockSpec(memory_space=pltpu.HBM)
    return pl.pallas_call(
        functools.partial(near_kernel, plan, len(sources)),
        grid_spec=pltpu.PrefetchScalarGridSpec(
            num_scalar_prefetch=1,
            grid=(steps,),
            in_specs=[held, held]
            + [held if source.ndim == 4 else pl.BlockSpec(memory_space=pl.ANY) for source in sources]
            + [held] * len(aliases),
            out_specs=[held, pl.BlockSpec((rank, rhs), lambda i, nb: (0, 0))],
            scratch_shapes=[
                pltpu.VMEM((*ext_shape, size, rhs), jnp.bfloat16),
                pltpu.VMEM((steps, count, slots, size, size), jnp.bfloat16),
                pltpu.VMEM((steps, count, size, rank), jnp.bfloat16),
                pltpu.VMEM((2, count, size, rhs), jnp.bfloat16),
                pltpu.SemaphoreType.DMA((len(spans) + 2 * steps,)),
                pltpu.SemaphoreType.DMA((2, count)),
            ],
        ),
        out_shape=[
            jax.ShapeDtypeStruct((gu, gv, size, rhs), jnp.bfloat16),
            jax.ShapeDtypeStruct((rank, rhs), jnp.float32),
        ],
        input_output_aliases=aliases,
        cost_estimate=cost(time),
        compiler_params=pltpu.CompilerParams(
            dimension_semantics=("arbitrary",), vmem_limit_bytes=near_vmem
        ),
    )(neighbours, *args)


def odd(axis):
    return lax.rem(lax.axis_index(axis), 2)


def row_span(row, ext_row):
    return lambda srcs, ext: (srcs[0].at[row], ext.at[ext_row])


def near_middle(density, near_blocks, far_right, neighbours, prior):
    gu, gv = density.shape[:2]
    spans = [(max(row - 2, 0), row_span(row, row)) for row in range(gu)]
    rows = list(range(1, gu - 1))
    plan = (spans, rows, rows, gv - 2, lambda: 1, 1)
    return near_part((density,), plan, (gu, gv), near_blocks, far_right, neighbours, prior, 8)


def near_rows(density, pu_near, pu_far, near_blocks, far_right, neighbours, prior):
    gu, gv = density.shape[:2]
    spans = [(at, row_span(row, ext_row)) for at, row, ext_row in ((0, 0, 1), (0, 1, 2), (1, gu - 2, 3), (1, gu - 1, 4))]
    spans.append((0, lambda srcs, ext: (srcs[1], ext.at[5 * (1 - odd("pu"))])))
    spans.append((0, lambda srcs, ext: (srcs[2], ext.at[5 * odd("pu")])))
    plan = (spans, [0, gu - 1], [1, 4], gv - 2, lambda: 1, 1)
    return near_part((density, pu_near, pu_far), plan, (6, gv), near_blocks, far_right, neighbours, prior, 1.5)


def near_column(far, density, pu_near, pu_far, corner_near, corner_far, halo, near_blocks, far_right, neighbours, prior):
    gu, gv = density.shape[:2]

    def left_side():
        return 1 - odd("pv") if far else odd("pv")

    spans = []

    def start_col():
        return (gv - 2) * (1 - left_side())

    def inner(source, at, ext_row):
        def views(srcs, ext):
            view = srcs[source]
            if at is not None:
                view = view.at[at]
            return view.at[pl.ds(start_col(), 2)], ext.at[ext_row(), pl.ds(left_side(), 2)]

        return views

    def outer(source, at, ext_row):
        return lambda srcs, ext: (srcs[source].at[at], ext.at[ext_row(), 2 * (1 - left_side())])

    def near_row():
        return (gu + 1) * (1 - odd("pu"))

    def far_row():
        return (gu + 1) * odd("pu")

    for row in range(gu):
        at = max(row - 1, 0)
        spans.append((at, inner(0, row, lambda row=row: row + 1)))
        if len(halo) == 1:
            spans.append((at, outer(5, row, lambda row=row: row + 1)))
        elif row in (0, gu - 1):
            spans.append((at, outer(5, min(row, 1), lambda row=row: row + 1)))
        else:
            spans.append((at, outer(6, row - 1, lambda row=row: row + 1)))
    spans.append((0, inner(1, None, near_row)))
    spans.append((0, inner(2, None, far_row)))
    spans.append((0, outer(3, int(far), near_row)))
    spans.append((0, outer(4, int(far), far_row)))
    rows = list(range(gu))
    plan = (spans, rows, [row + 1 for row in rows], 1, lambda: (gv - 1) * (1 - left_side()), 1)
    sources = (density, pu_near, pu_far, corner_near, corner_far, *halo)
    return near_part(sources, plan, (gu + 2, 3), near_blocks, far_right, neighbours, prior, 1.5)


def corners_kernel(beside, ends, to_near, to_far):
    low = odd("pu")
    rows = beside.shape[0]
    for target, last in ((to_near, 1 - low), (to_far, low)):
        target[0] = beside[(rows - 1) * last]
        target[1] = ends[last]


def patch_corners(beside, ends):
    whole = pl.BlockSpec(memory_space=pltpu.VMEM)
    return pl.pallas_call(
        corners_kernel,
        in_specs=[whole, whole],
        out_specs=[whole, whole],
        out_shape=[jax.ShapeDtypeStruct(ends.shape, ends.dtype)] * 2,
        cost_estimate=cost(0.7),
        compiler_params=pltpu.CompilerParams(vmem_limit_bytes=merge_vmem),
    )(beside, ends)


def reciprocal(value):
    guess = pl.reciprocal(value, approx=True)
    return guess * (2.0 - value * guess)


def eliminate(w_k, w_e):
    size = w_k.shape[0]
    step = 32
    tile = 8
    sub = lax.broadcasted_iota(jnp.int32, (tile, size), 0)

    def spread(value, row):
        return jnp.broadcast_to(value[row : row + 1, :], (tile, size))

    for base in range(0, size, step):
        count = step // tile
        k_rows = [w_k[base + tile * r : base + tile * (r + 1), :] for r in range(count)]
        e_rows = [w_e[base + tile * r : base + tile * (r + 1), :] for r in range(count)]
        for q in range(count):
            at = base + tile * q
            cols = {
                (r, k): jnp.broadcast_to(k_rows[r][:, at + k : at + k + 1], (tile, size))
                for r in range(q, count)
                for k in range(tile)
            }
            k_done = k_rows[q]
            e_done = e_rows[q]
            for k in range(0, tile, 2):
                a = spread(cols[q, k], k)
                b = spread(cols[q, k], k + 1)
                c = spread(cols[q, k + 1], k + 1)
                det = a * c - b * b
                inverse = reciprocal(det)

                def solved(one, two):
                    return (c * one - b * two) * inverse, (a * two - b * one) * inverse

                k_one, k_two = spread(k_rows[q], k), spread(k_rows[q], k + 1)
                e_one, e_two = spread(e_rows[q], k), spread(e_rows[q], k + 1)
                k_solved = solved(k_one, k_two)
                e_solved = solved(e_one, e_two)
                links = {
                    m: solved(spread(cols[q, k], m), spread(cols[q, k + 1], m)) for m in range(k + 2, tile)
                }
                root = lax.rsqrt(a)
                second = lax.rsqrt(det) * a * root
                slope = b * root * root
                k_done = jnp.where(sub == k, k_one * root, k_done)
                e_done = jnp.where(sub == k, e_one * root, e_done)
                k_done = jnp.where(sub == k + 1, (k_two - slope * k_one) * second, k_done)
                e_done = jnp.where(sub == k + 1, (e_two - slope * e_one) * second, e_done)
                for r in range(q, count):
                    one, two = cols[r, k], cols[r, k + 1]
                    if r == q:
                        if k + 2 == tile:
                            continue
                        one = jnp.where(sub > k + 1, one, 0.0)
                        two = jnp.where(sub > k + 1, two, 0.0)
                    for m in range(k + 2, tile):
                        cols[r, m] = cols[r, m] - (one * links[m][0] + two * links[m][1])
                    k_rows[r] = k_rows[r] - (one * k_solved[0] + two * k_solved[1])
                    e_rows[r] = e_rows[r] - (one * e_solved[0] + two * e_solved[1])
            k_rows[q] = k_done
            e_rows[q] = e_done
        e_now = jnp.concatenate(e_rows, axis=0)
        w_e[base : base + step, :] = e_now
        if base + step < size:
            k_now = jnp.concatenate(k_rows, axis=0)
            k_hi = k_now.astype(jnp.bfloat16)
            k_lo = (k_now - k_hi.astype(jnp.float32)).astype(jnp.bfloat16)
            e_hi = e_now.astype(jnp.bfloat16)
            e_lo = (e_now - e_hi.astype(jnp.float32)).astype(jnp.bfloat16)
            lhs = jnp.concatenate([k_hi, k_hi, k_lo], axis=0)
            k_rhs = jnp.concatenate([k_hi, k_lo, k_hi], axis=0)
            e_rhs = jnp.concatenate([e_hi, e_lo, e_hi], axis=0)
            k_fall = dot_t(lhs, k_rhs, ((0,), (0,)))
            e_fall = dot_t(lhs, e_rhs, ((0,), (0,)))
            w_k[base + step :, :] -= k_fall[base + step :, :]
            w_e[base + step :, :] -= e_fall[base + step :, :]


code_rows = 16


def encode(value, out_ref):
    rows = value.shape[0]
    top = jnp.max(jnp.abs(value), axis=0, keepdims=True)
    power = jnp.clip(jnp.floor(jnp.log2(32000.0 / jnp.maximum(top, 1e-30))), -60.0, 60.0)
    scaled = jnp.floor(value * jnp.exp2(power) + 0.5)
    out_ref[:rows, :] = scaled.astype(jnp.int32).astype(jnp.int16)
    powers = jnp.broadcast_to(power, (code_rows, value.shape[1]))
    out_ref[rows:, :] = powers.astype(jnp.int32).astype(jnp.int16)


def decode(ref):
    rows = ref.shape[0] - code_rows
    power = ref[rows:, :].astype(jnp.int32).astype(jnp.float32)[:1]
    return ref[:rows, :].astype(jnp.int32).astype(jnp.float32) * jnp.exp2(-power)


def first_kernel(counts, order_ref, value_ref, density, code_ref, info_ref, *refs):
    beside, ends, mids, pu_near, pu_far, sems = refs
    pu_count, pv_count = counts
    pu_index = lax.axis_index("pu")
    pv_index = lax.axis_index("pv")
    gu, gv = density.shape[:2]
    near_col = (gv - 1) * (1 - odd("pv"))
    far_col = (gv - 1) * odd("pv")
    pairs = [(density.at[row, near_col], beside.at[row]) for row in range(gu)]
    pairs += [(density.at[(gu - 1) * row, far_col], ends.at[row]) for row in range(2)]
    pairs += [(density.at[row + 1, far_col], mids.at[row]) for row in range(gu - 2)]
    pairs.append((density.at[(gu - 1) * (1 - odd("pu"))], pu_near))
    pairs.append((density.at[(gu - 1) * odd("pu")], pu_far))
    copies = [
        pltpu.make_async_copy(source, target, sems.at[index])
        for index, (source, target) in enumerate(pairs)
    ]
    for copy in copies:
        copy.start()

    def least(values):
        return functools.reduce(jnp.minimum, values)

    at = 0
    width = 1
    while width < pv_count:
        start = lax.div(pv_index, width) * width
        other = start + width - 2 * width * lax.rem(lax.div(pv_index, width), 2)
        mine = least([order_ref[pu_index * pv_count + start + k] for k in range(width)])
        theirs = least([order_ref[pu_index * pv_count + other + k] for k in range(width)])
        info_ref[at] = (mine < theirs).astype(jnp.int32)
        at += 1
        width *= 2
    width = 1
    while width < pu_count:
        start = lax.div(pu_index, width) * width
        other = start + width - 2 * width * lax.rem(lax.div(pu_index, width), 2)
        mine = least([order_ref[start * pv_count + k] for k in range(width * pv_count)])
        theirs = least([order_ref[other * pv_count + k] for k in range(width * pv_count)])
        info_ref[at] = (mine < theirs).astype(jnp.int32)
        at += 1
        width *= 2
    info_ref[at] = pu_index
    encode(value_ref[0, 0], code_ref)
    for copy in copies:
        copy.wait()


def first_step(value, density, order, counts, levels):
    rows, cols = value.shape[2:]
    gu, gv, size, rhs = density.shape
    blocks = (gu, 2, gu - 2, gv, gv)
    whole = pl.BlockSpec(memory_space=pltpu.VMEM)
    scalars = pl.BlockSpec(memory_space=pltpu.SMEM)
    return pl.pallas_call(
        functools.partial(first_kernel, counts),
        in_specs=[scalars, whole, pl.BlockSpec(memory_space=pltpu.HBM)],
        out_specs=[whole, scalars] + [whole] * len(blocks),
        out_shape=[
            jax.ShapeDtypeStruct((rows + code_rows, cols), jnp.int16),
            jax.ShapeDtypeStruct((levels + 1,), jnp.int32),
        ]
        + [jax.ShapeDtypeStruct((count, size, rhs), density.dtype) for count in blocks],
        scratch_shapes=[pltpu.SemaphoreType.DMA((2 * gu + 2,))],
        cost_estimate=cost(3),
        compiler_params=pltpu.CompilerParams(vmem_limit_bytes=merge_vmem),
    )(order, value, in_hbm(density))


def merge_kernel(level, has_path, last, info_ref, mine_ref, other_ref, sketch_ref, *refs):
    if has_path:
        path_ref, *refs = refs
    left_ref, new_path_ref, w_k, w_e, y_ref = refs
    rank = mine_ref.shape[1]
    lead = info_ref[level] > 0
    mine = decode(mine_ref)
    other = decode(other_ref)
    stacked = jnp.concatenate([jnp.where(lead, mine, other), jnp.where(lead, other, mine)], axis=1)
    sketched = split_dot(stacked, sketch_ref[...], ((1,), (0,)))
    w_k[...] = split_dot(sketched, sketched, ((0,), (0,)))
    rows = lax.broadcasted_iota(jnp.int32, (rank, rank), 0)
    cols = lax.broadcasted_iota(jnp.int32, (rank, rank), 1)
    w_e[...] = jnp.where(rows == cols, 1.0, 0.0)
    eliminate(w_k, w_e)
    inverse = w_e[...]
    if last:
        y_ref[...] = sketched
        count = left_ref.shape[0]
        part = y_ref[pl.ds(pl.multiple_of(info_ref[info_ref.shape[0] - 1] * count, 8), count), :]
        left_ref[...] = split_dot(part, inverse, ((1,), (1,)))
    else:
        encode(split_dot(sketched, inverse, ((1,), (1,))), left_ref)
    own = split_dot(sketched, mine, ((0,), (0,)))
    if has_path:
        own = split_dot(own, path_ref[...], ((1,), (0,)))
    new_path_ref[...] = split_dot(inverse, own, ((1,), (0,)))


def merge(level, info, mine, other, sketch, path, last_rows):
    rows, rank = mine.shape
    whole = pl.BlockSpec(memory_space=pltpu.VMEM)
    paths = () if path is None else (path,)
    if last_rows:
        left = jax.ShapeDtypeStruct((last_rows, rank), jnp.float32)
    else:
        left = jax.ShapeDtypeStruct(mine.shape, jnp.int16)
    return pl.pallas_call(
        functools.partial(merge_kernel, level, bool(paths), bool(last_rows)),
        in_specs=[pl.BlockSpec(memory_space=pltpu.SMEM), whole, whole, whole] + [whole] * len(paths),
        out_specs=[whole, whole],
        out_shape=[left, jax.ShapeDtypeStruct((rank, rank), jnp.float32)],
        scratch_shapes=[
            pltpu.VMEM((rank, rank), jnp.float32),
            pltpu.VMEM((rank, rank), jnp.float32),
            pltpu.VMEM((rows - code_rows, rank), jnp.float32),
        ],
        cost_estimate=cost(4 if level < 2 else 2),
        compiler_params=pltpu.CompilerParams(vmem_limit_bytes=merge_vmem),
    )(info, mine, other, sketch, *paths)


def from_partner(value, axis, distance):
    mask = 2**distance
    pairs = [(source, source ^ mask) for source in range(lax.axis_size(axis))]
    return lax.ppermute(value, axis, pairs)


def swapped(value, axis, far):
    count = lax.axis_size(axis)
    pairs = []
    for low in range(int(far), count - 1, 2):
        pairs += [(low, low + 1), (low + 1, low)]
    return lax.ppermute(value, axis, pairs)


def tied(*values):
    return lax.optimization_barrier(values)


def per_device(density, near_blocks, neighbours, far_right, far_left, sketch, patch_order):
    pu_count = lax.axis_size("pu")
    pv_count = lax.axis_size("pv")
    pv_index = lax.axis_index("pv")
    rhs = density.shape[3]
    pv_levels = pv_count.bit_length() - 1
    pu_levels = pu_count.bit_length() - 1
    levels = pv_levels + pu_levels

    def partner(value, level):
        if level < pv_levels:
            return from_partner(value, "pv", level)
        return from_partner(value, "pu", level - pv_levels)

    rows = far_left.shape[2]
    left, info, beside, ends, mids, pu_near, pu_far = first_step(
        far_left, density, patch_order, (pu_count, pv_count), levels
    )
    other = partner(left, 0)
    beside = swapped(beside, "pv", False)
    pu_near = swapped(pu_near, "pu", False)
    pu_far = swapped(pu_far, "pu", True)

    coefs = []
    corrected = None
    pv_path = pu_path = None
    for level in range(levels):
        coef = None
        if level:
            other = partner(left, level)
        if level in (1, 2, levels - 1):
            links, left = tied(neighbours, left)
        if level == 1:
            corrected, coef = near_middle(density, near_blocks, far_right, links, corrected)
        elif level == 2:
            ends, mids, left = tied(ends, mids, left)
            ends = swapped(ends, "pv", True)
            mids = swapped(mids, "pv", True)
            corrected, coef = near_rows(density, pu_near, pu_far, near_blocks, far_right, links, corrected)
        elif level == levels - 1:
            corner_near, corner_far = patch_corners(beside, ends)
            corner_near = swapped(corner_near, "pu", False)
            corner_far = swapped(corner_far, "pu", True)
            halo = (density, pu_near, pu_far, corner_near, corner_far)
            corrected, coef = near_column(False, *halo, (beside,), near_blocks, far_right, links, corrected)
        if coef is not None:
            other, coef = tied(other, coef)
            coefs.append(coef)
        path = pv_path if level < pv_levels else pu_path
        last_rows = rows // pu_count if level == levels - 1 else 0
        left, path = merge(level, info, left, other, sketch, path, last_rows)
        if level < pv_levels:
            pv_path = path
        else:
            pu_path = path

    corrected, coef = near_column(True, *halo, (ends, mids), near_blocks, far_right, neighbours, corrected)
    coefs.append(coef)

    coef = functools.reduce(lambda a, b: a + b, coefs)
    share = lax.dot_general(coef, pv_path, (((0,), (1,)), ((), ())), precision=high)
    share = share.reshape(pv_count, rhs // pv_count, -1)
    for level in range(pv_levels):
        bit = (pv_index >> level) & 1
        pairs = share.reshape(share.shape[0] // 2, 2, *share.shape[1:])
        keep = lax.dynamic_index_in_dim(pairs, bit, 1, keepdims=False)
        give = lax.dynamic_index_in_dim(pairs, 1 - bit, 1, keepdims=False)
        share = keep + from_partner(give, "pv", level)
    root_coef = lax.dot_general(share[0], pu_path, (((1,), (1,)), ((), ())), precision=high)
    for level in range(pu_levels):
        root_coef = root_coef + from_partner(root_coef, "pu", level)
    far_field = lax.dot_general(left, root_coef, (((1,), (1,)), ((), ())), precision=high)
    return (corrected, far_field)


def solution(mesh):
    in_specs = (
        P("pu", "pv", None, None),
        P("pu", "pv", None, None, None),
        P("pu", "pv", None),
        P("pu", "pv", None, None),
        P("pu", "pv", None, None),
        P(),
        P(),
    )
    out_specs = (P("pu", "pv", None, None), P("pu", "pv"))
    return jax.shard_map(
        per_device, mesh=mesh, in_specs=in_specs, out_specs=out_specs, check_vma=False
    )
```

```python
import functools

import jax
import jax.numpy as jnp
from jax import lax
from jax.experimental import pallas as pl
from jax.experimental.pallas import tpu as pltpu
from jax.sharding import PartitionSpec as P

high = lax.Precision.HIGH
empty_slot = 9
near_vmem = 26 * 1024 * 1024
merge_vmem = 12 * 1024 * 1024


def dot_t(a, b, dims, precision=None):
    return lax.dot_general(
        a, b, (dims, ((), ())), precision=precision, preferred_element_type=jnp.float32
    )


def split_dot(a, b, dims):
    return dot_t(a, b, dims, high)


def in_hbm(value):
    return pltpu.with_memory_space_constraint(value, pltpu.HBM)


def cost(microseconds):
    return pl.CostEstimate(flops=int(microseconds * 1.1e9), bytes_accessed=0, transcendentals=0)


def near_kernel(plan, n_src, nb_ref, near_hbm, right_hbm, *refs):
    steps, spans, parts = plan
    srcs = refs[:n_src]
    out_ref, coef_ref, ext_ref, near_ref, right_ref, stage_ref, sems, out_sems = refs[-8:]
    step = pl.program_id(0)
    count = len(parts)

    def fetch(at_step):
        found = []
        for index, (needed, views) in enumerate(spans):
            if needed == at_step:
                source, target = views(srcs, ext_ref)
                found.append(pltpu.make_async_copy(source, target, sems.at[index]))
        for part, (row, by, col, *_) in enumerate(parts):
            at = len(spans) + 2 * (at_step * count + part)
            for offset, source, target in ((0, near_hbm, near_ref), (1, right_hbm, right_ref)):
                found.append(
                    pltpu.make_async_copy(
                        source.at[row + by * at_step, col()], target.at[at_step, part], sems.at[at + offset]
                    )
                )
        return found

    def send(place, at_step, part):
        row, by, col = parts[part][:3]
        return pltpu.make_async_copy(
            stage_ref.at[place, part], out_ref.at[row + by * at_step, col()], out_sems.at[place, part]
        )

    @pl.when(step == 0)
    def _():
        for at_step in range(steps):
            for copy in fetch(at_step):
                copy.start()

    for at_step in range(steps):

        @pl.when(step == at_step)
        def _():
            for copy in fetch(at_step):
                copy.wait()

    place = lax.rem(step, 2)

    @pl.when(step >= 2)
    def _():
        for part in range(count):
            send(place, step - 2, part).wait()

    rhs = ext_ref.shape[-1]
    tile = 256 if rhs % 256 == 0 else rhs
    for part, (row, by, col, ext_row, ext_by, middle) in enumerate(parts):
        centre = ext_row + ext_by * step
        weights = []
        places = []
        for slot in range(near_ref.shape[2]):
            link = nb_ref[row + by * step, col(), slot]
            there = jnp.minimum(link, empty_slot - 1)
            weight = near_ref[step, part, slot]
            weights.append(jnp.where(link < empty_slot, weight, jnp.zeros_like(weight)))
            places.append((centre - 1 + lax.div(there, 3), middle - 1 + lax.rem(there, 3)))
        weights = jnp.concatenate(weights, axis=1)
        for at in range(0, rhs, tile):
            values = [ext_ref[i, j, :, at : at + tile] for i, j in places]
            total = jnp.dot(weights, jnp.concatenate(values, axis=0), preferred_element_type=jnp.float32)
            own = ext_ref[centre, middle, :, at : at + tile].astype(jnp.float32)
            stage_ref[place, part, :, at : at + tile] = (own + total).astype(jnp.bfloat16)
        send(place, step, part).start()
    rights = jnp.concatenate([right_ref[step, part] for part in range(count)], axis=0)
    blocks = jnp.concatenate([stage_ref[place, part] for part in range(count)], axis=0)
    coef = dot_t(rights, blocks, ((0,), (0,)))

    @pl.when(step == 0)
    def _():
        coef_ref[...] = coef

    @pl.when(step > 0)
    def _():
        coef_ref[...] += coef

    @pl.when(step == steps - 1)
    def _():
        for at_step in range(max(steps - 2, 0), steps):
            for part in range(count):
                send(at_step % 2, at_step, part).wait()


def near_part(sources, plan, ext_shape, near_blocks, far_right, neighbours, prior, time):
    steps, spans, parts = plan
    count = len(parts)
    gu, gv, slots, size, _ = near_blocks.shape
    rhs = sources[0].shape[-1]
    rank = far_right.shape[-1]
    args = [near_blocks, far_right, *sources]
    args = [in_hbm(value) if value.ndim > 3 else value for value in args]
    aliases = {}
    if prior is not None:
        args.append(prior)
        aliases = {len(args): 0}
    held = pl.BlockSpec(memory_space=pltpu.HBM)
    return pl.pallas_call(
        functools.partial(near_kernel, plan, len(sources)),
        grid_spec=pltpu.PrefetchScalarGridSpec(
            num_scalar_prefetch=1,
            grid=(steps,),
            in_specs=[held, held]
            + [held if source.ndim == 4 else pl.BlockSpec(memory_space=pl.ANY) for source in sources]
            + [held] * len(aliases),
            out_specs=[held, pl.BlockSpec((rank, rhs), lambda i, nb: (0, 0))],
            scratch_shapes=[
                pltpu.VMEM((*ext_shape, size, rhs), jnp.bfloat16),
                pltpu.VMEM((steps, count, slots, size, size), jnp.bfloat16),
                pltpu.VMEM((steps, count, size, rank), jnp.bfloat16),
                pltpu.VMEM((2, count, size, rhs), jnp.bfloat16),
                pltpu.SemaphoreType.DMA((len(spans) + 2 * steps * count,)),
                pltpu.SemaphoreType.DMA((2, count)),
            ],
        ),
        out_shape=[
            jax.ShapeDtypeStruct((gu, gv, size, rhs), jnp.bfloat16),
            jax.ShapeDtypeStruct((rank, rhs), jnp.float32),
        ],
        input_output_aliases=aliases,
        cost_estimate=cost(time),
        compiler_params=pltpu.CompilerParams(
            dimension_semantics=("arbitrary",), vmem_limit_bytes=near_vmem
        ),
    )(neighbours, *args)


def odd(axis):
    return lax.rem(lax.axis_index(axis), 2)


def row_span(row, ext_row):
    return lambda srcs, ext: (srcs[0].at[row], ext.at[ext_row])


def near_middle(density, near_blocks, far_right, neighbours, prior):
    gu, gv = density.shape[:2]
    spans = [(max(row - 2, 0), row_span(row, row)) for row in range(gu)]
    parts = [(1, 1, lambda col=col: col, 1, 1, col) for col in range(1, gv - 1)]
    plan = (gu - 2, spans, parts)
    return near_part((density,), plan, (gu, gv), near_blocks, far_right, neighbours, prior, 8)


def near_rows(density, pu_near, pu_far, near_blocks, far_right, neighbours, prior):
    gu, gv = density.shape[:2]
    spans = [(at, row_span(row, ext_row)) for at, row, ext_row in ((0, 0, 1), (0, 1, 2), (1, gu - 2, 3), (1, gu - 1, 4))]
    spans.append((0, lambda srcs, ext: (srcs[1], ext.at[5 * (1 - odd("pu"))])))
    spans.append((0, lambda srcs, ext: (srcs[2], ext.at[5 * odd("pu")])))
    parts = [(0, gu - 1, lambda col=col: col, 1, 3, col) for col in range(1, gv - 1)]
    plan = (2, spans, parts)
    return near_part((density, pu_near, pu_far), plan, (6, gv), near_blocks, far_right, neighbours, prior, 1.5)


def near_columns(density, pu_near, pu_far, corner_near, corner_far, beside, ends, mids, near_blocks, far_right, neighbours, prior):
    gu, gv = density.shape[:2]
    per_step = 2
    spans = []
    parts = []

    def near_row():
        return (gu + 1) * (1 - odd("pu"))

    def far_row():
        return (gu + 1) * odd("pu")

    for far in (0, 1):

        def left_side(far=far):
            return 1 - odd("pv") if far else odd("pv")

        def inner(source, at, ext_row, far=far, left_side=left_side):
            def views(srcs, ext):
                view = srcs[source]
                if at is not None:
                    view = view.at[at]
                from_cols = pl.ds((gv - 2) * (1 - left_side()), 2)
                return view.at[from_cols], ext.at[ext_row(), pl.ds(3 * far + left_side(), 2)]

            return views

        def outer(source, at, ext_row, far=far, left_side=left_side):
            return lambda srcs, ext: (srcs[source].at[at], ext.at[ext_row(), 3 * far + 2 * (1 - left_side())])

        for row in range(gu):
            at = max((row - 1) // per_step, 0)
            here = lambda row=row: row + 1
            spans.append((at, inner(0, row, here)))
            if not far:
                spans.append((at, outer(5, row, here)))
            elif row in (0, gu - 1):
                spans.append((at, outer(6, min(row, 1), here)))
            else:
                spans.append((at, outer(7, row - 1, here)))
        spans.append((0, inner(1, None, near_row)))
        spans.append((0, inner(2, None, far_row)))
        spans.append((0, outer(3, far, near_row)))
        spans.append((0, outer(4, far, far_row)))
        col = lambda left_side=left_side: (gv - 1) * (1 - left_side())
        parts += [(row, per_step, col, row + 1, per_step, 3 * far + 1) for row in range(per_step)]
    plan = (gu // per_step, spans, parts)
    sources = (density, pu_near, pu_far, corner_near, corner_far, beside, ends, mids)
    return near_part(sources, plan, (gu + 2, 6), near_blocks, far_right, neighbours, prior, 1.5)


def corners_kernel(beside, ends, to_near, to_far):
    low = odd("pu")
    rows = beside.shape[0]
    for target, last in ((to_near, 1 - low), (to_far, low)):
        target[0] = beside[(rows - 1) * last]
        target[1] = ends[last]


def patch_corners(beside, ends):
    whole = pl.BlockSpec(memory_space=pltpu.VMEM)
    return pl.pallas_call(
        corners_kernel,
        in_specs=[whole, whole],
        out_specs=[whole, whole],
        out_shape=[jax.ShapeDtypeStruct(ends.shape, ends.dtype)] * 2,
        cost_estimate=cost(0.7),
        compiler_params=pltpu.CompilerParams(vmem_limit_bytes=merge_vmem),
    )(beside, ends)


def reciprocal(value):
    guess = pl.reciprocal(value, approx=True)
    return guess * (2.0 - value * guess)


def eliminate(w_k, w_e):
    size = w_k.shape[0]
    step = 32
    tile = 8
    sub = lax.broadcasted_iota(jnp.int32, (tile, size), 0)

    def spread(value, row):
        return jnp.broadcast_to(value[row : row + 1, :], (tile, size))

    for base in range(0, size, step):
        count = step // tile
        k_rows = [w_k[base + tile * r : base + tile * (r + 1), :] for r in range(count)]
        e_rows = [w_e[base + tile * r : base + tile * (r + 1), :] for r in range(count)]
        for q in range(count):
            at = base + tile * q
            cols = {
                (r, k): jnp.broadcast_to(k_rows[r][:, at + k : at + k + 1], (tile, size))
                for r in range(q, count)
                for k in range(tile)
            }
            k_done = k_rows[q]
            e_done = e_rows[q]
            for k in range(0, tile, 2):
                a = spread(cols[q, k], k)
                b = spread(cols[q, k], k + 1)
                c = spread(cols[q, k + 1], k + 1)
                det = a * c - b * b
                inverse = reciprocal(det)

                def solved(one, two):
                    return (c * one - b * two) * inverse, (a * two - b * one) * inverse

                k_one, k_two = spread(k_rows[q], k), spread(k_rows[q], k + 1)
                e_one, e_two = spread(e_rows[q], k), spread(e_rows[q], k + 1)
                k_solved = solved(k_one, k_two)
                e_solved = solved(e_one, e_two)
                links = {
                    m: solved(spread(cols[q, k], m), spread(cols[q, k + 1], m)) for m in range(k + 2, tile)
                }
                root = lax.rsqrt(a)
                second = lax.rsqrt(det) * a * root
                slope = b * root * root
                k_done = jnp.where(sub == k, k_one * root, k_done)
                e_done = jnp.where(sub == k, e_one * root, e_done)
                k_done = jnp.where(sub == k + 1, (k_two - slope * k_one) * second, k_done)
                e_done = jnp.where(sub == k + 1, (e_two - slope * e_one) * second, e_done)
                for r in range(q, count):
                    one, two = cols[r, k], cols[r, k + 1]
                    if r == q:
                        if k + 2 == tile:
                            continue
                        one = jnp.where(sub > k + 1, one, 0.0)
                        two = jnp.where(sub > k + 1, two, 0.0)
                    for m in range(k + 2, tile):
                        cols[r, m] = cols[r, m] - (one * links[m][0] + two * links[m][1])
                    k_rows[r] = k_rows[r] - (one * k_solved[0] + two * k_solved[1])
                    e_rows[r] = e_rows[r] - (one * e_solved[0] + two * e_solved[1])
            k_rows[q] = k_done
            e_rows[q] = e_done
        e_now = jnp.concatenate(e_rows, axis=0)
        w_e[base : base + step, :] = e_now
        if base + step < size:
            k_now = jnp.concatenate(k_rows, axis=0)
            k_hi = k_now.astype(jnp.bfloat16)
            k_lo = (k_now - k_hi.astype(jnp.float32)).astype(jnp.bfloat16)
            e_hi = e_now.astype(jnp.bfloat16)
            e_lo = (e_now - e_hi.astype(jnp.float32)).astype(jnp.bfloat16)
            lhs = jnp.concatenate([k_hi, k_hi, k_lo], axis=0)
            k_rhs = jnp.concatenate([k_hi, k_lo, k_hi], axis=0)
            e_rhs = jnp.concatenate([e_hi, e_lo, e_hi], axis=0)
            k_fall = dot_t(lhs, k_rhs, ((0,), (0,)))
            e_fall = dot_t(lhs, e_rhs, ((0,), (0,)))
            w_k[base + step :, :] -= k_fall[base + step :, :]
            w_e[base + step :, :] -= e_fall[base + step :, :]


tail_lanes = 128


def encode(value, key, out_ref):
    cols = value.shape[1]
    top = jnp.max(jnp.abs(value), axis=1, keepdims=True)
    power = jnp.clip(jnp.floor(jnp.log2(32000.0 / jnp.maximum(top, 1e-30))), -60.0, 60.0)
    scaled = jnp.floor(value * jnp.exp2(power) + 0.5)
    out_ref[:, :cols] = scaled.astype(jnp.int32).astype(jnp.int16)
    lanes = lax.broadcasted_iota(jnp.int32, (value.shape[0], tail_lanes), 1)
    out_ref[:, cols:] = jnp.where(lanes < tail_lanes // 2, power, key).astype(jnp.int32).astype(jnp.int16)


def decode(ref):
    cols = ref.shape[1] - tail_lanes
    tail = ref[:, cols:].astype(jnp.int32).astype(jnp.float32)
    value = ref[:, :cols].astype(jnp.int32).astype(jnp.float32) * jnp.exp2(-tail[:, :1])
    return value, tail[:, tail_lanes - 1 :]


def first_kernel(counts, order_hbm, value_hbm, sketch_hbm, density, code_ref, sketch_ref, *refs):
    beside, ends, mids, pu_near, pu_far, order, value, sketch, sems = refs
    gu, gv = density.shape[:2]
    near_col = (gv - 1) * (1 - odd("pv"))
    far_col = (gv - 1) * odd("pv")
    pairs = [(value_hbm.at[0, 0], value), (order_hbm, order), (sketch_hbm, sketch)]
    inputs = len(pairs)
    pairs += [(density.at[row, near_col], beside.at[row]) for row in range(gu)]
    pairs.append((density.at[(gu - 1) * (1 - odd("pu"))], pu_near))
    pairs.append((density.at[(gu - 1) * odd("pu")], pu_far))
    pairs += [(density.at[(gu - 1) * row, far_col], ends.at[row]) for row in range(2)]
    pairs += [(density.at[row + 1, far_col], mids.at[row]) for row in range(gu - 2)]
    copies = [
        pltpu.make_async_copy(source, target, sems.at[index])
        for index, (source, target) in enumerate(pairs)
    ]
    for copy in copies:
        copy.start()
    for copy in copies[:inputs]:
        copy.wait()
    key = order[lax.axis_index("pu") * counts[1] + lax.axis_index("pv")]
    encode(jnp.transpose(value[...]), key.astype(jnp.float32), code_ref)
    sketch_ref[...] = jnp.transpose(sketch[...])
    for copy in copies[inputs:]:
        copy.wait()


def first_step(value, sketch, density, order, counts):
    rows, cols = value.shape[2:]
    gu, gv, size, rhs = density.shape
    blocks = (gu, 2, gu - 2, gv, gv)
    whole = pl.BlockSpec(memory_space=pltpu.VMEM)
    held = pl.BlockSpec(memory_space=pltpu.HBM)
    args = [in_hbm(array) for array in (order, value, sketch, density)]
    return pl.pallas_call(
        functools.partial(first_kernel, counts),
        in_specs=[held] * len(args),
        out_specs=[whole] * (2 + len(blocks)),
        out_shape=[
            jax.ShapeDtypeStruct((cols, rows + tail_lanes), jnp.int16),
            jax.ShapeDtypeStruct(sketch.shape[::-1], jnp.float32),
        ]
        + [jax.ShapeDtypeStruct((count, size, rhs), density.dtype) for count in blocks],
        scratch_shapes=[
            pltpu.SMEM(order.shape, jnp.int32),
            pltpu.VMEM((rows, cols), jnp.float32),
            pltpu.VMEM(sketch.shape, jnp.float32),
            pltpu.SemaphoreType.DMA((2 * gu + 5,)),
        ],
        cost_estimate=cost(3),
        compiler_params=pltpu.CompilerParams(vmem_limit_bytes=merge_vmem),
    )(*args)


natural = ((1,), (0,))


def merge_kernel(has_path, last, mine_ref, other_ref, sketch_ref, *refs):
    if has_path:
        path_ref, *refs = refs
    left_ref, new_path_ref, w_k, w_e, z_ref = refs
    rank = mine_ref.shape[0]
    mine, my_key = decode(mine_ref)
    other, other_key = decode(other_ref)
    lead = my_key < other_key
    z_ref[:rank, :] = jnp.where(lead, mine, other)
    z_ref[rank:, :] = jnp.where(lead, other, mine)
    stacked = z_ref[...]
    sketch = sketch_ref[...]
    gram = split_dot(stacked, stacked, ((1,), (1,)))
    reduced = split_dot(sketch, gram, natural)
    w_k[...] = split_dot(reduced, sketch, ((1,), (1,)))
    rows = lax.broadcasted_iota(jnp.int32, (rank, rank), 0)
    cols = lax.broadcasted_iota(jnp.int32, (rank, rank), 1)
    w_e[...] = jnp.where(rows == cols, 1.0, 0.0)
    own = jnp.where(lead, reduced[:, :rank], reduced[:, rank:])
    if has_path:
        own = split_dot(own, path_ref[...], natural)
    eliminate(w_k, w_e)
    inverse = w_e[...]
    mixed = split_dot(inverse, sketch, natural)
    if last:
        count = left_ref.shape[1]
        part = z_ref[:, pl.ds(pl.multiple_of(lax.axis_index("pu") * count, 128), count)]
        left_ref[...] = split_dot(mixed, part, natural)
    else:
        encode(split_dot(mixed, z_ref[...], natural), jnp.minimum(my_key, other_key), left_ref)
    new_path_ref[...] = split_dot(inverse, own, natural)


def merge(level, mine, other, sketch, path, last_rows):
    rank, cols = mine.shape
    whole = pl.BlockSpec(memory_space=pltpu.VMEM)
    paths = () if path is None else (path,)
    if last_rows:
        left = jax.ShapeDtypeStruct((rank, last_rows), jnp.float32)
    else:
        left = jax.ShapeDtypeStruct(mine.shape, jnp.int16)
    return pl.pallas_call(
        functools.partial(merge_kernel, bool(paths), bool(last_rows)),
        in_specs=[whole, whole, whole] + [whole] * len(paths),
        out_specs=[whole, whole],
        out_shape=[left, jax.ShapeDtypeStruct((rank, rank), jnp.float32)],
        scratch_shapes=[
            pltpu.VMEM((rank, rank), jnp.float32),
            pltpu.VMEM((rank, rank), jnp.float32),
            pltpu.VMEM((2 * rank, cols - tail_lanes), jnp.float32),
        ],
        cost_estimate=cost(4 if level < 2 else 2),
        compiler_params=pltpu.CompilerParams(vmem_limit_bytes=merge_vmem),
    )(mine, other, sketch, *paths)


def from_partner(value, axis, distance):
    mask = 2**distance
    pairs = [(source, source ^ mask) for source in range(lax.axis_size(axis))]
    return lax.ppermute(value, axis, pairs)


def swapped(value, axis, far):
    count = lax.axis_size(axis)
    pairs = []
    for low in range(int(far), count - 1, 2):
        pairs += [(low, low + 1), (low + 1, low)]
    return lax.ppermute(value, axis, pairs)


def tied(*values):
    return lax.optimization_barrier(values)


def per_device(density, near_blocks, neighbours, far_right, far_left, sketch, patch_order):
    pu_count = lax.axis_size("pu")
    pv_count = lax.axis_size("pv")
    pv_index = lax.axis_index("pv")
    rhs = density.shape[3]
    pv_levels = pv_count.bit_length() - 1
    pu_levels = pu_count.bit_length() - 1
    levels = pv_levels + pu_levels

    def partner(value, level):
        if level < pv_levels:
            return from_partner(value, "pv", level)
        return from_partner(value, "pu", level - pv_levels)

    def scattered(share, level):
        bit = (pv_index >> level) & 1
        pairs = share.reshape(share.shape[0] // 2, 2, *share.shape[1:])
        keep = lax.dynamic_index_in_dim(pairs, bit, 1, keepdims=False)
        give = lax.dynamic_index_in_dim(pairs, 1 - bit, 1, keepdims=False)
        return keep + from_partner(give, "pv", level)

    rows = far_left.shape[2]
    left, sketch, beside, ends, mids, pu_near, pu_far = first_step(
        far_left, sketch, density, patch_order, (pu_count, pv_count)
    )
    other = partner(left, 0)
    beside = swapped(beside, "pv", False)
    pu_near = swapped(pu_near, "pu", False)
    pu_far = swapped(pu_far, "pu", True)

    coefs = []
    corrected = share = None
    pv_path = pu_path = None
    for level in range(levels):
        last = level == levels - 1
        coef = None
        if level:
            other = partner(left, level)
        if level in (1, 2) or last:
            links, left = tied(neighbours, left)
        if level == 1:
            corrected, coef = near_middle(density, near_blocks, far_right, links, corrected)
        elif level == 2:
            ends, mids, left = tied(ends, mids, left)
            ends = swapped(ends, "pv", True)
            mids = swapped(mids, "pv", True)
            corrected, coef = near_rows(density, pu_near, pu_far, near_blocks, far_right, links, corrected)
        elif last:
            corner_near, corner_far = patch_corners(beside, ends)
            corner_near = swapped(corner_near, "pu", False)
            corner_far = swapped(corner_far, "pu", True)
            corrected, coef = near_columns(
                density,
                pu_near,
                pu_far,
                corner_near,
                corner_far,
                beside,
                ends,
                mids,
                near_blocks,
                far_right,
                links,
                corrected,
            )
        if coef is not None:
            other, coef = tied(other, coef)
            coefs.append(coef)
        if last:
            coef = functools.reduce(lambda a, b: a + b, coefs)
            share = lax.dot_general(coef, pv_path, (((0,), (1,)), ((), ())), precision=high)
            share = share.reshape(pv_count, rhs // pv_count, -1)
            share, other = tied(share, other)
            share = scattered(share, 0)
        path = pv_path if level < pv_levels else pu_path
        last_rows = rows // pu_count if last else 0
        left, path = merge(level, left, other, sketch, path, last_rows)
        if level < pv_levels:
            pv_path = path
        else:
            pu_path = path

    share, left = tied(share, left)
    for level in range(1, pv_levels):
        share = scattered(share, level)
    root_coef = lax.dot_general(share[0], pu_path, (((1,), (1,)), ((), ())), precision=high)
    for level in range(pu_levels):
        root_coef = root_coef + from_partner(root_coef, "pu", level)
    far_field = lax.dot_general(left, root_coef, (((0,), (1,)), ((), ())), precision=high)
    return (corrected, far_field)


def solution(mesh):
    in_specs = (
        P("pu", "pv", None, None),
        P("pu", "pv", None, None, None),
        P("pu", "pv", None),
        P("pu", "pv", None, None),
        P("pu", "pv", None, None),
        P(),
        P(),
    )
    out_specs = (P("pu", "pv", None, None), P("pu", "pv"))
    return jax.shard_map(
        per_device, mesh=mesh, in_specs=in_specs, out_specs=out_specs, check_vma=False
    )
```

```python
import functools

import jax
import jax.numpy as jnp
from jax import lax
from jax.experimental import pallas as pl
from jax.experimental.pallas import tpu as pltpu
from jax.sharding import PartitionSpec as P

high = lax.Precision.HIGH
empty_slot = 9
near_vmem = 18 * 1024 * 1024
merge_vmem = 12 * 1024 * 1024


def dot_t(a, b, dims, precision=None):
    return lax.dot_general(
        a, b, (dims, ((), ())), precision=precision, preferred_element_type=jnp.float32
    )


def split_dot(a, b, dims):
    return dot_t(a, b, dims, high)


def in_hbm(value):
    return pltpu.with_memory_space_constraint(value, pltpu.HBM)


def cost(microseconds):
    return pl.CostEstimate(flops=int(microseconds * 1.1e9), bytes_accessed=0, transcendentals=0)


def near_kernel(plan, n_src, nb_ref, near_hbm, right_hbm, *refs):
    steps, spans, parts = plan
    srcs = refs[:n_src]
    out_ref, coef_ref, ext_ref, near_ref, right_ref, stage_ref, sems, out_sems = refs[-8:]
    step = pl.program_id(0)
    count = len(parts)

    def fetch(at_step):
        found = []
        for index, (needed, views) in enumerate(spans):
            if needed == at_step:
                source, target = views(srcs, ext_ref)
                found.append(pltpu.make_async_copy(source, target, sems.at[index]))
        for part, (row, by, col, *_) in enumerate(parts):
            at = len(spans) + 2 * (at_step * count + part)
            for offset, source, target in ((0, near_hbm, near_ref), (1, right_hbm, right_ref)):
                found.append(
                    pltpu.make_async_copy(
                        source.at[row + by * at_step, col()], target.at[at_step, part], sems.at[at + offset]
                    )
                )
        return found

    def send(place, at_step, part):
        row, by, col = parts[part][:3]
        return pltpu.make_async_copy(
            stage_ref.at[place, part], out_ref.at[row + by * at_step, col()], out_sems.at[place, part]
        )

    @pl.when(step == 0)
    def _():
        for at_step in range(steps):
            for copy in fetch(at_step):
                copy.start()

    for at_step in range(steps):

        @pl.when(step == at_step)
        def _():
            for copy in fetch(at_step):
                copy.wait()

    place = lax.rem(step, 2)

    @pl.when(step >= 2)
    def _():
        for part in range(count):
            send(place, step - 2, part).wait()

    rhs = ext_ref.shape[-1]
    tile = 256 if rhs % 256 == 0 else rhs
    for part, (row, by, col, ext_row, ext_by, middle) in enumerate(parts):
        centre = ext_row + ext_by * step
        weights = []
        places = []
        for slot in range(near_ref.shape[2]):
            link = nb_ref[row + by * step, col(), slot]
            there = jnp.minimum(link, empty_slot - 1)
            weight = near_ref[step, part, slot]
            weights.append(jnp.where(link < empty_slot, weight, jnp.zeros_like(weight)))
            places.append((centre - 1 + lax.div(there, 3), middle - 1 + lax.rem(there, 3)))
        weights = jnp.concatenate(weights, axis=1)
        for at in range(0, rhs, tile):
            values = [ext_ref[i, j, :, at : at + tile] for i, j in places]
            total = jnp.dot(weights, jnp.concatenate(values, axis=0), preferred_element_type=jnp.float32)
            own = ext_ref[centre, middle, :, at : at + tile].astype(jnp.float32)
            stage_ref[place, part, :, at : at + tile] = (own + total).astype(jnp.bfloat16)
        send(place, step, part).start()
    rights = jnp.concatenate([right_ref[step, part] for part in range(count)], axis=0)
    blocks = jnp.concatenate([stage_ref[place, part] for part in range(count)], axis=0)
    coef = dot_t(rights, blocks, ((0,), (0,)))

    @pl.when(step == 0)
    def _():
        coef_ref[...] = coef

    @pl.when(step > 0)
    def _():
        coef_ref[...] += coef

    @pl.when(step == steps - 1)
    def _():
        for at_step in range(max(steps - 2, 0), steps):
            for part in range(count):
                send(at_step % 2, at_step, part).wait()


def near_part(sources, plan, ext_shape, near_blocks, far_right, neighbours, prior, time):
    steps, spans, parts = plan
    count = len(parts)
    gu, gv, slots, size, _ = near_blocks.shape
    rhs = sources[0].shape[-1]
    rank = far_right.shape[-1]
    args = [near_blocks, far_right, *sources]
    args = [in_hbm(value) if value.ndim > 3 else value for value in args]
    aliases = {}
    if prior is not None:
        args.append(prior)
        aliases = {len(args): 0}
    held = pl.BlockSpec(memory_space=pltpu.HBM)
    return pl.pallas_call(
        functools.partial(near_kernel, plan, len(sources)),
        grid_spec=pltpu.PrefetchScalarGridSpec(
            num_scalar_prefetch=1,
            grid=(steps,),
            in_specs=[held, held]
            + [held if source.ndim == 4 else pl.BlockSpec(memory_space=pl.ANY) for source in sources]
            + [held] * len(aliases),
            out_specs=[held, pl.BlockSpec((rank, rhs), lambda i, nb: (0, 0))],
            scratch_shapes=[
                pltpu.VMEM((*ext_shape, size, rhs), jnp.bfloat16),
                pltpu.VMEM((steps, count, slots, size, size), jnp.bfloat16),
                pltpu.VMEM((steps, count, size, rank), jnp.bfloat16),
                pltpu.VMEM((2, count, size, rhs), jnp.bfloat16),
                pltpu.SemaphoreType.DMA((len(spans) + 2 * steps * count,)),
                pltpu.SemaphoreType.DMA((2, count)),
            ],
        ),
        out_shape=[
            jax.ShapeDtypeStruct((gu, gv, size, rhs), jnp.bfloat16),
            jax.ShapeDtypeStruct((rank, rhs), jnp.float32),
        ],
        input_output_aliases=aliases,
        cost_estimate=cost(time),
        compiler_params=pltpu.CompilerParams(
            dimension_semantics=("arbitrary",), vmem_limit_bytes=near_vmem
        ),
    )(neighbours, *args)


def odd(axis):
    return lax.rem(lax.axis_index(axis), 2)


def row_span(row, ext_row):
    return lambda srcs, ext: (srcs[0].at[row], ext.at[ext_row])


def near_middle(density, near_blocks, far_right, neighbours, prior):
    gu, gv = density.shape[:2]
    spans = [(max(row - 2, 0), row_span(row, row)) for row in range(gu)]
    parts = [(1, 1, lambda col=col: col, 1, 1, col) for col in range(1, gv - 1)]
    plan = (gu - 2, spans, parts)
    return near_part((density,), plan, (gu, gv), near_blocks, far_right, neighbours, prior, 1.5)


def near_rows(density, pu_near, pu_far, near_blocks, far_right, neighbours, prior):
    gu, gv = density.shape[:2]
    spans = [(at, row_span(row, ext_row)) for at, row, ext_row in ((0, 0, 1), (0, 1, 2), (1, gu - 2, 3), (1, gu - 1, 4))]
    spans.append((0, lambda srcs, ext: (srcs[1], ext.at[5 * (1 - odd("pu"))])))
    spans.append((0, lambda srcs, ext: (srcs[2], ext.at[5 * odd("pu")])))
    parts = [(0, gu - 1, lambda col=col: col, 1, 3, col) for col in range(1, gv - 1)]
    plan = (2, spans, parts)
    return near_part((density, pu_near, pu_far), plan, (6, gv), near_blocks, far_right, neighbours, prior, 1.5)


def near_columns(density, pu_near, pu_far, corner_near, corner_far, beside, ends, mids, near_blocks, far_right, neighbours, prior):
    gu, gv = density.shape[:2]
    per_step = 2
    spans = []
    parts = []

    def near_row():
        return (gu + 1) * (1 - odd("pu"))

    def far_row():
        return (gu + 1) * odd("pu")

    for far in (0, 1):

        def left_side(far=far):
            return 1 - odd("pv") if far else odd("pv")

        def inner(source, at, ext_row, far=far, left_side=left_side):
            def views(srcs, ext):
                view = srcs[source]
                if at is not None:
                    view = view.at[at]
                from_cols = pl.ds((gv - 2) * (1 - left_side()), 2)
                return view.at[from_cols], ext.at[ext_row(), pl.ds(3 * far + left_side(), 2)]

            return views

        def outer(source, at, ext_row, far=far, left_side=left_side):
            return lambda srcs, ext: (srcs[source].at[at], ext.at[ext_row(), 3 * far + 2 * (1 - left_side())])

        for row in range(gu):
            at = max((row - 1) // per_step, 0)
            here = lambda row=row: row + 1
            spans.append((at, inner(0, row, here)))
            if not far:
                spans.append((at, outer(5, row, here)))
            elif row in (0, gu - 1):
                spans.append((at, outer(6, min(row, 1), here)))
            else:
                spans.append((at, outer(7, row - 1, here)))
        spans.append((0, inner(1, None, near_row)))
        spans.append((0, inner(2, None, far_row)))
        spans.append((0, outer(3, far, near_row)))
        spans.append((0, outer(4, far, far_row)))
        col = lambda left_side=left_side: (gv - 1) * (1 - left_side())
        parts += [(row, per_step, col, row + 1, per_step, 3 * far + 1) for row in range(per_step)]
    plan = (gu // per_step, spans, parts)
    sources = (density, pu_near, pu_far, corner_near, corner_far, beside, ends, mids)
    return near_part(sources, plan, (gu + 2, 6), near_blocks, far_right, neighbours, prior, 1.5)


def corners_kernel(beside, ends, to_near, to_far):
    low = odd("pu")
    rows = beside.shape[0]
    for target, last in ((to_near, 1 - low), (to_far, low)):
        target[0] = beside[(rows - 1) * last]
        target[1] = ends[last]


def patch_corners(beside, ends):
    whole = pl.BlockSpec(memory_space=pltpu.VMEM)
    return pl.pallas_call(
        corners_kernel,
        in_specs=[whole, whole],
        out_specs=[whole, whole],
        out_shape=[jax.ShapeDtypeStruct(ends.shape, ends.dtype)] * 2,
        cost_estimate=cost(0.7),
        compiler_params=pltpu.CompilerParams(vmem_limit_bytes=merge_vmem),
    )(beside, ends)


def reciprocal(value):
    guess = pl.reciprocal(value, approx=True)
    return guess * (2.0 - value * guess)


def eliminate(w_k, w_e):
    size = w_k.shape[0]
    step = 32
    tile = 8
    sub = lax.broadcasted_iota(jnp.int32, (tile, size), 0)

    def spread(value, row):
        return jnp.broadcast_to(value[row : row + 1, :], (tile, size))

    for base in range(0, size, step):
        count = step // tile
        k_rows = [w_k[base + tile * r : base + tile * (r + 1), :] for r in range(count)]
        e_rows = [w_e[base + tile * r : base + tile * (r + 1), :] for r in range(count)]
        for q in range(count):
            at = base + tile * q
            cols = {
                (r, k): jnp.broadcast_to(k_rows[r][:, at + k : at + k + 1], (tile, size))
                for r in range(q, count)
                for k in range(tile)
            }
            k_done = k_rows[q]
            e_done = e_rows[q]
            for k in range(0, tile, 2):
                a = spread(cols[q, k], k)
                b = spread(cols[q, k], k + 1)
                c = spread(cols[q, k + 1], k + 1)
                det = a * c - b * b
                inverse = reciprocal(det)

                def solved(one, two):
                    return (c * one - b * two) * inverse, (a * two - b * one) * inverse

                k_one, k_two = spread(k_rows[q], k), spread(k_rows[q], k + 1)
                e_one, e_two = spread(e_rows[q], k), spread(e_rows[q], k + 1)
                k_solved = solved(k_one, k_two)
                e_solved = solved(e_one, e_two)
                links = {
                    m: solved(spread(cols[q, k], m), spread(cols[q, k + 1], m)) for m in range(k + 2, tile)
                }
                root = lax.rsqrt(a)
                second = lax.rsqrt(det) * a * root
                slope = b * root * root
                k_done = jnp.where(sub == k, k_one * root, k_done)
                e_done = jnp.where(sub == k, e_one * root, e_done)
                k_done = jnp.where(sub == k + 1, (k_two - slope * k_one) * second, k_done)
                e_done = jnp.where(sub == k + 1, (e_two - slope * e_one) * second, e_done)
                for r in range(q, count):
                    one, two = cols[r, k], cols[r, k + 1]
                    if r == q:
                        if k + 2 == tile:
                            continue
                        one = jnp.where(sub > k + 1, one, 0.0)
                        two = jnp.where(sub > k + 1, two, 0.0)
                    for m in range(k + 2, tile):
                        cols[r, m] = cols[r, m] - (one * links[m][0] + two * links[m][1])
                    k_rows[r] = k_rows[r] - (one * k_solved[0] + two * k_solved[1])
                    e_rows[r] = e_rows[r] - (one * e_solved[0] + two * e_solved[1])
            k_rows[q] = k_done
            e_rows[q] = e_done
        e_now = jnp.concatenate(e_rows, axis=0)
        w_e[base : base + step, :] = e_now
        if base + step < size:
            k_now = jnp.concatenate(k_rows, axis=0)
            k_hi = k_now.astype(jnp.bfloat16)
            k_lo = (k_now - k_hi.astype(jnp.float32)).astype(jnp.bfloat16)
            e_hi = e_now.astype(jnp.bfloat16)
            e_lo = (e_now - e_hi.astype(jnp.float32)).astype(jnp.bfloat16)
            lhs = jnp.concatenate([k_hi, k_hi, k_lo], axis=0)
            k_rhs = jnp.concatenate([k_hi, k_lo, k_hi], axis=0)
            e_rhs = jnp.concatenate([e_hi, e_lo, e_hi], axis=0)
            k_fall = dot_t(lhs, k_rhs, ((0,), (0,)))
            e_fall = dot_t(lhs, e_rhs, ((0,), (0,)))
            w_k[base + step :, :] -= k_fall[base + step :, :]
            w_e[base + step :, :] -= e_fall[base + step :, :]


tail_lanes = 128


def encode(value, key, out_ref):
    cols = value.shape[1]
    top = jnp.max(jnp.abs(value), axis=1, keepdims=True)
    power = jnp.clip(jnp.floor(jnp.log2(32000.0 / jnp.maximum(top, 1e-30))), -60.0, 60.0)
    scaled = jnp.floor(value * jnp.exp2(power) + 0.5)
    out_ref[:, :cols] = scaled.astype(jnp.int32).astype(jnp.int16)
    lanes = lax.broadcasted_iota(jnp.int32, (value.shape[0], tail_lanes), 1)
    out_ref[:, cols:] = jnp.where(lanes < tail_lanes // 2, power, key).astype(jnp.int32).astype(jnp.int16)


def decode(ref):
    cols = ref.shape[1] - tail_lanes
    tail = ref[:, cols:].astype(jnp.int32).astype(jnp.float32)
    value = ref[:, :cols].astype(jnp.int32).astype(jnp.float32) * jnp.exp2(-tail[:, :1])
    return value, tail[:, tail_lanes - 1 :]


def first_kernel(counts, order_hbm, value_hbm, sketch_hbm, density, code_ref, sketch_ref, *refs):
    beside, ends, mids, pu_near, pu_far, order, value, sketch, sems = refs
    gu, gv = density.shape[:2]
    near_col = (gv - 1) * (1 - odd("pv"))
    far_col = (gv - 1) * odd("pv")
    pairs = [(value_hbm.at[0, 0], value), (order_hbm, order), (sketch_hbm, sketch)]
    inputs = len(pairs)
    pairs += [(density.at[row, near_col], beside.at[row]) for row in range(gu)]
    pairs.append((density.at[(gu - 1) * (1 - odd("pu"))], pu_near))
    pairs.append((density.at[(gu - 1) * odd("pu")], pu_far))
    pairs += [(density.at[(gu - 1) * row, far_col], ends.at[row]) for row in range(2)]
    pairs += [(density.at[row + 1, far_col], mids.at[row]) for row in range(gu - 2)]
    copies = [
        pltpu.make_async_copy(source, target, sems.at[index])
        for index, (source, target) in enumerate(pairs)
    ]
    for copy in copies:
        copy.start()
    for copy in copies[:inputs]:
        copy.wait()
    key = order[lax.axis_index("pu") * counts[1] + lax.axis_index("pv")]
    encode(jnp.transpose(value[...]), key.astype(jnp.float32), code_ref)
    sketch_ref[...] = jnp.transpose(sketch[...])
    for copy in copies[inputs:]:
        copy.wait()


def first_step(value, sketch, density, order, counts):
    rows, cols = value.shape[2:]
    gu, gv, size, rhs = density.shape
    blocks = (gu, 2, gu - 2, gv, gv)
    whole = pl.BlockSpec(memory_space=pltpu.VMEM)
    held = pl.BlockSpec(memory_space=pltpu.HBM)
    args = [in_hbm(array) for array in (order, value, sketch, density)]
    return pl.pallas_call(
        functools.partial(first_kernel, counts),
        in_specs=[held] * len(args),
        out_specs=[whole] * (2 + len(blocks)),
        out_shape=[
            jax.ShapeDtypeStruct((cols, rows + tail_lanes), jnp.int16),
            jax.ShapeDtypeStruct(sketch.shape[::-1], jnp.float32),
        ]
        + [jax.ShapeDtypeStruct((count, size, rhs), density.dtype) for count in blocks],
        scratch_shapes=[
            pltpu.SMEM(order.shape, jnp.int32),
            pltpu.VMEM((rows, cols), jnp.float32),
            pltpu.VMEM(sketch.shape, jnp.float32),
            pltpu.SemaphoreType.DMA((2 * gu + 5,)),
        ],
        cost_estimate=cost(3),
        compiler_params=pltpu.CompilerParams(vmem_limit_bytes=merge_vmem),
    )(*args)


natural = ((1,), (0,))


def merge_kernel(has_path, last, mine_ref, other_ref, sketch_ref, *refs):
    if has_path:
        path_ref, *refs = refs
    left_ref, new_path_ref, w_k, w_e, z_ref = refs
    rank = mine_ref.shape[0]
    mine, my_key = decode(mine_ref)
    other, other_key = decode(other_ref)
    lead = my_key < other_key
    z_ref[:rank, :] = jnp.where(lead, mine, other)
    z_ref[rank:, :] = jnp.where(lead, other, mine)
    stacked = z_ref[...]
    sketch = sketch_ref[...]
    gram = split_dot(stacked, stacked, ((1,), (1,)))
    reduced = split_dot(sketch, gram, natural)
    w_k[...] = split_dot(reduced, sketch, ((1,), (1,)))
    rows = lax.broadcasted_iota(jnp.int32, (rank, rank), 0)
    cols = lax.broadcasted_iota(jnp.int32, (rank, rank), 1)
    w_e[...] = jnp.where(rows == cols, 1.0, 0.0)
    own = jnp.where(lead, reduced[:, :rank], reduced[:, rank:])
    if has_path:
        own = split_dot(own, path_ref[...], natural)
    eliminate(w_k, w_e)
    inverse = w_e[...]
    mixed = split_dot(inverse, sketch, natural)
    if last:
        count = left_ref.shape[1]
        part = z_ref[:, pl.ds(pl.multiple_of(lax.axis_index("pu") * count, 128), count)]
        left_ref[...] = split_dot(mixed, part, natural)
    else:
        encode(split_dot(mixed, z_ref[...], natural), jnp.minimum(my_key, other_key), left_ref)
    new_path_ref[...] = split_dot(inverse, own, natural)


def merge(level, mine, other, sketch, path, last_rows):
    rank, cols = mine.shape
    whole = pl.BlockSpec(memory_space=pltpu.VMEM)
    paths = () if path is None else (path,)
    if last_rows:
        left = jax.ShapeDtypeStruct((rank, last_rows), jnp.float32)
    else:
        left = jax.ShapeDtypeStruct(mine.shape, jnp.int16)
    return pl.pallas_call(
        functools.partial(merge_kernel, bool(paths), bool(last_rows)),
        in_specs=[whole, whole, whole] + [whole] * len(paths),
        out_specs=[whole, whole],
        out_shape=[left, jax.ShapeDtypeStruct((rank, rank), jnp.float32)],
        scratch_shapes=[
            pltpu.VMEM((rank, rank), jnp.float32),
            pltpu.VMEM((rank, rank), jnp.float32),
            pltpu.VMEM((2 * rank, cols - tail_lanes), jnp.float32),
        ],
        cost_estimate=cost((9, 1.5)[level] if level < 2 else 2),
        compiler_params=pltpu.CompilerParams(vmem_limit_bytes=merge_vmem),
    )(mine, other, sketch, *paths)


def from_partner(value, axis, distance):
    mask = 2**distance
    pairs = [(source, source ^ mask) for source in range(lax.axis_size(axis))]
    return lax.ppermute(value, axis, pairs)


def swapped(value, axis, far):
    count = lax.axis_size(axis)
    pairs = []
    for low in range(int(far), count - 1, 2):
        pairs += [(low, low + 1), (low + 1, low)]
    return lax.ppermute(value, axis, pairs)


def tied(*values):
    return lax.optimization_barrier(values)


def per_device(density, near_blocks, neighbours, far_right, far_left, sketch, patch_order):
    pu_count = lax.axis_size("pu")
    pv_count = lax.axis_size("pv")
    pv_index = lax.axis_index("pv")
    rhs = density.shape[3]
    pv_levels = pv_count.bit_length() - 1
    pu_levels = pu_count.bit_length() - 1
    levels = pv_levels + pu_levels

    def partner(value, level):
        if level < pv_levels:
            return from_partner(value, "pv", level)
        return from_partner(value, "pu", level - pv_levels)

    def scattered(share, level):
        bit = (pv_index >> level) & 1
        pairs = share.reshape(share.shape[0] // 2, 2, *share.shape[1:])
        keep = lax.dynamic_index_in_dim(pairs, bit, 1, keepdims=False)
        give = lax.dynamic_index_in_dim(pairs, 1 - bit, 1, keepdims=False)
        return keep + from_partner(give, "pv", level)

    rows = far_left.shape[2]
    left, sketch, beside, ends, mids, pu_near, pu_far = first_step(
        far_left, sketch, density, patch_order, (pu_count, pv_count)
    )
    other = partner(left, 0)
    beside = swapped(beside, "pv", False)
    pu_near = swapped(pu_near, "pu", False)
    pu_far = swapped(pu_far, "pu", True)

    coefs = []
    corrected = share = None
    pv_path = pu_path = None
    for level in range(levels):
        coef = None
        if level:
            other = partner(left, level)
        if level in (1, 2, pv_levels):
            links, left = tied(neighbours, left)
        if level == 1:
            ends, mids, left = tied(ends, mids, left)
            ends = swapped(ends, "pv", True)
            mids = swapped(mids, "pv", True)
            corrected, coef = near_rows(density, pu_near, pu_far, near_blocks, far_right, links, corrected)
        elif level == 2:
            corrected, coef = near_middle(density, near_blocks, far_right, links, corrected)
        elif level == pv_levels:
            beside, ends, coefs[-1] = tied(beside, ends, coefs[-1])
            corner_near, corner_far = patch_corners(beside, ends)
            corner_near = swapped(corner_near, "pu", False)
            corner_far = swapped(corner_far, "pu", True)
            corrected, coef = near_columns(
                density,
                pu_near,
                pu_far,
                corner_near,
                corner_far,
                beside,
                ends,
                mids,
                near_blocks,
                far_right,
                links,
                corrected,
            )
        if coef is not None:
            other, coef = tied(other, coef)
            coefs.append(coef)
        if level == pv_levels:
            coef = functools.reduce(lambda a, b: a + b, coefs)
            share = lax.dot_general(coef, pv_path, (((0,), (1,)), ((), ())), precision=high)
            share = share.reshape(pv_count, rhs // pv_count, -1)
        if pv_levels <= level < 2 * pv_levels:
            share, other = tied(share, other)
            share = scattered(share, level - pv_levels)
        path = pv_path if level < pv_levels else pu_path
        last_rows = rows // pu_count if level == levels - 1 else 0
        left, path = merge(level, left, other, sketch, path, last_rows)
        if level < pv_levels:
            pv_path = path
        else:
            pu_path = path

    share, left = tied(share, left)
    for level in range(pu_levels, pv_levels):
        share = scattered(share, level)
    root_coef = lax.dot_general(share[0], pu_path, (((1,), (1,)), ((), ())), precision=high)
    for level in range(pu_levels):
        root_coef = root_coef + from_partner(root_coef, "pu", level)
    far_field = lax.dot_general(left, root_coef, (((0,), (1,)), ((), ())), precision=high)
    return (corrected, far_field)


def solution(mesh):
    in_specs = (
        P("pu", "pv", None, None),
        P("pu", "pv", None, None, None),
        P("pu", "pv", None),
        P("pu", "pv", None, None),
        P("pu", "pv", None, None),
        P(),
        P(),
    )
    out_specs = (P("pu", "pv", None, None), P("pu", "pv"))
    return jax.shard_map(
        per_device, mesh=mesh, in_specs=in_specs, out_specs=out_specs, check_vma=False
    )
```

```python
import functools

import jax
import jax.numpy as jnp
from jax import lax
from jax.experimental import pallas as pl
from jax.experimental.pallas import tpu as pltpu
from jax.sharding import PartitionSpec as P

high = lax.Precision.HIGH
empty_slot = 9
near_vmem = 18 * 1024 * 1024
merge_vmem = 12 * 1024 * 1024


def dot_t(a, b, dims, precision=None):
    return lax.dot_general(
        a, b, (dims, ((), ())), precision=precision, preferred_element_type=jnp.float32
    )


def split_dot(a, b, dims):
    return dot_t(a, b, dims, high)


def in_hbm(value):
    return pltpu.with_memory_space_constraint(value, pltpu.HBM)


def cost(microseconds):
    return pl.CostEstimate(flops=int(microseconds * 1.1e9), bytes_accessed=0, transcendentals=0)


def near_kernel(plan, n_src, nb_ref, near_hbm, right_hbm, *refs):
    steps, spans, parts = plan
    srcs = refs[:n_src]
    out_ref, coef_ref, ext_ref, near_ref, right_ref, stage_ref, sems, out_sems = refs[-8:]
    step = pl.program_id(0)
    count = len(parts)

    def fetch(at_step):
        found = []
        for index, (needed, views) in enumerate(spans):
            if needed == at_step:
                source, target = views(srcs, ext_ref)
                found.append(pltpu.make_async_copy(source, target, sems.at[index]))
        for part, (row, by, col, *_) in enumerate(parts):
            at = len(spans) + 2 * (at_step * count + part)
            for offset, source, target in ((0, near_hbm, near_ref), (1, right_hbm, right_ref)):
                found.append(
                    pltpu.make_async_copy(
                        source.at[row + by * at_step, col()], target.at[at_step, part], sems.at[at + offset]
                    )
                )
        return found

    def send(place, at_step, part):
        row, by, col = parts[part][:3]
        return pltpu.make_async_copy(
            stage_ref.at[place, part], out_ref.at[row + by * at_step, col()], out_sems.at[place, part]
        )

    @pl.when(step == 0)
    def _():
        for at_step in range(steps):
            for copy in fetch(at_step):
                copy.start()

    for at_step in range(steps):

        @pl.when(step == at_step)
        def _():
            for copy in fetch(at_step):
                copy.wait()

    place = lax.rem(step, 2)

    @pl.when(step >= 2)
    def _():
        for part in range(count):
            send(place, step - 2, part).wait()

    rhs = ext_ref.shape[-1]
    tile = 256 if rhs % 256 == 0 else rhs
    for part, (row, by, col, ext_row, ext_by, middle) in enumerate(parts):
        centre = ext_row + ext_by * step
        weights = []
        places = []
        for slot in range(near_ref.shape[2]):
            link = nb_ref[row + by * step, col(), slot]
            there = jnp.minimum(link, empty_slot - 1)
            weight = near_ref[step, part, slot]
            weights.append(jnp.where(link < empty_slot, weight, jnp.zeros_like(weight)))
            places.append((centre - 1 + lax.div(there, 3), middle - 1 + lax.rem(there, 3)))
        weights = jnp.concatenate(weights, axis=1)
        for at in range(0, rhs, tile):
            values = [ext_ref[i, j, :, at : at + tile] for i, j in places]
            total = jnp.dot(weights, jnp.concatenate(values, axis=0), preferred_element_type=jnp.float32)
            own = ext_ref[centre, middle, :, at : at + tile].astype(jnp.float32)
            stage_ref[place, part, :, at : at + tile] = (own + total).astype(jnp.bfloat16)
        send(place, step, part).start()
    rights = jnp.concatenate([right_ref[step, part] for part in range(count)], axis=0)
    blocks = jnp.concatenate([stage_ref[place, part] for part in range(count)], axis=0)
    coef = dot_t(rights, blocks, ((0,), (0,)))

    @pl.when(step == 0)
    def _():
        coef_ref[...] = coef

    @pl.when(step > 0)
    def _():
        coef_ref[...] += coef

    @pl.when(step == steps - 1)
    def _():
        for at_step in range(max(steps - 2, 0), steps):
            for part in range(count):
                send(at_step % 2, at_step, part).wait()


def near_part(sources, plan, ext_shape, near_blocks, far_right, neighbours, prior, time):
    steps, spans, parts = plan
    count = len(parts)
    gu, gv, slots, size, _ = near_blocks.shape
    rhs = sources[0].shape[-1]
    rank = far_right.shape[-1]
    args = [near_blocks, far_right, *sources]
    args = [in_hbm(value) if value.ndim > 3 else value for value in args]
    aliases = {}
    if prior is not None:
        args.append(prior)
        aliases = {len(args): 0}
    held = pl.BlockSpec(memory_space=pltpu.HBM)
    return pl.pallas_call(
        functools.partial(near_kernel, plan, len(sources)),
        grid_spec=pltpu.PrefetchScalarGridSpec(
            num_scalar_prefetch=1,
            grid=(steps,),
            in_specs=[held, held]
            + [held if source.ndim == 4 else pl.BlockSpec(memory_space=pl.ANY) for source in sources]
            + [held] * len(aliases),
            out_specs=[held, pl.BlockSpec((rank, rhs), lambda i, nb: (0, 0))],
            scratch_shapes=[
                pltpu.VMEM((*ext_shape, size, rhs), jnp.bfloat16),
                pltpu.VMEM((steps, count, slots, size, size), jnp.bfloat16),
                pltpu.VMEM((steps, count, size, rank), jnp.bfloat16),
                pltpu.VMEM((2, count, size, rhs), jnp.bfloat16),
                pltpu.SemaphoreType.DMA((len(spans) + 2 * steps * count,)),
                pltpu.SemaphoreType.DMA((2, count)),
            ],
        ),
        out_shape=[
            jax.ShapeDtypeStruct((gu, gv, size, rhs), jnp.bfloat16),
            jax.ShapeDtypeStruct((rank, rhs), jnp.float32),
        ],
        input_output_aliases=aliases,
        cost_estimate=cost(time),
        compiler_params=pltpu.CompilerParams(
            dimension_semantics=("arbitrary",), vmem_limit_bytes=near_vmem
        ),
    )(neighbours, *args)


def odd(axis):
    return lax.rem(lax.axis_index(axis), 2)


def row_span(row, ext_row):
    return lambda srcs, ext: (srcs[0].at[row], ext.at[ext_row])


def near_middle(density, near_blocks, far_right, neighbours, prior):
    gu, gv = density.shape[:2]
    spans = [(max(row - 2, 0), row_span(row, row)) for row in range(gu)]
    parts = [(1, 1, lambda col=col: col, 1, 1, col) for col in range(1, gv - 1)]
    plan = (gu - 2, spans, parts)
    return near_part((density,), plan, (gu, gv), near_blocks, far_right, neighbours, prior, 1.5)


def near_rows(density, pu_near, pu_far, near_blocks, far_right, neighbours, prior):
    gu, gv = density.shape[:2]
    spans = [(at, row_span(row, ext_row)) for at, row, ext_row in ((0, 0, 1), (0, 1, 2), (1, gu - 2, 3), (1, gu - 1, 4))]
    spans.append((0, lambda srcs, ext: (srcs[1], ext.at[5 * (1 - odd("pu"))])))
    spans.append((0, lambda srcs, ext: (srcs[2], ext.at[5 * odd("pu")])))
    parts = [(0, gu - 1, lambda col=col: col, 1, 3, col) for col in range(1, gv - 1)]
    plan = (2, spans, parts)
    return near_part((density, pu_near, pu_far), plan, (6, gv), near_blocks, far_right, neighbours, prior, 1.5)


def near_columns(density, pu_near, pu_far, corner_near, corner_far, across, ends, mids, near_blocks, far_right, neighbours, prior):
    gu, gv = density.shape[:2]
    per_step = 2
    spans = []
    parts = []

    def near_row():
        return (gu + 1) * (1 - odd("pu"))

    def far_row():
        return (gu + 1) * odd("pu")

    for far in (0, 1):

        def left_side(far=far):
            return 1 - odd("pv") if far else odd("pv")

        def inner(source, at, ext_row, far=far, left_side=left_side):
            def views(srcs, ext):
                view = srcs[source]
                if at is not None:
                    view = view.at[at]
                from_cols = pl.ds((gv - 2) * (1 - left_side()), 2)
                return view.at[from_cols], ext.at[ext_row(), pl.ds(3 * far + left_side(), 2)]

            return views

        def outer(source, at, ext_row, far=far, left_side=left_side):
            return lambda srcs, ext: (srcs[source].at[at], ext.at[ext_row(), 3 * far + 2 * (1 - left_side())])

        for row in range(gu):
            at = max((row - 1) // per_step, 0)
            here = lambda row=row: row + 1
            spans.append((at, inner(0, row, here)))
            if far:
                spans.append((at, outer(5, row, here)))
            elif row in (0, gu - 1):
                spans.append((at, outer(6, min(row, 1), here)))
            else:
                spans.append((at, outer(7, row - 1, here)))
        spans.append((0, inner(1, None, near_row)))
        spans.append((0, inner(2, None, far_row)))
        spans.append((0, outer(3, 1 - far, near_row)))
        spans.append((0, outer(4, 1 - far, far_row)))
        col = lambda left_side=left_side: (gv - 1) * (1 - left_side())
        parts += [(row, per_step, col, row + 1, per_step, 3 * far + 1) for row in range(per_step)]
    plan = (gu // per_step, spans, parts)
    sources = (density, pu_near, pu_far, corner_near, corner_far, across, ends, mids)
    return near_part(sources, plan, (gu + 2, 6), near_blocks, far_right, neighbours, prior, 1.5)


def corners_kernel(across, ends, to_near, to_far):
    low = odd("pu")
    rows = across.shape[0]
    for target, last in ((to_near, 1 - low), (to_far, low)):
        target[0] = across[(rows - 1) * last]
        target[1] = ends[last]


def patch_corners(across, ends):
    whole = pl.BlockSpec(memory_space=pltpu.VMEM)
    return pl.pallas_call(
        corners_kernel,
        in_specs=[whole, whole],
        out_specs=[whole, whole],
        out_shape=[jax.ShapeDtypeStruct(ends.shape, ends.dtype)] * 2,
        cost_estimate=cost(0.7),
        compiler_params=pltpu.CompilerParams(vmem_limit_bytes=merge_vmem),
    )(across, ends)


def reciprocal(value):
    guess = pl.reciprocal(value, approx=True)
    return guess * (2.0 - value * guess)


def eliminate(w_k, w_e):
    size = w_k.shape[0]
    step = 32
    tile = 8
    sub = lax.broadcasted_iota(jnp.int32, (tile, size), 0)

    def spread(value, row):
        return jnp.broadcast_to(value[row : row + 1, :], (tile, size))

    for base in range(0, size, step):
        count = step // tile
        k_rows = [w_k[base + tile * r : base + tile * (r + 1), :] for r in range(count)]
        e_rows = [w_e[base + tile * r : base + tile * (r + 1), :] for r in range(count)]
        for q in range(count):
            at = base + tile * q
            cols = {
                (r, k): jnp.broadcast_to(k_rows[r][:, at + k : at + k + 1], (tile, size))
                for r in range(q, count)
                for k in range(tile)
            }
            k_done = k_rows[q]
            e_done = e_rows[q]
            for k in range(0, tile, 2):
                a = spread(cols[q, k], k)
                b = spread(cols[q, k], k + 1)
                c = spread(cols[q, k + 1], k + 1)
                det = a * c - b * b
                inverse = reciprocal(det)

                def solved(one, two):
                    return (c * one - b * two) * inverse, (a * two - b * one) * inverse

                k_one, k_two = spread(k_rows[q], k), spread(k_rows[q], k + 1)
                e_one, e_two = spread(e_rows[q], k), spread(e_rows[q], k + 1)
                k_solved = solved(k_one, k_two)
                e_solved = solved(e_one, e_two)
                links = {
                    m: solved(spread(cols[q, k], m), spread(cols[q, k + 1], m)) for m in range(k + 2, tile)
                }
                root = lax.rsqrt(a)
                second = lax.rsqrt(det) * a * root
                slope = b * root * root
                k_done = jnp.where(sub == k, k_one * root, k_done)
                e_done = jnp.where(sub == k, e_one * root, e_done)
                k_done = jnp.where(sub == k + 1, (k_two - slope * k_one) * second, k_done)
                e_done = jnp.where(sub == k + 1, (e_two - slope * e_one) * second, e_done)
                for r in range(q, count):
                    one, two = cols[r, k], cols[r, k + 1]
                    if r == q:
                        if k + 2 == tile:
                            continue
                        one = jnp.where(sub > k + 1, one, 0.0)
                        two = jnp.where(sub > k + 1, two, 0.0)
                    for m in range(k + 2, tile):
                        cols[r, m] = cols[r, m] - (one * links[m][0] + two * links[m][1])
                    k_rows[r] = k_rows[r] - (one * k_solved[0] + two * k_solved[1])
                    e_rows[r] = e_rows[r] - (one * e_solved[0] + two * e_solved[1])
            k_rows[q] = k_done
            e_rows[q] = e_done
        e_now = jnp.concatenate(e_rows, axis=0)
        w_e[base : base + step, :] = e_now
        if base + step < size:
            k_now = jnp.concatenate(k_rows, axis=0)
            k_hi = k_now.astype(jnp.bfloat16)
            k_lo = (k_now - k_hi.astype(jnp.float32)).astype(jnp.bfloat16)
            e_hi = e_now.astype(jnp.bfloat16)
            e_lo = (e_now - e_hi.astype(jnp.float32)).astype(jnp.bfloat16)
            lhs = jnp.concatenate([k_hi, k_hi, k_lo], axis=0)
            k_rhs = jnp.concatenate([k_hi, k_lo, k_hi], axis=0)
            e_rhs = jnp.concatenate([e_hi, e_lo, e_hi], axis=0)
            k_fall = dot_t(lhs, k_rhs, ((0,), (0,)))
            e_fall = dot_t(lhs, e_rhs, ((0,), (0,)))
            w_k[base + step :, :] -= k_fall[base + step :, :]
            w_e[base + step :, :] -= e_fall[base + step :, :]


tail_lanes = 128


def encode(value, key, out_ref):
    cols = value.shape[1]
    top = jnp.max(jnp.abs(value), axis=1, keepdims=True)
    power = jnp.clip(jnp.floor(jnp.log2(32000.0 / jnp.maximum(top, 1e-30))), -60.0, 60.0)
    scaled = jnp.floor(value * jnp.exp2(power) + 0.5)
    out_ref[:, :cols] = scaled.astype(jnp.int32).astype(jnp.int16)
    lanes = lax.broadcasted_iota(jnp.int32, (value.shape[0], tail_lanes), 1)
    out_ref[:, cols:] = jnp.where(lanes < tail_lanes // 2, power, key).astype(jnp.int32).astype(jnp.int16)


def decode(ref):
    cols = ref.shape[1] - tail_lanes
    tail = ref[:, cols:].astype(jnp.int32).astype(jnp.float32)
    value = ref[:, :cols].astype(jnp.int32).astype(jnp.float32) * jnp.exp2(-tail[:, :1])
    return value, tail[:, tail_lanes - 1 :]


def first_kernel(counts, order_hbm, value_hbm, sketch_hbm, density, code_ref, sketch_ref, *refs):
    across, ends, mids, pu_near, pu_far, order, value, sketch, sems = refs
    gu, gv = density.shape[:2]
    near_col = (gv - 1) * (1 - odd("pv"))
    far_col = (gv - 1) * odd("pv")
    pairs = [(value_hbm.at[0, 0], value), (order_hbm, order), (sketch_hbm, sketch)]
    inputs = len(pairs)
    pairs += [(density.at[row, far_col], across.at[row]) for row in range(gu)]
    pairs.append((density.at[(gu - 1) * (1 - odd("pu"))], pu_near))
    pairs.append((density.at[(gu - 1) * odd("pu")], pu_far))
    pairs += [(density.at[(gu - 1) * row, near_col], ends.at[row]) for row in range(2)]
    pairs += [(density.at[row + 1, near_col], mids.at[row]) for row in range(gu - 2)]
    copies = [
        pltpu.make_async_copy(source, target, sems.at[index])
        for index, (source, target) in enumerate(pairs)
    ]
    for copy in copies:
        copy.start()
    for copy in copies[:inputs]:
        copy.wait()
    key = order[lax.axis_index("pu") * counts[1] + lax.axis_index("pv")]
    encode(jnp.transpose(value[...]), key.astype(jnp.float32), code_ref)
    sketch_ref[...] = jnp.transpose(sketch[...])
    for copy in copies[inputs:]:
        copy.wait()


def first_step(value, sketch, density, order, counts):
    rows, cols = value.shape[2:]
    gu, gv, size, rhs = density.shape
    blocks = (gu, 2, gu - 2, gv, gv)
    whole = pl.BlockSpec(memory_space=pltpu.VMEM)
    held = pl.BlockSpec(memory_space=pltpu.HBM)
    args = [in_hbm(array) for array in (order, value, sketch, density)]
    return pl.pallas_call(
        functools.partial(first_kernel, counts),
        in_specs=[held] * len(args),
        out_specs=[whole] * (2 + len(blocks)),
        out_shape=[
            jax.ShapeDtypeStruct((cols, rows + tail_lanes), jnp.int16),
            jax.ShapeDtypeStruct(sketch.shape[::-1], jnp.float32),
        ]
        + [jax.ShapeDtypeStruct((count, size, rhs), density.dtype) for count in blocks],
        scratch_shapes=[
            pltpu.SMEM(order.shape, jnp.int32),
            pltpu.VMEM((rows, cols), jnp.float32),
            pltpu.VMEM(sketch.shape, jnp.float32),
            pltpu.SemaphoreType.DMA((2 * gu + 5,)),
        ],
        cost_estimate=cost(3),
        compiler_params=pltpu.CompilerParams(vmem_limit_bytes=merge_vmem),
    )(*args)


natural = ((1,), (0,))


def merge_kernel(has_path, last, mine_ref, other_ref, sketch_ref, *refs):
    if has_path:
        path_ref, *refs = refs
    left_ref, new_path_ref, w_k, w_e, z_ref = refs
    rank = mine_ref.shape[0]
    mine, my_key = decode(mine_ref)
    other, other_key = decode(other_ref)
    lead = my_key < other_key
    z_ref[:rank, :] = jnp.where(lead, mine, other)
    z_ref[rank:, :] = jnp.where(lead, other, mine)
    stacked = z_ref[...]
    sketch = sketch_ref[...]
    gram = split_dot(stacked, stacked, ((1,), (1,)))
    reduced = split_dot(sketch, gram, natural)
    w_k[...] = split_dot(reduced, sketch, ((1,), (1,)))
    rows = lax.broadcasted_iota(jnp.int32, (rank, rank), 0)
    cols = lax.broadcasted_iota(jnp.int32, (rank, rank), 1)
    w_e[...] = jnp.where(rows == cols, 1.0, 0.0)
    own = jnp.where(lead, reduced[:, :rank], reduced[:, rank:])
    if has_path:
        own = split_dot(own, path_ref[...], natural)
    eliminate(w_k, w_e)
    inverse = w_e[...]
    mixed = split_dot(inverse, sketch, natural)
    if last:
        count = left_ref.shape[1]
        part = z_ref[:, pl.ds(pl.multiple_of(lax.axis_index("pu") * count, 128), count)]
        left_ref[...] = split_dot(mixed, part, natural)
    else:
        encode(split_dot(mixed, z_ref[...], natural), jnp.minimum(my_key, other_key), left_ref)
    new_path_ref[...] = split_dot(inverse, own, natural)


def merge(level, mine, other, sketch, path, last_rows):
    rank, cols = mine.shape
    whole = pl.BlockSpec(memory_space=pltpu.VMEM)
    paths = () if path is None else (path,)
    if last_rows:
        left = jax.ShapeDtypeStruct((rank, last_rows), jnp.float32)
    else:
        left = jax.ShapeDtypeStruct(mine.shape, jnp.int16)
    return pl.pallas_call(
        functools.partial(merge_kernel, bool(paths), bool(last_rows)),
        in_specs=[whole, whole, whole] + [whole] * len(paths),
        out_specs=[whole, whole],
        out_shape=[left, jax.ShapeDtypeStruct((rank, rank), jnp.float32)],
        scratch_shapes=[
            pltpu.VMEM((rank, rank), jnp.float32),
            pltpu.VMEM((rank, rank), jnp.float32),
            pltpu.VMEM((2 * rank, cols - tail_lanes), jnp.float32),
        ],
        cost_estimate=cost((9, 1.5)[level] if level < 2 else 2),
        compiler_params=pltpu.CompilerParams(vmem_limit_bytes=merge_vmem),
    )(mine, other, sketch, *paths)


def from_partner(value, axis, distance):
    mask = 2**distance
    pairs = [(source, source ^ mask) for source in range(lax.axis_size(axis))]
    return lax.ppermute(value, axis, pairs)


def swapped(value, axis, far):
    count = lax.axis_size(axis)
    pairs = []
    for low in range(int(far), count - 1, 2):
        pairs += [(low, low + 1), (low + 1, low)]
    return lax.ppermute(value, axis, pairs)


def tied(*values):
    return lax.optimization_barrier(values)


def per_device(density, near_blocks, neighbours, far_right, far_left, sketch, patch_order):
    pu_count = lax.axis_size("pu")
    pv_count = lax.axis_size("pv")
    pv_index = lax.axis_index("pv")
    rhs = density.shape[3]
    pv_levels = pv_count.bit_length() - 1
    pu_levels = pu_count.bit_length() - 1
    levels = pv_levels + pu_levels

    def partner(value, level):
        if level < pv_levels:
            return from_partner(value, "pv", level)
        return from_partner(value, "pu", level - pv_levels)

    def scattered(share, level):
        bit = (pv_index >> level) & 1
        pairs = share.reshape(share.shape[0] // 2, 2, *share.shape[1:])
        keep = lax.dynamic_index_in_dim(pairs, bit, 1, keepdims=False)
        give = lax.dynamic_index_in_dim(pairs, 1 - bit, 1, keepdims=False)
        return keep + from_partner(give, "pv", level)

    rows = far_left.shape[2]
    left, sketch, across, ends, mids, pu_near, pu_far = first_step(
        far_left, sketch, density, patch_order, (pu_count, pv_count)
    )
    other = partner(left, 0)
    across = swapped(across, "pv", True)
    pu_near = swapped(pu_near, "pu", False)
    pu_far = swapped(pu_far, "pu", True)

    coefs = []
    corrected = share = None
    pv_path = pu_path = None
    for level in range(levels):
        coef = None
        if level:
            other = partner(left, level)
        if level in (1, 2, pv_levels):
            links, left = tied(neighbours, left)
        if level == 1:
            corrected, coef = near_rows(density, pu_near, pu_far, near_blocks, far_right, links, corrected)
            ends, mids, coef = tied(ends, mids, coef)
            ends = swapped(ends, "pv", False)
            mids = swapped(mids, "pv", False)
        elif level == 2:
            corrected, coef = near_middle(density, near_blocks, far_right, links, corrected)
        elif level == pv_levels:
            across, ends, coefs[-1] = tied(across, ends, coefs[-1])
            corner_near, corner_far = patch_corners(across, ends)
            corner_near = swapped(corner_near, "pu", False)
            corner_far = swapped(corner_far, "pu", True)
            corrected, coef = near_columns(
                density,
                pu_near,
                pu_far,
                corner_near,
                corner_far,
                across,
                ends,
                mids,
                near_blocks,
                far_right,
                links,
                corrected,
            )
        if coef is not None:
            other, coef = tied(other, coef)
            coefs.append(coef)
        if level == pv_levels:
            coef = functools.reduce(lambda a, b: a + b, coefs)
            share = lax.dot_general(coef, pv_path, (((0,), (1,)), ((), ())), precision=high)
            share = share.reshape(pv_count, rhs // pv_count, -1)
        if pv_levels <= level < 2 * pv_levels:
            share, other = tied(share, other)
            share = scattered(share, level - pv_levels)
        path = pv_path if level < pv_levels else pu_path
        last_rows = rows // pu_count if level == levels - 1 else 0
        left, path = merge(level, left, other, sketch, path, last_rows)
        if level < pv_levels:
            pv_path = path
        else:
            pu_path = path

    share, left = tied(share, left)
    for level in range(pu_levels, pv_levels):
        share = scattered(share, level)
    root_coef = lax.dot_general(share[0], pu_path, (((1,), (1,)), ((), ())), precision=high)
    for level in range(pu_levels):
        root_coef = root_coef + from_partner(root_coef, "pu", level)
    far_field = lax.dot_general(left, root_coef, (((0,), (1,)), ((), ())), precision=high)
    return (corrected, far_field)


def solution(mesh):
    in_specs = (
        P("pu", "pv", None, None),
        P("pu", "pv", None, None, None),
        P("pu", "pv", None),
        P("pu", "pv", None, None),
        P("pu", "pv", None, None),
        P(),
        P(),
    )
    out_specs = (P("pu", "pv", None, None), P("pu", "pv"))
    return jax.shard_map(
        per_device, mesh=mesh, in_specs=in_specs, out_specs=out_specs, check_vma=False
    )
```

```python
import functools

import jax
import jax.numpy as jnp
from jax import lax
from jax.experimental import pallas as pl
from jax.experimental.pallas import tpu as pltpu
from jax.sharding import PartitionSpec as P

high = lax.Precision.HIGH
empty_slot = 9
near_vmem = 18 * 1024 * 1024
merge_vmem = 12 * 1024 * 1024


def dot_t(a, b, dims, precision=None):
    return lax.dot_general(
        a, b, (dims, ((), ())), precision=precision, preferred_element_type=jnp.float32
    )


def split_dot(a, b, dims):
    return dot_t(a, b, dims, high)


def in_hbm(value):
    return pltpu.with_memory_space_constraint(value, pltpu.HBM)


def cost(microseconds):
    return pl.CostEstimate(flops=int(microseconds * 1.1e9), bytes_accessed=0, transcendentals=0)


def near_kernel(plan, n_src, nb_ref, near_hbm, right_hbm, *refs):
    steps, spans, parts = plan
    srcs = refs[:n_src]
    out_ref, coef_ref, ext_ref, near_ref, right_ref, stage_ref, sems, out_sems = refs[-8:]
    step = pl.program_id(0)
    count = len(parts)

    def fetch(at_step):
        found = []
        for index, (needed, views) in enumerate(spans):
            if needed == at_step:
                source, target = views(srcs, ext_ref)
                found.append(pltpu.make_async_copy(source, target, sems.at[index]))
        for part, (row, by, col, *_) in enumerate(parts):
            at = len(spans) + 2 * (at_step * count + part)
            for offset, source, target in ((0, near_hbm, near_ref), (1, right_hbm, right_ref)):
                found.append(
                    pltpu.make_async_copy(
                        source.at[row + by * at_step, col()], target.at[at_step, part], sems.at[at + offset]
                    )
                )
        return found

    def send(place, at_step, part):
        row, by, col = parts[part][:3]
        return pltpu.make_async_copy(
            stage_ref.at[place, part], out_ref.at[row + by * at_step, col()], out_sems.at[place, part]
        )

    @pl.when(step == 0)
    def _():
        for at_step in range(steps):
            for copy in fetch(at_step):
                copy.start()

    for at_step in range(steps):

        @pl.when(step == at_step)
        def _():
            for copy in fetch(at_step):
                copy.wait()

    place = lax.rem(step, 2)

    @pl.when(step >= 2)
    def _():
        for part in range(count):
            send(place, step - 2, part).wait()

    rhs = ext_ref.shape[-1]
    tile = 256 if rhs % 256 == 0 else rhs
    for part, (row, by, col, ext_row, ext_by, middle) in enumerate(parts):
        centre = ext_row + ext_by * step
        weights = []
        places = []
        for slot in range(near_ref.shape[2]):
            link = nb_ref[row + by * step, col(), slot]
            there = jnp.minimum(link, empty_slot - 1)
            weight = near_ref[step, part, slot]
            weights.append(jnp.where(link < empty_slot, weight, jnp.zeros_like(weight)))
            places.append((centre - 1 + lax.div(there, 3), middle - 1 + lax.rem(there, 3)))
        weights = jnp.concatenate(weights, axis=1)
        for at in range(0, rhs, tile):
            values = [ext_ref[i, j, :, at : at + tile] for i, j in places]
            total = jnp.dot(weights, jnp.concatenate(values, axis=0), preferred_element_type=jnp.float32)
            own = ext_ref[centre, middle, :, at : at + tile].astype(jnp.float32)
            stage_ref[place, part, :, at : at + tile] = (own + total).astype(jnp.bfloat16)
        send(place, step, part).start()
    rights = jnp.concatenate([right_ref[step, part] for part in range(count)], axis=0)
    blocks = jnp.concatenate([stage_ref[place, part] for part in range(count)], axis=0)
    coef = dot_t(rights, blocks, ((0,), (0,)))

    @pl.when(step == 0)
    def _():
        coef_ref[...] = coef

    @pl.when(step > 0)
    def _():
        coef_ref[...] += coef

    @pl.when(step == steps - 1)
    def _():
        for at_step in range(max(steps - 2, 0), steps):
            for part in range(count):
                send(at_step % 2, at_step, part).wait()


def near_part(sources, plan, ext_shape, near_blocks, far_right, neighbours, prior, time):
    steps, spans, parts = plan
    count = len(parts)
    gu, gv, slots, size, _ = near_blocks.shape
    rhs = sources[0].shape[-1]
    rank = far_right.shape[-1]
    args = [near_blocks, far_right, *sources]
    args = [in_hbm(value) if value.ndim > 3 else value for value in args]
    aliases = {}
    if prior is not None:
        args.append(prior)
        aliases = {len(args): 0}
    held = pl.BlockSpec(memory_space=pltpu.HBM)
    return pl.pallas_call(
        functools.partial(near_kernel, plan, len(sources)),
        grid_spec=pltpu.PrefetchScalarGridSpec(
            num_scalar_prefetch=1,
            grid=(steps,),
            in_specs=[held, held]
            + [held if source.ndim == 4 else pl.BlockSpec(memory_space=pl.ANY) for source in sources]
            + [held] * len(aliases),
            out_specs=[held, pl.BlockSpec((rank, rhs), lambda i, nb: (0, 0))],
            scratch_shapes=[
                pltpu.VMEM((*ext_shape, size, rhs), jnp.bfloat16),
                pltpu.VMEM((steps, count, slots, size, size), jnp.bfloat16),
                pltpu.VMEM((steps, count, size, rank), jnp.bfloat16),
                pltpu.VMEM((2, count, size, rhs), jnp.bfloat16),
                pltpu.SemaphoreType.DMA((len(spans) + 2 * steps * count,)),
                pltpu.SemaphoreType.DMA((2, count)),
            ],
        ),
        out_shape=[
            jax.ShapeDtypeStruct((gu, gv, size, rhs), jnp.bfloat16),
            jax.ShapeDtypeStruct((rank, rhs), jnp.float32),
        ],
        input_output_aliases=aliases,
        cost_estimate=cost(time),
        compiler_params=pltpu.CompilerParams(
            dimension_semantics=("arbitrary",), vmem_limit_bytes=near_vmem
        ),
    )(neighbours, *args)


def odd(axis):
    return lax.rem(lax.axis_index(axis), 2)


def row_span(row, ext_row):
    return lambda srcs, ext: (srcs[0].at[row], ext.at[ext_row])


def near_middle(density, near_blocks, far_right, neighbours, prior):
    gu, gv = density.shape[:2]
    spans = [(max(row - 2, 0), row_span(row, row)) for row in range(gu)]
    parts = [(1, 1, lambda col=col: col, 1, 1, col) for col in range(1, gv - 1)]
    plan = (gu - 2, spans, parts)
    return near_part((density,), plan, (gu, gv), near_blocks, far_right, neighbours, prior, 0.5)


def near_rows(density, pu_near, pu_far, near_blocks, far_right, neighbours, prior):
    gu, gv = density.shape[:2]
    spans = [(at, row_span(row, ext_row)) for at, row, ext_row in ((0, 0, 1), (0, 1, 2), (1, gu - 2, 3), (1, gu - 1, 4))]
    spans.append((0, lambda srcs, ext: (srcs[1], ext.at[5 * (1 - odd("pu"))])))
    spans.append((0, lambda srcs, ext: (srcs[2], ext.at[5 * odd("pu")])))
    parts = [(0, gu - 1, lambda col=col: col, 1, 3, col) for col in range(1, gv - 1)]
    plan = (2, spans, parts)
    return near_part((density, pu_near, pu_far), plan, (6, gv), near_blocks, far_right, neighbours, prior, 0.5)


def near_columns(density, pu_near, pu_far, corner_near, corner_far, beside, ends, mids, near_blocks, far_right, neighbours, prior):
    gu, gv = density.shape[:2]
    per_step = 2
    spans = []
    parts = []

    def near_row():
        return (gu + 1) * (1 - odd("pu"))

    def far_row():
        return (gu + 1) * odd("pu")

    for far in (0, 1):

        def left_side(far=far):
            return 1 - odd("pv") if far else odd("pv")

        def inner(source, at, ext_row, far=far, left_side=left_side):
            def views(srcs, ext):
                view = srcs[source]
                if at is not None:
                    view = view.at[at]
                from_cols = pl.ds((gv - 2) * (1 - left_side()), 2)
                return view.at[from_cols], ext.at[ext_row(), pl.ds(3 * far + left_side(), 2)]

            return views

        def outer(source, at, ext_row, far=far, left_side=left_side):
            return lambda srcs, ext: (srcs[source].at[at], ext.at[ext_row(), 3 * far + 2 * (1 - left_side())])

        for row in range(gu):
            at = max((row - 1) // per_step, 0)
            here = lambda row=row: row + 1
            spans.append((at, inner(0, row, here)))
            if not far:
                spans.append((at, outer(5, row, here)))
            elif row in (0, gu - 1):
                spans.append((at, outer(6, min(row, 1), here)))
            else:
                spans.append((at, outer(7, row - 1, here)))
        spans.append((0, inner(1, None, near_row)))
        spans.append((0, inner(2, None, far_row)))
        spans.append((0, outer(3, far, near_row)))
        spans.append((0, outer(4, far, far_row)))
        col = lambda left_side=left_side: (gv - 1) * (1 - left_side())
        parts += [(row, per_step, col, row + 1, per_step, 3 * far + 1) for row in range(per_step)]
    plan = (gu // per_step, spans, parts)
    sources = (density, pu_near, pu_far, corner_near, corner_far, beside, ends, mids)
    return near_part(sources, plan, (gu + 2, 6), near_blocks, far_right, neighbours, prior, 0.5)


def corners_kernel(beside, ends, to_near, to_far):
    low = odd("pu")
    rows = beside.shape[0]
    for target, last in ((to_near, 1 - low), (to_far, low)):
        target[0] = beside[(rows - 1) * last]
        target[1] = ends[last]


def patch_corners(beside, ends):
    whole = pl.BlockSpec(memory_space=pltpu.VMEM)
    return pl.pallas_call(
        corners_kernel,
        in_specs=[whole, whole],
        out_specs=[whole, whole],
        out_shape=[jax.ShapeDtypeStruct(ends.shape, ends.dtype)] * 2,
        cost_estimate=cost(0.7),
        compiler_params=pltpu.CompilerParams(vmem_limit_bytes=merge_vmem),
    )(beside, ends)


def reciprocal(value):
    guess = pl.reciprocal(value, approx=True)
    return guess * (2.0 - value * guess)


def eliminate(w_k, w_e):
    size = w_k.shape[0]
    step = 32
    tile = 8
    sub = lax.broadcasted_iota(jnp.int32, (tile, size), 0)

    def spread(value, row):
        return jnp.broadcast_to(value[row : row + 1, :], (tile, size))

    for base in range(0, size, step):
        count = step // tile
        k_rows = [w_k[base + tile * r : base + tile * (r + 1), :] for r in range(count)]
        e_rows = [w_e[base + tile * r : base + tile * (r + 1), :] for r in range(count)]
        for q in range(count):
            at = base + tile * q
            cols = {
                (r, k): jnp.broadcast_to(k_rows[r][:, at + k : at + k + 1], (tile, size))
                for r in range(q, count)
                for k in range(tile)
            }
            k_done = k_rows[q]
            e_done = e_rows[q]
            for k in range(0, tile, 4):
                pivots = [[spread(cols[q, k + j], k + i) for j in range(i + 1)] for i in range(4)]
                (a,), (b, c), (d, e, h), (f, g, i, j) = pivots
                upper = reciprocal(a * c - b * b)

                def halved(one, two):
                    return (c * one - b * two) * upper, (a * two - b * one) * upper

                t_one, t_two = halved(d, e)
                u_one, u_two = halved(f, g)
                s_one = h - (t_one * d + t_two * e)
                s_mix = i - (t_one * f + t_two * g)
                s_two = j - (u_one * f + u_two * g)
                lower_det = s_one * s_two - s_mix * s_mix
                lower = reciprocal(lower_det)

                def reduced(rows):
                    y_one, y_two = halved(rows[0], rows[1])
                    return rows[2] - (d * y_one + e * y_two), rows[3] - (f * y_one + g * y_two), y_one, y_two

                def solved(rows):
                    q_one, q_two, y_one, y_two = reduced(rows)
                    x_three = (s_two * q_one - s_mix * q_two) * lower
                    x_four = (s_one * q_two - s_mix * q_one) * lower
                    x_one = y_one - (t_one * x_three + u_one * x_four)
                    x_two = y_two - (t_two * x_three + u_two * x_four)
                    return x_one, x_two, x_three, x_four

                def finished(rows):
                    q_one, q_two, _, _ = reduced(rows)
                    return (
                        rows[0] * root_one,
                        (rows[1] - slope_one * rows[0]) * root_two,
                        q_one * root_three,
                        (q_two - slope_three * q_one) * root_four,
                    )

                root_one = lax.rsqrt(a)
                slope_one = b * root_one * root_one
                root_two = lax.rsqrt(a * c - b * b) * a * root_one
                root_three = lax.rsqrt(s_one)
                slope_three = s_mix * root_three * root_three
                root_four = lax.rsqrt(lower_det) * s_one * root_three
                k_four = [spread(k_rows[q], k + n) for n in range(4)]
                e_four = [spread(e_rows[q], k + n) for n in range(4)]
                k_solved = solved(k_four)
                e_solved = solved(e_four)
                links = {
                    m: solved([spread(cols[q, k + n], m) for n in range(4)]) for m in range(k + 4, tile)
                }
                for n, (k_row, e_row) in enumerate(zip(finished(k_four), finished(e_four))):
                    k_done = jnp.where(sub == k + n, k_row, k_done)
                    e_done = jnp.where(sub == k + n, e_row, e_done)

                def fallen(value, factors, rows):
                    return value - ((factors[0] * rows[0] + factors[1] * rows[1]) + (factors[2] * rows[2] + factors[3] * rows[3]))

                for r in range(q, count):
                    factors = [cols[r, k + n] for n in range(4)]
                    if r == q:
                        if k + 4 == tile:
                            continue
                        factors = [jnp.where(sub > k + 3, factor, 0.0) for factor in factors]
                    for m in range(k + 4, tile):
                        cols[r, m] = fallen(cols[r, m], factors, links[m])
                    k_rows[r] = fallen(k_rows[r], factors, k_solved)
                    e_rows[r] = fallen(e_rows[r], factors, e_solved)
            k_rows[q] = k_done
            e_rows[q] = e_done
        e_now = jnp.concatenate(e_rows, axis=0)
        w_e[base : base + step, :] = e_now
        if base + step < size:
            k_now = jnp.concatenate(k_rows, axis=0)
            k_hi = k_now.astype(jnp.bfloat16)
            k_lo = (k_now - k_hi.astype(jnp.float32)).astype(jnp.bfloat16)
            e_hi = e_now.astype(jnp.bfloat16)
            e_lo = (e_now - e_hi.astype(jnp.float32)).astype(jnp.bfloat16)
            lhs = jnp.concatenate([k_hi, k_hi, k_lo], axis=0)
            k_rhs = jnp.concatenate([k_hi, k_lo, k_hi], axis=0)
            e_rhs = jnp.concatenate([e_hi, e_lo, e_hi], axis=0)
            k_fall = dot_t(lhs, k_rhs, ((0,), (0,)))
            e_fall = dot_t(lhs, e_rhs, ((0,), (0,)))
            w_k[base + step :, :] -= k_fall[base + step :, :]
            w_e[base + step :, :] -= e_fall[base + step :, :]


tail_lanes = 128


def encode(value, key, out_ref):
    cols = value.shape[1]
    top = jnp.max(jnp.abs(value), axis=1, keepdims=True)
    power = jnp.clip(jnp.floor(jnp.log2(32000.0 / jnp.maximum(top, 1e-30))), -60.0, 60.0)
    scaled = jnp.floor(value * jnp.exp2(power) + 0.5)
    out_ref[:, :cols] = scaled.astype(jnp.int32).astype(jnp.int16)
    lanes = lax.broadcasted_iota(jnp.int32, (value.shape[0], tail_lanes), 1)
    out_ref[:, cols:] = jnp.where(lanes < tail_lanes // 2, power, key).astype(jnp.int32).astype(jnp.int16)


def decode(ref):
    cols = ref.shape[1] - tail_lanes
    tail = ref[:, cols:].astype(jnp.int32).astype(jnp.float32)
    value = ref[:, :cols].astype(jnp.int32).astype(jnp.float32) * jnp.exp2(-tail[:, :1])
    return value, tail[:, tail_lanes - 1 :]


def run_copies(pairs, sems):
    copies = [
        pltpu.make_async_copy(source, target, sems.at[index])
        for index, (source, target) in enumerate(pairs)
    ]
    for copy in copies:
        copy.start()
    return copies


def leaf_kernel(counts, order_hbm, value_hbm, sketch_hbm, code_ref, sketch_ref, order, value, sketch, sems):
    pairs = [(value_hbm.at[0, 0], value), (order_hbm, order), (sketch_hbm, sketch)]
    for copy in run_copies(pairs, sems):
        copy.wait()
    key = order[lax.axis_index("pu") * counts[1] + lax.axis_index("pv")]
    encode(jnp.transpose(value[...]), key.astype(jnp.float32), code_ref)
    sketch_ref[...] = jnp.transpose(sketch[...])


def coded_leaf(value, sketch, order, counts):
    rows, cols = value.shape[2:]
    whole = pl.BlockSpec(memory_space=pltpu.VMEM)
    held = pl.BlockSpec(memory_space=pltpu.HBM)
    return pl.pallas_call(
        functools.partial(leaf_kernel, counts),
        in_specs=[held] * 3,
        out_specs=[whole] * 2,
        out_shape=[
            jax.ShapeDtypeStruct((cols, rows + tail_lanes), jnp.int16),
            jax.ShapeDtypeStruct(sketch.shape[::-1], jnp.float32),
        ],
        scratch_shapes=[
            pltpu.SMEM(order.shape, jnp.int32),
            pltpu.VMEM((rows, cols), jnp.float32),
            pltpu.VMEM(sketch.shape, jnp.float32),
            pltpu.SemaphoreType.DMA((3,)),
        ],
        cost_estimate=cost(1.5),
        compiler_params=pltpu.CompilerParams(vmem_limit_bytes=merge_vmem),
    )(in_hbm(order), in_hbm(value), in_hbm(sketch))


def edges_kernel(density, beside, across, pu_near, pu_far, sems):
    gu, gv = density.shape[:2]
    near_col = (gv - 1) * (1 - odd("pv"))
    far_col = (gv - 1) * odd("pv")
    pairs = [(density.at[row, near_col], beside.at[row]) for row in range(gu)]
    pairs += [(density.at[row, far_col], across.at[at]) for at, row in enumerate([0, gu - 1, *range(1, gu - 1)])]
    pairs.append((density.at[(gu - 1) * (1 - odd("pu"))], pu_near))
    pairs.append((density.at[(gu - 1) * odd("pu")], pu_far))
    for copy in run_copies(pairs, sems):
        copy.wait()


def patch_edges(density):
    gu, gv, size, rhs = density.shape
    blocks = (gu, gu, gv, gv)
    return pl.pallas_call(
        edges_kernel,
        in_specs=[pl.BlockSpec(memory_space=pltpu.HBM)],
        out_specs=[pl.BlockSpec(memory_space=pltpu.VMEM)] * len(blocks),
        out_shape=[jax.ShapeDtypeStruct((count, size, rhs), density.dtype) for count in blocks],
        scratch_shapes=[pltpu.SemaphoreType.DMA((2 * gu + 2,))],
        cost_estimate=cost(2.5),
        compiler_params=pltpu.CompilerParams(vmem_limit_bytes=merge_vmem),
    )(in_hbm(density))


natural = ((1,), (0,))


def merge_kernel(has_path, last, mine_ref, other_ref, sketch_ref, *refs):
    if has_path:
        path_ref, *refs = refs
    left_ref, new_path_ref, w_k, w_e, z_ref = refs
    rank = mine_ref.shape[0]
    mine, my_key = decode(mine_ref)
    other, other_key = decode(other_ref)
    lead = my_key < other_key
    z_ref[:rank, :] = jnp.where(lead, mine, other)
    z_ref[rank:, :] = jnp.where(lead, other, mine)
    stacked = z_ref[...]
    sketch = sketch_ref[...]
    gram = split_dot(stacked, stacked, ((1,), (1,)))
    reduced = split_dot(sketch, gram, natural)
    w_k[...] = split_dot(reduced, sketch, ((1,), (1,)))
    rows = lax.broadcasted_iota(jnp.int32, (rank, rank), 0)
    cols = lax.broadcasted_iota(jnp.int32, (rank, rank), 1)
    w_e[...] = jnp.where(rows == cols, 1.0, 0.0)
    own = jnp.where(lead, reduced[:, :rank], reduced[:, rank:])
    if has_path:
        own = split_dot(own, path_ref[...], natural)
    eliminate(w_k, w_e)
    inverse = w_e[...]
    mixed = split_dot(inverse, sketch, natural)
    if last:
        count = left_ref.shape[1]
        part = z_ref[:, pl.ds(pl.multiple_of(lax.axis_index("pu") * count, 128), count)]
        left_ref[...] = split_dot(mixed, part, natural)
    else:
        encode(split_dot(mixed, z_ref[...], natural), jnp.minimum(my_key, other_key), left_ref)
    new_path_ref[...] = split_dot(inverse, own, natural)


def merge(level, mine, other, sketch, path, last_rows):
    rank, cols = mine.shape
    whole = pl.BlockSpec(memory_space=pltpu.VMEM)
    paths = () if path is None else (path,)
    if last_rows:
        left = jax.ShapeDtypeStruct((rank, last_rows), jnp.float32)
    else:
        left = jax.ShapeDtypeStruct(mine.shape, jnp.int16)
    return pl.pallas_call(
        functools.partial(merge_kernel, bool(paths), bool(last_rows)),
        in_specs=[whole, whole, whole] + [whole] * len(paths),
        out_specs=[whole, whole],
        out_shape=[left, jax.ShapeDtypeStruct((rank, rank), jnp.float32)],
        scratch_shapes=[
            pltpu.VMEM((rank, rank), jnp.float32),
            pltpu.VMEM((rank, rank), jnp.float32),
            pltpu.VMEM((2 * rank, cols - tail_lanes), jnp.float32),
        ],
        cost_estimate=cost((9, 1.5)[level] if level < 2 else 0.5),
        compiler_params=pltpu.CompilerParams(vmem_limit_bytes=merge_vmem),
    )(mine, other, sketch, *paths)


def from_partner(value, axis, distance):
    mask = 2**distance
    pairs = [(source, source ^ mask) for source in range(lax.axis_size(axis))]
    return lax.ppermute(value, axis, pairs)


def swapped(value, axis, far):
    count = lax.axis_size(axis)
    pairs = []
    for low in range(int(far), count - 1, 2):
        pairs += [(low, low + 1), (low + 1, low)]
    return lax.ppermute(value, axis, pairs)


def relayed(value, axis):
    count = lax.axis_size(axis)
    pairs = [(at, at + 2) for at in range(1, count - 2, 2)] + [(at, at - 2) for at in range(2, count, 2)]
    return lax.ppermute(value, axis, pairs)


def tied(*values):
    return lax.optimization_barrier(values)


def per_device(density, near_blocks, neighbours, far_right, far_left, sketch, patch_order):
    pu_count = lax.axis_size("pu")
    pv_count = lax.axis_size("pv")
    pv_index = lax.axis_index("pv")
    rhs = density.shape[3]
    pv_levels = pv_count.bit_length() - 1
    pu_levels = pu_count.bit_length() - 1
    levels = pv_levels + pu_levels

    def partner(value, level):
        if level < pv_levels:
            return from_partner(value, "pv", level)
        return from_partner(value, "pu", level - pv_levels)

    def scattered(share, level):
        bit = (pv_index >> level) & 1
        pairs = share.reshape(share.shape[0] // 2, 2, *share.shape[1:])
        keep = lax.dynamic_index_in_dim(pairs, bit, 1, keepdims=False)
        give = lax.dynamic_index_in_dim(pairs, 1 - bit, 1, keepdims=False)
        return keep + from_partner(give, "pv", level)

    rows = far_left.shape[2]
    left, sketch = coded_leaf(far_left, sketch, patch_order, (pu_count, pv_count))
    other = partner(left, 0)
    density, left = tied(density, left)
    beside, across, pu_near, pu_far = patch_edges(density)
    beside = swapped(beside, "pv", False)
    across = relayed(across, "pv")
    pu_near = swapped(pu_near, "pu", False)
    pu_far = swapped(pu_far, "pu", True)

    coefs = []
    corrected = share = None
    pv_path = pu_path = None
    for level in range(levels):
        last = level == levels - 1
        coef = None
        if level:
            other = partner(left, level)
        if level in (1, 2) or last:
            links, left = tied(neighbours, left)
        if level == 1:
            corrected, coef = near_middle(density, near_blocks, far_right, links, corrected)
        elif level == 2:
            across, left = tied(across, left)
            ends = swapped(across[:2], "pv", False)
            mids = swapped(across[2:], "pv", False)
            corrected, coef = near_rows(density, pu_near, pu_far, near_blocks, far_right, links, corrected)
        elif last:
            corner_near, corner_far = patch_corners(beside, ends)
            corner_near = swapped(corner_near, "pu", False)
            corner_far = swapped(corner_far, "pu", True)
            corrected, coef = near_columns(
                density,
                pu_near,
                pu_far,
                corner_near,
                corner_far,
                beside,
                ends,
                mids,
                near_blocks,
                far_right,
                links,
                corrected,
            )
        if coef is not None:
            other, coef = tied(other, coef)
            coefs.append(coef)
        if last:
            coef = functools.reduce(lambda a, b: a + b, coefs)
            share = lax.dot_general(coef, pv_path, (((0,), (1,)), ((), ())), precision=high)
            share = share.reshape(pv_count, rhs // pv_count, -1)
            share, other = tied(share, other)
            share = scattered(share, 0)
        path = pv_path if level < pv_levels else pu_path
        last_rows = rows // pu_count if last else 0
        left, path = merge(level, left, other, sketch, path, last_rows)
        if level < pv_levels:
            pv_path = path
        else:
            pu_path = path

    share, left = tied(share, left)
    for level in range(1, pv_levels):
        share = scattered(share, level)
    root_coef = lax.dot_general(share[0], pu_path, (((1,), (1,)), ((), ())), precision=high)
    for level in range(pu_levels):
        root_coef = root_coef + from_partner(root_coef, "pu", level)
    far_field = lax.dot_general(left, root_coef, (((0,), (1,)), ((), ())), precision=high)
    return (corrected, far_field)


def solution(mesh):
    in_specs = (
        P("pu", "pv", None, None),
        P("pu", "pv", None, None, None),
        P("pu", "pv", None),
        P("pu", "pv", None, None),
        P("pu", "pv", None, None),
        P(),
        P(),
    )
    out_specs = (P("pu", "pv", None, None), P("pu", "pv"))
    return jax.shard_map(
        per_device, mesh=mesh, in_specs=in_specs, out_specs=out_specs, check_vma=False
    )
```

```python
import functools

import jax
import jax.numpy as jnp
from jax import lax
from jax.experimental import pallas as pl
from jax.experimental.pallas import tpu as pltpu
from jax.sharding import PartitionSpec as P

high = lax.Precision.HIGH
empty_slot = 9
near_vmem = 18 * 1024 * 1024
merge_vmem = 12 * 1024 * 1024


def dot_t(a, b, dims, precision=None):
    return lax.dot_general(
        a, b, (dims, ((), ())), precision=precision, preferred_element_type=jnp.float32
    )


def split_dot(a, b, dims):
    return dot_t(a, b, dims, high)


def in_hbm(value):
    return pltpu.with_memory_space_constraint(value, pltpu.HBM)


def cost(microseconds):
    return pl.CostEstimate(flops=int(microseconds * 1.1e9), bytes_accessed=0, transcendentals=0)


def near_kernel(plan, n_src, nb_hbm, near_hbm, right_hbm, *refs):
    steps, spans, parts = plan
    srcs = refs[:n_src]
    out_ref, coef_ref, nb_ref, ext_ref, near_ref, right_ref, stage_ref, sems, out_sems, nb_sem = refs[-10:]
    step = pl.program_id(0)
    count = len(parts)
    links = pltpu.make_async_copy(nb_hbm, nb_ref, nb_sem)

    def fetch(at_step):
        found = []
        for index, (needed, views) in enumerate(spans):
            if needed == at_step:
                source, target = views(srcs, ext_ref)
                found.append(pltpu.make_async_copy(source, target, sems.at[index]))
        for part, (row, by, col, *_) in enumerate(parts):
            at = len(spans) + 2 * (at_step * count + part)
            for offset, source, target in ((0, near_hbm, near_ref), (1, right_hbm, right_ref)):
                found.append(
                    pltpu.make_async_copy(
                        source.at[row + by * at_step, col()], target.at[at_step, part], sems.at[at + offset]
                    )
                )
        return found

    def send(place, at_step, part):
        row, by, col = parts[part][:3]
        return pltpu.make_async_copy(
            stage_ref.at[place, part], out_ref.at[row + by * at_step, col()], out_sems.at[place, part]
        )

    @pl.when(step == 0)
    def _():
        links.start()
        for at_step in range(steps):
            for copy in fetch(at_step):
                copy.start()
        links.wait()

    for at_step in range(steps):

        @pl.when(step == at_step)
        def _():
            for copy in fetch(at_step):
                copy.wait()

    place = lax.rem(step, 2)

    @pl.when(step >= 2)
    def _():
        for part in range(count):
            send(place, step - 2, part).wait()

    rhs = ext_ref.shape[-1]
    tile = 256 if rhs % 256 == 0 else rhs
    for part, (row, by, col, ext_row, ext_by, middle) in enumerate(parts):
        centre = ext_row + ext_by * step
        weights = []
        places = []
        for slot in range(near_ref.shape[2]):
            link = nb_ref[row + by * step, col(), slot]
            there = jnp.minimum(link, empty_slot - 1)
            weight = near_ref[step, part, slot]
            weights.append(jnp.where(link < empty_slot, weight, jnp.zeros_like(weight)))
            places.append((centre - 1 + lax.div(there, 3), middle - 1 + lax.rem(there, 3)))
        weights = jnp.concatenate(weights, axis=1)
        for at in range(0, rhs, tile):
            values = [ext_ref[i, j, :, at : at + tile] for i, j in places]
            total = jnp.dot(weights, jnp.concatenate(values, axis=0), preferred_element_type=jnp.float32)
            own = ext_ref[centre, middle, :, at : at + tile].astype(jnp.float32)
            stage_ref[place, part, :, at : at + tile] = (own + total).astype(jnp.bfloat16)
        send(place, step, part).start()
    rights = jnp.concatenate([right_ref[step, part] for part in range(count)], axis=0)
    blocks = jnp.concatenate([stage_ref[place, part] for part in range(count)], axis=0)
    coef = dot_t(rights, blocks, ((0,), (0,)))

    @pl.when(step == 0)
    def _():
        coef_ref[...] = coef

    @pl.when(step > 0)
    def _():
        coef_ref[...] += coef

    @pl.when(step == steps - 1)
    def _():
        for at_step in range(max(steps - 2, 0), steps):
            for part in range(count):
                send(at_step % 2, at_step, part).wait()


def near_part(sources, plan, ext_shape, near_blocks, far_right, neighbours, prior, time):
    steps, spans, parts = plan
    count = len(parts)
    gu, gv, slots, size, _ = near_blocks.shape
    rhs = sources[0].shape[-1]
    rank = far_right.shape[-1]
    args = [neighbours, near_blocks, far_right, *sources]
    args = [in_hbm(value) if at < 3 or value.ndim > 3 else value for at, value in enumerate(args)]
    aliases = {}
    if prior is not None:
        aliases = {len(args): 0}
        args.append(prior)
    held = pl.BlockSpec(memory_space=pltpu.HBM)
    return pl.pallas_call(
        functools.partial(near_kernel, plan, len(sources)),
        grid=(steps,),
        in_specs=[held] * 3
        + [held if source.ndim == 4 else pl.BlockSpec(memory_space=pl.ANY) for source in sources]
        + [held] * len(aliases),
        out_specs=[held, pl.BlockSpec((rank, rhs), lambda i: (0, 0))],
        scratch_shapes=[
            pltpu.SMEM(neighbours.shape, jnp.int32),
            pltpu.VMEM((*ext_shape, size, rhs), jnp.bfloat16),
            pltpu.VMEM((steps, count, slots, size, size), jnp.bfloat16),
            pltpu.VMEM((steps, count, size, rank), jnp.bfloat16),
            pltpu.VMEM((2, count, size, rhs), jnp.bfloat16),
            pltpu.SemaphoreType.DMA((len(spans) + 2 * steps * count,)),
            pltpu.SemaphoreType.DMA((2, count)),
            pltpu.SemaphoreType.DMA,
        ],
        out_shape=[
            jax.ShapeDtypeStruct((gu, gv, size, rhs), jnp.bfloat16),
            jax.ShapeDtypeStruct((rank, rhs), jnp.float32),
        ],
        input_output_aliases=aliases,
        cost_estimate=cost(time),
        compiler_params=pltpu.CompilerParams(
            dimension_semantics=("arbitrary",), vmem_limit_bytes=near_vmem
        ),
    )(*args)


def odd(axis):
    return lax.rem(lax.axis_index(axis), 2)


def row_span(row, ext_row):
    return lambda srcs, ext: (srcs[0].at[row], ext.at[ext_row])


def near_middle(density, near_blocks, far_right, neighbours, prior):
    gu, gv = density.shape[:2]
    spans = [(max(row - 2, 0), row_span(row, row)) for row in range(gu)]
    parts = [(1, 1, lambda col=col: col, 1, 1, col) for col in range(1, gv - 1)]
    plan = (gu - 2, spans, parts)
    return near_part((density,), plan, (gu, gv), near_blocks, far_right, neighbours, prior, 0.5)


def near_rows(density, pu_near, pu_far, near_blocks, far_right, neighbours, prior):
    gu, gv = density.shape[:2]
    spans = [(at, row_span(row, ext_row)) for at, row, ext_row in ((0, 0, 1), (0, 1, 2), (1, gu - 2, 3), (1, gu - 1, 4))]
    spans.append((0, lambda srcs, ext: (srcs[1], ext.at[5 * (1 - odd("pu"))])))
    spans.append((0, lambda srcs, ext: (srcs[2], ext.at[5 * odd("pu")])))
    parts = [(0, gu - 1, lambda col=col: col, 1, 3, col) for col in range(1, gv - 1)]
    plan = (2, spans, parts)
    return near_part((density, pu_near, pu_far), plan, (6, gv), near_blocks, far_right, neighbours, prior, 0.5)


def near_columns(density, pu_near, pu_far, corner_near, corner_far, beside, ends, mids, near_blocks, far_right, neighbours, prior):
    gu, gv = density.shape[:2]
    per_step = 2
    spans = []
    parts = []

    def near_row():
        return (gu + 1) * (1 - odd("pu"))

    def far_row():
        return (gu + 1) * odd("pu")

    for far in (0, 1):

        def left_side(far=far):
            return 1 - odd("pv") if far else odd("pv")

        def inner(source, at, ext_row, far=far, left_side=left_side):
            def views(srcs, ext):
                view = srcs[source]
                if at is not None:
                    view = view.at[at]
                from_cols = pl.ds((gv - 2) * (1 - left_side()), 2)
                return view.at[from_cols], ext.at[ext_row(), pl.ds(3 * far + left_side(), 2)]

            return views

        def outer(source, at, ext_row, far=far, left_side=left_side):
            return lambda srcs, ext: (srcs[source].at[at], ext.at[ext_row(), 3 * far + 2 * (1 - left_side())])

        for row in range(gu):
            at = max((row - 1) // per_step, 0)
            here = lambda row=row: row + 1
            spans.append((at, inner(0, row, here)))
            if not far:
                spans.append((at, outer(5, row, here)))
            elif row in (0, gu - 1):
                spans.append((at, outer(6, min(row, 1), here)))
            else:
                spans.append((at, outer(7, row - 1, here)))
        spans.append((0, inner(1, None, near_row)))
        spans.append((0, inner(2, None, far_row)))
        spans.append((0, outer(3, far, near_row)))
        spans.append((0, outer(4, far, far_row)))
        col = lambda left_side=left_side: (gv - 1) * (1 - left_side())
        parts += [(row, per_step, col, row + 1, per_step, 3 * far + 1) for row in range(per_step)]
    plan = (gu // per_step, spans, parts)
    sources = (density, pu_near, pu_far, corner_near, corner_far, beside, ends, mids)
    return near_part(sources, plan, (gu + 2, 6), near_blocks, far_right, neighbours, prior, 0.5)


def corners_kernel(beside, ends, to_near, to_far):
    low = odd("pu")
    rows = beside.shape[0]
    for target, last in ((to_near, 1 - low), (to_far, low)):
        target[0] = beside[(rows - 1) * last]
        target[1] = ends[last]


def patch_corners(beside, ends):
    whole = pl.BlockSpec(memory_space=pltpu.VMEM)
    return pl.pallas_call(
        corners_kernel,
        in_specs=[whole, whole],
        out_specs=[whole, whole],
        out_shape=[jax.ShapeDtypeStruct(ends.shape, ends.dtype)] * 2,
        cost_estimate=cost(0.7),
        compiler_params=pltpu.CompilerParams(vmem_limit_bytes=merge_vmem),
    )(beside, ends)


def reciprocal(value):
    guess = pl.reciprocal(value, approx=True)
    return guess * (2.0 - value * guess)


def eliminate(w_k, w_e):
    size = w_k.shape[0]
    step = 32
    tile = 8
    sub = lax.broadcasted_iota(jnp.int32, (tile, size), 0)

    def spread(value, row):
        return jnp.broadcast_to(value[row : row + 1, :], (tile, size))

    for base in range(0, size, step):
        count = step // tile
        k_rows = [w_k[base + tile * r : base + tile * (r + 1), :] for r in range(count)]
        e_rows = [w_e[base + tile * r : base + tile * (r + 1), :] for r in range(count)]
        for q in range(count):
            at = base + tile * q
            cols = {
                (r, k): jnp.broadcast_to(k_rows[r][:, at + k : at + k + 1], (tile, size))
                for r in range(q, count)
                for k in range(tile)
            }
            k_done = k_rows[q]
            e_done = e_rows[q]
            for k in range(0, tile, 2):
                a = spread(cols[q, k], k)
                b = spread(cols[q, k], k + 1)
                c = spread(cols[q, k + 1], k + 1)
                det = a * c - b * b
                inverse = reciprocal(det)

                def solved(one, two):
                    return (c * one - b * two) * inverse, (a * two - b * one) * inverse

                k_one, k_two = spread(k_rows[q], k), spread(k_rows[q], k + 1)
                e_one, e_two = spread(e_rows[q], k), spread(e_rows[q], k + 1)
                k_solved = solved(k_one, k_two)
                e_solved = solved(e_one, e_two)
                links = {
                    m: solved(spread(cols[q, k], m), spread(cols[q, k + 1], m)) for m in range(k + 2, tile)
                }
                root = lax.rsqrt(a)
                second = lax.rsqrt(det) * a * root
                slope = b * root * root
                k_done = jnp.where(sub == k, k_one * root, k_done)
                e_done = jnp.where(sub == k, e_one * root, e_done)
                k_done = jnp.where(sub == k + 1, (k_two - slope * k_one) * second, k_done)
                e_done = jnp.where(sub == k + 1, (e_two - slope * e_one) * second, e_done)
                for r in range(q, count):
                    one, two = cols[r, k], cols[r, k + 1]
                    if r == q:
                        if k + 2 == tile:
                            continue
                        one = jnp.where(sub > k + 1, one, 0.0)
                        two = jnp.where(sub > k + 1, two, 0.0)
                    for m in range(k + 2, tile):
                        cols[r, m] = cols[r, m] - (one * links[m][0] + two * links[m][1])
                    k_rows[r] = k_rows[r] - (one * k_solved[0] + two * k_solved[1])
                    e_rows[r] = e_rows[r] - (one * e_solved[0] + two * e_solved[1])
            k_rows[q] = k_done
            e_rows[q] = e_done
        e_now = jnp.concatenate(e_rows, axis=0)
        w_e[base : base + step, :] = e_now
        if base + step < size:
            k_now = jnp.concatenate(k_rows, axis=0)
            k_hi = k_now.astype(jnp.bfloat16)
            k_lo = (k_now - k_hi.astype(jnp.float32)).astype(jnp.bfloat16)
            e_hi = e_now.astype(jnp.bfloat16)
            e_lo = (e_now - e_hi.astype(jnp.float32)).astype(jnp.bfloat16)
            lhs = jnp.concatenate([k_hi, k_hi, k_lo], axis=0)
            k_rhs = jnp.concatenate([k_hi, k_lo, k_hi], axis=0)
            e_rhs = jnp.concatenate([e_hi, e_lo, e_hi], axis=0)
            k_fall = dot_t(lhs, k_rhs, ((0,), (0,)))
            e_fall = dot_t(lhs, e_rhs, ((0,), (0,)))
            w_k[base + step :, :] -= k_fall[base + step :, :]
            w_e[base + step :, :] -= e_fall[base + step :, :]


tail_lanes = 128


def encode(value, key, out_ref):
    cols = value.shape[1]
    top = jnp.max(jnp.abs(value), axis=1, keepdims=True)
    power = jnp.clip(jnp.floor(jnp.log2(32000.0 / jnp.maximum(top, 1e-30))), -60.0, 60.0)
    scaled = jnp.floor(value * jnp.exp2(power) + 0.5)
    out_ref[:, :cols] = scaled.astype(jnp.int32).astype(jnp.int16)
    lanes = lax.broadcasted_iota(jnp.int32, (value.shape[0], tail_lanes), 1)
    out_ref[:, cols:] = jnp.where(lanes < tail_lanes // 2, power, key).astype(jnp.int32).astype(jnp.int16)


def decode(ref):
    cols = ref.shape[1] - tail_lanes
    tail = ref[:, cols:].astype(jnp.int32).astype(jnp.float32)
    value = ref[:, :cols].astype(jnp.int32).astype(jnp.float32) * jnp.exp2(-tail[:, :1])
    return value, tail[:, tail_lanes - 1 :]


def run_copies(pairs, sems):
    copies = [
        pltpu.make_async_copy(source, target, sems.at[index])
        for index, (source, target) in enumerate(pairs)
    ]
    for copy in copies:
        copy.start()
    return copies


def leaf_kernel(counts, order_hbm, value_hbm, sketch_hbm, code_ref, sketch_ref, order, value, sketch, sems):
    pairs = [(value_hbm.at[0, 0], value), (order_hbm, order), (sketch_hbm, sketch)]
    for copy in run_copies(pairs, sems):
        copy.wait()
    key = order[lax.axis_index("pu") * counts[1] + lax.axis_index("pv")]
    encode(jnp.transpose(value[...]), key.astype(jnp.float32), code_ref)
    sketch_ref[...] = jnp.transpose(sketch[...])


def coded_leaf(value, sketch, order, counts):
    rows, cols = value.shape[2:]
    whole = pl.BlockSpec(memory_space=pltpu.VMEM)
    held = pl.BlockSpec(memory_space=pltpu.HBM)
    return pl.pallas_call(
        functools.partial(leaf_kernel, counts),
        in_specs=[held] * 3,
        out_specs=[whole] * 2,
        out_shape=[
            jax.ShapeDtypeStruct((cols, rows + tail_lanes), jnp.int16),
            jax.ShapeDtypeStruct(sketch.shape[::-1], jnp.float32),
        ],
        scratch_shapes=[
            pltpu.SMEM(order.shape, jnp.int32),
            pltpu.VMEM((rows, cols), jnp.float32),
            pltpu.VMEM(sketch.shape, jnp.float32),
            pltpu.SemaphoreType.DMA((3,)),
        ],
        cost_estimate=cost(1.5),
        compiler_params=pltpu.CompilerParams(vmem_limit_bytes=merge_vmem),
    )(in_hbm(order), in_hbm(value), in_hbm(sketch))


def edges_kernel(density, beside, ends, mids, pu_near, pu_far, sems):
    gu, gv = density.shape[:2]
    near_col = (gv - 1) * (1 - odd("pv"))
    far_col = (gv - 1) * odd("pv")
    pairs = [(density.at[(gu - 1) * (1 - odd("pu"))], pu_near), (density.at[(gu - 1) * odd("pu")], pu_far)]
    pairs += [(density.at[row, near_col], beside.at[row]) for row in range(gu)]
    pairs += [(density.at[(gu - 1) * row, far_col], ends.at[row]) for row in range(2)]
    pairs += [(density.at[row + 1, far_col], mids.at[row]) for row in range(gu - 2)]
    for copy in run_copies(pairs, sems):
        copy.wait()


def patch_edges(density):
    gu, gv, size, rhs = density.shape
    blocks = (gu, 2, gu - 2, gv, gv)
    return pl.pallas_call(
        edges_kernel,
        in_specs=[pl.BlockSpec(memory_space=pltpu.HBM)],
        out_specs=[pl.BlockSpec(memory_space=pltpu.VMEM)] * len(blocks),
        out_shape=[jax.ShapeDtypeStruct((count, size, rhs), density.dtype) for count in blocks],
        scratch_shapes=[pltpu.SemaphoreType.DMA((2 * gu + 2,))],
        cost_estimate=cost(2.5),
        compiler_params=pltpu.CompilerParams(vmem_limit_bytes=merge_vmem),
    )(in_hbm(density))


natural = ((1,), (0,))


def merge_kernel(has_path, last, mine_ref, other_ref, sketch_ref, *refs):
    if has_path:
        path_ref, *refs = refs
    left_ref, new_path_ref, w_k, w_e, z_ref = refs
    rank = mine_ref.shape[0]
    mine, my_key = decode(mine_ref)
    other, other_key = decode(other_ref)
    lead = my_key < other_key
    z_ref[:rank, :] = jnp.where(lead, mine, other)
    z_ref[rank:, :] = jnp.where(lead, other, mine)
    stacked = z_ref[...]
    sketch = sketch_ref[...]
    gram = split_dot(stacked, stacked, ((1,), (1,)))
    reduced = split_dot(sketch, gram, natural)
    w_k[...] = split_dot(reduced, sketch, ((1,), (1,)))
    rows = lax.broadcasted_iota(jnp.int32, (rank, rank), 0)
    cols = lax.broadcasted_iota(jnp.int32, (rank, rank), 1)
    w_e[...] = jnp.where(rows == cols, 1.0, 0.0)
    own = jnp.where(lead, reduced[:, :rank], reduced[:, rank:])
    if has_path:
        own = split_dot(own, path_ref[...], natural)
    eliminate(w_k, w_e)
    inverse = w_e[...]
    mixed = split_dot(inverse, sketch, natural)
    if last:
        count = left_ref.shape[1]
        part = z_ref[:, pl.ds(pl.multiple_of(lax.axis_index("pu") * count, 128), count)]
        left_ref[...] = split_dot(mixed, part, natural)
    else:
        encode(split_dot(mixed, z_ref[...], natural), jnp.minimum(my_key, other_key), left_ref)
    new_path_ref[...] = split_dot(inverse, own, natural)


def merge(level, mine, other, sketch, path, last_rows):
    rank, cols = mine.shape
    whole = pl.BlockSpec(memory_space=pltpu.VMEM)
    paths = () if path is None else (path,)
    if last_rows:
        left = jax.ShapeDtypeStruct((rank, last_rows), jnp.float32)
    else:
        left = jax.ShapeDtypeStruct(mine.shape, jnp.int16)
    return pl.pallas_call(
        functools.partial(merge_kernel, bool(paths), bool(last_rows)),
        in_specs=[whole, whole, whole] + [whole] * len(paths),
        out_specs=[whole, whole],
        out_shape=[left, jax.ShapeDtypeStruct((rank, rank), jnp.float32)],
        scratch_shapes=[
            pltpu.VMEM((rank, rank), jnp.float32),
            pltpu.VMEM((rank, rank), jnp.float32),
            pltpu.VMEM((2 * rank, cols - tail_lanes), jnp.float32),
        ],
        cost_estimate=cost((9, 1.5)[level] if level < 2 else 0.5),
        compiler_params=pltpu.CompilerParams(vmem_limit_bytes=merge_vmem),
    )(mine, other, sketch, *paths)


def from_partner(value, axis, mask):
    pairs = [(source, source ^ mask) for source in range(lax.axis_size(axis))]
    return lax.ppermute(value, axis, pairs)


def summed(values):
    return functools.reduce(lambda a, b: a + b, values)


def swapped(value, axis, far):
    count = lax.axis_size(axis)
    pairs = []
    for low in range(int(far), count - 1, 2):
        pairs += [(low, low + 1), (low + 1, low)]
    return lax.ppermute(value, axis, pairs)


def tied(*values):
    return lax.optimization_barrier(values)


def per_device(density, near_blocks, neighbours, far_right, far_left, sketch, patch_order):
    pu_count = lax.axis_size("pu")
    pv_count = lax.axis_size("pv")
    pv_index = lax.axis_index("pv")
    rhs = density.shape[3]
    pv_levels = pv_count.bit_length() - 1
    pu_levels = pu_count.bit_length() - 1
    levels = pv_levels + pu_levels

    def partner(value, level):
        if level < pv_levels:
            return from_partner(value, "pv", 1 << level)
        return from_partner(value, "pu", 1 << level - pv_levels)

    def halved(share):
        bit = pv_index & 1
        pairs = share.reshape(share.shape[0] // 2, 2, *share.shape[1:])
        keep = lax.dynamic_index_in_dim(pairs, bit, 1, keepdims=False)
        give = lax.dynamic_index_in_dim(pairs, 1 - bit, 1, keepdims=False)
        return keep + from_partner(give, "pv", 1)

    rows = far_left.shape[2]
    left, sketch = coded_leaf(far_left, sketch, patch_order, (pu_count, pv_count))
    other = partner(left, 0)
    density, left = tied(density, left)
    beside, ends, mids, pu_near, pu_far = patch_edges(density)
    beside = swapped(beside, "pv", False)
    pu_near = swapped(pu_near, "pu", False)
    pu_far = swapped(pu_far, "pu", True)

    coefs = []
    corrected = share = None
    pv_path = pu_path = None
    for level in range(levels):
        last = level == levels - 1
        coef = None
        if level:
            other = partner(left, level)
        if level in (1, 2) or last:
            links, left = tied(neighbours, left)
        if level == 1:
            corrected, coef = near_rows(density, pu_near, pu_far, near_blocks, far_right, links, corrected)
        elif level == 2:
            ends, mids, left = tied(ends, mids, left)
            ends = swapped(ends, "pv", True)
            mids = swapped(mids, "pv", True)
            corrected, coef = near_middle(density, near_blocks, far_right, links, corrected)
        elif last:
            corner_near, corner_far = patch_corners(beside, ends)
            corner_near = swapped(corner_near, "pu", False)
            corner_far = swapped(corner_far, "pu", True)
            corrected, coef = near_columns(
                density,
                pu_near,
                pu_far,
                corner_near,
                corner_far,
                beside,
                ends,
                mids,
                near_blocks,
                far_right,
                links,
                corrected,
            )
        if coef is not None:
            other, coef = tied(other, coef)
            coefs.append(coef)
        if last:
            coef = summed(coefs)
            share = lax.dot_general(coef, pv_path, (((0,), (1,)), ((), ())), precision=high)
            share = share.reshape(pv_count, rhs // pv_count, -1)
            share, other = tied(share, other)
            share = halved(share)
        path = pv_path if level < pv_levels else pu_path
        last_rows = rows // pu_count if last else 0
        left, path = merge(level, left, other, sketch, path, last_rows)
        if level < pv_levels:
            pv_path = path
        else:
            pu_path = path

    share, left = tied(share, left)
    far_index = pv_index // 2
    mine = lax.dynamic_index_in_dim(share, far_index, 0, keepdims=False)
    parts = [mine]
    for by in range(1, pv_count // 2):
        give = lax.dynamic_index_in_dim(share, far_index ^ by, 0, keepdims=False)
        parts.append(from_partner(give, "pv", 2 * by))
    root_coef = lax.dot_general(summed(parts), pu_path, (((1,), (1,)), ((), ())), precision=high)
    root_coef = summed([root_coef] + [from_partner(root_coef, "pu", by) for by in range(1, pu_count)])
    far_field = lax.dot_general(left, root_coef, (((0,), (1,)), ((), ())), precision=high)
    return (corrected, far_field)


def solution(mesh):
    in_specs = (
        P("pu", "pv", None, None),
        P("pu", "pv", None, None, None),
        P("pu", "pv", None),
        P("pu", "pv", None, None),
        P("pu", "pv", None, None),
        P(),
        P(),
    )
    out_specs = (P("pu", "pv", None, None), P("pu", "pv"))
    return jax.shard_map(
        per_device, mesh=mesh, in_specs=in_specs, out_specs=out_specs, check_vma=False
    )
```

```python
import functools

import jax
import jax.numpy as jnp
from jax import lax
from jax.experimental import pallas as pl
from jax.experimental.pallas import tpu as pltpu
from jax.sharding import PartitionSpec as P

high = lax.Precision.HIGH
empty_slot = 9
near_vmem = 17 * 1024 * 1024
merge_vmem = 8 * 1024 * 1024


def dot_t(a, b, dims, precision=None):
    return lax.dot_general(
        a, b, (dims, ((), ())), precision=precision, preferred_element_type=jnp.float32
    )


def split_dot(a, b, dims):
    return dot_t(a, b, dims, high)


def in_hbm(value):
    return pltpu.with_memory_space_constraint(value, pltpu.HBM)


def cost(microseconds):
    return pl.CostEstimate(flops=int(microseconds * 1.1e9), bytes_accessed=0, transcendentals=0)


def near_kernel(plan, n_src, nb_hbm, near_hbm, right_hbm, *refs):
    steps, spans, parts = plan
    srcs = refs[:n_src]
    out_ref, coef_ref, nb_ref, ext_ref, near_ref, right_ref, stage_ref, sems, out_sems, nb_sem = refs[-10:]
    step = pl.program_id(0)
    count = len(parts)
    links = pltpu.make_async_copy(nb_hbm, nb_ref, nb_sem)

    def fetch(at_step):
        found = []
        for index, (needed, views) in enumerate(spans):
            if needed == at_step:
                source, target = views(srcs, ext_ref)
                found.append(pltpu.make_async_copy(source, target, sems.at[index]))
        for part, (row, by, col, *_) in enumerate(parts):
            at = len(spans) + 2 * (at_step * count + part)
            for offset, source, target in ((0, near_hbm, near_ref), (1, right_hbm, right_ref)):
                found.append(
                    pltpu.make_async_copy(
                        source.at[row + by * at_step, col()], target.at[at_step, part], sems.at[at + offset]
                    )
                )
        return found

    def send(place, at_step, part):
        row, by, col = parts[part][:3]
        return pltpu.make_async_copy(
            stage_ref.at[place, part], out_ref.at[row + by * at_step, col()], out_sems.at[place, part]
        )

    @pl.when(step == 0)
    def _():
        links.start()
        for at_step in range(steps):
            for copy in fetch(at_step):
                copy.start()
        links.wait()

    for at_step in range(steps):

        @pl.when(step == at_step)
        def _():
            for copy in fetch(at_step):
                copy.wait()

    place = lax.rem(step, 2)

    @pl.when(step >= 2)
    def _():
        for part in range(count):
            send(place, step - 2, part).wait()

    rhs = ext_ref.shape[-1]
    tile = 256 if rhs % 256 == 0 else rhs
    for part, (row, by, col, ext_row, ext_by, middle) in enumerate(parts):
        centre = ext_row + ext_by * step
        weights = []
        places = []
        for slot in range(near_ref.shape[2]):
            link = nb_ref[row + by * step, col(), slot]
            there = jnp.minimum(link, empty_slot - 1)
            weight = near_ref[step, part, slot]
            weights.append(jnp.where(link < empty_slot, weight, jnp.zeros_like(weight)))
            places.append((centre - 1 + lax.div(there, 3), middle - 1 + lax.rem(there, 3)))
        weights = jnp.concatenate(weights, axis=1)
        for at in range(0, rhs, tile):
            values = [ext_ref[i, j, :, at : at + tile] for i, j in places]
            total = jnp.dot(weights, jnp.concatenate(values, axis=0), preferred_element_type=jnp.float32)
            own = ext_ref[centre, middle, :, at : at + tile].astype(jnp.float32)
            stage_ref[place, part, :, at : at + tile] = (own + total).astype(jnp.bfloat16)
        send(place, step, part).start()
    rights = jnp.concatenate([right_ref[step, part] for part in range(count)], axis=0)
    blocks = jnp.concatenate([stage_ref[place, part] for part in range(count)], axis=0)
    coef = dot_t(rights, blocks, ((0,), (0,)))

    @pl.when(step == 0)
    def _():
        coef_ref[...] = coef

    @pl.when(step > 0)
    def _():
        coef_ref[...] += coef

    @pl.when(step == steps - 1)
    def _():
        for at_step in range(max(steps - 2, 0), steps):
            for part in range(count):
                send(at_step % 2, at_step, part).wait()


def near_part(sources, plan, ext_shape, near_blocks, far_right, neighbours, prior, time):
    steps, spans, parts = plan
    count = len(parts)
    gu, gv, slots, size, _ = near_blocks.shape
    rhs = sources[0].shape[-1]
    rank = far_right.shape[-1]
    args = [neighbours, near_blocks, far_right, *sources]
    args = [in_hbm(value) if at < 3 or value.ndim > 3 else value for at, value in enumerate(args)]
    aliases = {}
    if prior is not None:
        aliases = {len(args): 0}
        args.append(prior)
    held = pl.BlockSpec(memory_space=pltpu.HBM)
    return pl.pallas_call(
        functools.partial(near_kernel, plan, len(sources)),
        grid=(steps,),
        in_specs=[held] * 3
        + [held if source.ndim == 4 else pl.BlockSpec(memory_space=pl.ANY) for source in sources]
        + [held] * len(aliases),
        out_specs=[held, pl.BlockSpec((rank, rhs), lambda i: (0, 0))],
        scratch_shapes=[
            pltpu.SMEM(neighbours.shape, jnp.int32),
            pltpu.VMEM((*ext_shape, size, rhs), jnp.bfloat16),
            pltpu.VMEM((steps, count, slots, size, size), jnp.bfloat16),
            pltpu.VMEM((steps, count, size, rank), jnp.bfloat16),
            pltpu.VMEM((2, count, size, rhs), jnp.bfloat16),
            pltpu.SemaphoreType.DMA((len(spans) + 2 * steps * count,)),
            pltpu.SemaphoreType.DMA((2, count)),
            pltpu.SemaphoreType.DMA,
        ],
        out_shape=[
            jax.ShapeDtypeStruct((gu, gv, size, rhs), jnp.bfloat16),
            jax.ShapeDtypeStruct((rank, rhs), jnp.float32),
        ],
        input_output_aliases=aliases,
        cost_estimate=cost(time),
        compiler_params=pltpu.CompilerParams(
            dimension_semantics=("arbitrary",), vmem_limit_bytes=near_vmem
        ),
    )(*args)


def odd(axis):
    return lax.rem(lax.axis_index(axis), 2)


def row_span(row, ext_row):
    return lambda srcs, ext: (srcs[0].at[row], ext.at[ext_row])


def near_middle(density, near_blocks, far_right, neighbours, prior):
    gu, gv = density.shape[:2]
    spans = [(max(row - 2, 0), row_span(row, row)) for row in range(gu)]
    parts = [(1, 1, lambda col=col: col, 1, 1, col) for col in range(1, gv - 1)]
    plan = (gu - 2, spans, parts)
    return near_part((density,), plan, (gu, gv), near_blocks, far_right, neighbours, prior, 0.5)


def near_rows(density, pu_near, pu_far, near_blocks, far_right, neighbours, prior):
    gu, gv = density.shape[:2]
    spans = [(at, row_span(row, ext_row)) for at, row, ext_row in ((0, 0, 1), (0, 1, 2), (1, gu - 2, 3), (1, gu - 1, 4))]
    spans.append((0, lambda srcs, ext: (srcs[1], ext.at[5 * (1 - odd("pu"))])))
    spans.append((0, lambda srcs, ext: (srcs[2], ext.at[5 * odd("pu")])))
    parts = [(0, gu - 1, lambda col=col: col, 1, 3, col) for col in range(1, gv - 1)]
    plan = (2, spans, parts)
    return near_part((density, pu_near, pu_far), plan, (6, gv), near_blocks, far_right, neighbours, prior, 0.5)


def near_columns(density, pu_near, pu_far, corner_near, corner_far, beside, ends, mids, near_blocks, far_right, neighbours, prior):
    gu, gv = density.shape[:2]
    per_step = 2
    spans = []
    parts = []

    def near_row():
        return (gu + 1) * (1 - odd("pu"))

    def far_row():
        return (gu + 1) * odd("pu")

    for far in (0, 1):

        def left_side(far=far):
            return 1 - odd("pv") if far else odd("pv")

        def inner(source, at, ext_row, far=far, left_side=left_side):
            def views(srcs, ext):
                view = srcs[source]
                if at is not None:
                    view = view.at[at]
                from_cols = pl.ds((gv - 2) * (1 - left_side()), 2)
                return view.at[from_cols], ext.at[ext_row(), pl.ds(3 * far + left_side(), 2)]

            return views

        def outer(source, at, ext_row, far=far, left_side=left_side):
            return lambda srcs, ext: (srcs[source].at[at], ext.at[ext_row(), 3 * far + 2 * (1 - left_side())])

        for row in range(gu):
            at = max((row - 1) // per_step, 0)
            here = lambda row=row: row + 1
            spans.append((at, inner(0, row, here)))
            if not far:
                spans.append((at, outer(5, row, here)))
            elif row in (0, gu - 1):
                spans.append((at, outer(6, min(row, 1), here)))
            else:
                spans.append((at, outer(7, row - 1, here)))
        spans.append((0, inner(1, None, near_row)))
        spans.append((0, inner(2, None, far_row)))
        spans.append((0, outer(3, far, near_row)))
        spans.append((0, outer(4, far, far_row)))
        col = lambda left_side=left_side: (gv - 1) * (1 - left_side())
        parts += [(row, per_step, col, row + 1, per_step, 3 * far + 1) for row in range(per_step)]
    plan = (gu // per_step, spans, parts)
    sources = (density, pu_near, pu_far, corner_near, corner_far, beside, ends, mids)
    return near_part(sources, plan, (gu + 2, 6), near_blocks, far_right, neighbours, prior, 0.5)


def corners_kernel(beside, ends, to_near, to_far):
    low = odd("pu")
    rows = beside.shape[0]
    for target, last in ((to_near, 1 - low), (to_far, low)):
        target[0] = beside[(rows - 1) * last]
        target[1] = ends[last]


def patch_corners(beside, ends):
    whole = pl.BlockSpec(memory_space=pltpu.VMEM)
    return pl.pallas_call(
        corners_kernel,
        in_specs=[whole, whole],
        out_specs=[whole, whole],
        out_shape=[jax.ShapeDtypeStruct(ends.shape, ends.dtype)] * 2,
        cost_estimate=cost(0.7),
        compiler_params=pltpu.CompilerParams(vmem_limit_bytes=merge_vmem),
    )(beside, ends)


def reciprocal(value):
    guess = pl.reciprocal(value, approx=True)
    return guess * (2.0 - value * guess)


def eliminate(w_k, w_e):
    size = w_k.shape[0]
    step = 32
    tile = 8
    sub = lax.broadcasted_iota(jnp.int32, (tile, size), 0)

    def spread(value, row):
        return jnp.broadcast_to(value[row : row + 1, :], (tile, size))

    for base in range(0, size, step):
        count = step // tile
        k_rows = [w_k[base + tile * r : base + tile * (r + 1), :] for r in range(count)]
        e_rows = [w_e[base + tile * r : base + tile * (r + 1), :] for r in range(count)]
        for q in range(count):
            at = base + tile * q
            cols = {
                (r, k): jnp.broadcast_to(k_rows[r][:, at + k : at + k + 1], (tile, size))
                for r in range(q, count)
                for k in range(tile)
            }
            k_done = k_rows[q]
            e_done = e_rows[q]
            for k in range(0, tile, 2):
                a = spread(cols[q, k], k)
                b = spread(cols[q, k], k + 1)
                c = spread(cols[q, k + 1], k + 1)
                det = a * c - b * b
                inverse = reciprocal(det)

                def solved(one, two):
                    return (c * one - b * two) * inverse, (a * two - b * one) * inverse

                k_one, k_two = spread(k_rows[q], k), spread(k_rows[q], k + 1)
                e_one, e_two = spread(e_rows[q], k), spread(e_rows[q], k + 1)
                k_solved = solved(k_one, k_two)
                e_solved = solved(e_one, e_two)
                links = {
                    m: solved(spread(cols[q, k], m), spread(cols[q, k + 1], m)) for m in range(k + 2, tile)
                }
                root = lax.rsqrt(a)
                second = lax.rsqrt(det) * a * root
                slope = b * root * root
                k_done = jnp.where(sub == k, k_one * root, k_done)
                e_done = jnp.where(sub == k, e_one * root, e_done)
                k_done = jnp.where(sub == k + 1, (k_two - slope * k_one) * second, k_done)
                e_done = jnp.where(sub == k + 1, (e_two - slope * e_one) * second, e_done)
                for r in range(q, count):
                    one, two = cols[r, k], cols[r, k + 1]
                    if r == q:
                        if k + 2 == tile:
                            continue
                        one = jnp.where(sub > k + 1, one, 0.0)
                        two = jnp.where(sub > k + 1, two, 0.0)
                    for m in range(k + 2, tile):
                        cols[r, m] = cols[r, m] - (one * links[m][0] + two * links[m][1])
                    k_rows[r] = k_rows[r] - (one * k_solved[0] + two * k_solved[1])
                    e_rows[r] = e_rows[r] - (one * e_solved[0] + two * e_solved[1])
            k_rows[q] = k_done
            e_rows[q] = e_done
        e_now = jnp.concatenate(e_rows, axis=0)
        w_e[base : base + step, :] = e_now
        if base + step < size:
            k_now = jnp.concatenate(k_rows, axis=0)
            k_hi = k_now.astype(jnp.bfloat16)
            k_lo = (k_now - k_hi.astype(jnp.float32)).astype(jnp.bfloat16)
            e_hi = e_now.astype(jnp.bfloat16)
            e_lo = (e_now - e_hi.astype(jnp.float32)).astype(jnp.bfloat16)
            lhs = jnp.concatenate([k_hi, k_hi, k_lo], axis=0)
            k_rhs = jnp.concatenate([k_hi, k_lo, k_hi], axis=0)
            e_rhs = jnp.concatenate([e_hi, e_lo, e_hi], axis=0)
            k_fall = dot_t(lhs, k_rhs, ((0,), (0,)))
            e_fall = dot_t(lhs, e_rhs, ((0,), (0,)))
            w_k[base + step :, :] -= k_fall[base + step :, :]
            w_e[base + step :, :] -= e_fall[base + step :, :]


tail_lanes = 128


def encode(value, key, out_ref):
    cols = value.shape[1]
    top = jnp.max(jnp.abs(value), axis=1, keepdims=True)
    power = jnp.clip(jnp.floor(jnp.log2(32000.0 / jnp.maximum(top, 1e-30))), -60.0, 60.0)
    scaled = jnp.floor(value * jnp.exp2(power) + 0.5)
    out_ref[:, :cols] = scaled.astype(jnp.int32).astype(jnp.int16)
    lanes = lax.broadcasted_iota(jnp.int32, (value.shape[0], tail_lanes), 1)
    out_ref[:, cols:] = jnp.where(lanes < tail_lanes // 2, power, key).astype(jnp.int32).astype(jnp.int16)


def decode(ref):
    cols = ref.shape[1] - tail_lanes
    tail = ref[:, cols:].astype(jnp.int32).astype(jnp.float32)
    value = ref[:, :cols].astype(jnp.int32).astype(jnp.float32) * jnp.exp2(-tail[:, :1])
    return value, tail[:, tail_lanes - 1 :]


def run_copies(pairs, sems):
    copies = [
        pltpu.make_async_copy(source, target, sems.at[index])
        for index, (source, target) in enumerate(pairs)
    ]
    for copy in copies:
        copy.start()
    return copies


def leaf_kernel(counts, order_hbm, value_hbm, sketch_hbm, code_ref, sketch_ref, order, value, sketch, sems):
    pairs = [(value_hbm.at[0, 0], value), (order_hbm, order), (sketch_hbm, sketch)]
    for copy in run_copies(pairs, sems):
        copy.wait()
    key = order[lax.axis_index("pu") * counts[1] + lax.axis_index("pv")]
    encode(jnp.transpose(value[...]), key.astype(jnp.float32), code_ref)
    sketch_ref[...] = jnp.transpose(sketch[...])


def coded_leaf(value, sketch, order, counts):
    rows, cols = value.shape[2:]
    whole = pl.BlockSpec(memory_space=pltpu.VMEM)
    held = pl.BlockSpec(memory_space=pltpu.HBM)
    return pl.pallas_call(
        functools.partial(leaf_kernel, counts),
        in_specs=[held] * 3,
        out_specs=[whole] * 2,
        out_shape=[
            jax.ShapeDtypeStruct((cols, rows + tail_lanes), jnp.int16),
            jax.ShapeDtypeStruct(sketch.shape[::-1], jnp.float32),
        ],
        scratch_shapes=[
            pltpu.SMEM(order.shape, jnp.int32),
            pltpu.VMEM((rows, cols), jnp.float32),
            pltpu.VMEM(sketch.shape, jnp.float32),
            pltpu.SemaphoreType.DMA((3,)),
        ],
        cost_estimate=cost(1.5),
        compiler_params=pltpu.CompilerParams(vmem_limit_bytes=merge_vmem),
    )(in_hbm(order), in_hbm(value), in_hbm(sketch))


def edges_kernel(density, beside, ends, mids, pu_near, pu_far, sems):
    gu, gv = density.shape[:2]
    near_col = (gv - 1) * (1 - odd("pv"))
    far_col = (gv - 1) * odd("pv")
    pairs = [(density.at[(gu - 1) * odd("pu"), col], pu_far.at[col]) for col in range(gv)]
    pairs += [(density.at[(gu - 1) * (1 - odd("pu")), col], pu_near.at[col]) for col in range(gv)]
    pairs += [(density.at[row, near_col], beside.at[row]) for row in range(gu)]
    pairs += [(density.at[(gu - 1) * row, far_col], ends.at[row]) for row in range(2)]
    pairs += [(density.at[row + 1, far_col], mids.at[row]) for row in range(gu - 2)]
    for copy in run_copies(pairs, sems):
        copy.wait()


def patch_edges(density):
    gu, gv, size, rhs = density.shape
    blocks = (gu, 2, gu - 2, gv, gv)
    return pl.pallas_call(
        edges_kernel,
        in_specs=[pl.BlockSpec(memory_space=pltpu.HBM)],
        out_specs=[pl.BlockSpec(memory_space=pltpu.VMEM)] * len(blocks),
        out_shape=[jax.ShapeDtypeStruct((count, size, rhs), density.dtype) for count in blocks],
        scratch_shapes=[pltpu.SemaphoreType.DMA((2 * gu + 2 * gv,))],
        cost_estimate=cost(2.5),
        compiler_params=pltpu.CompilerParams(vmem_limit_bytes=merge_vmem),
    )(in_hbm(density))


natural = ((1,), (0,))


def merge_kernel(has_path, last, mine_ref, other_ref, sketch_ref, *refs):
    if has_path:
        path_ref, *refs = refs
    left_ref, new_path_ref, w_k, w_e, z_ref = refs
    rank = mine_ref.shape[0]
    mine, my_key = decode(mine_ref)
    other, other_key = decode(other_ref)
    lead = my_key < other_key
    z_ref[:rank, :] = jnp.where(lead, mine, other)
    z_ref[rank:, :] = jnp.where(lead, other, mine)
    stacked = z_ref[...]
    sketch = sketch_ref[...]
    gram = split_dot(stacked, stacked, ((1,), (1,)))
    reduced = split_dot(sketch, gram, natural)
    w_k[...] = split_dot(reduced, sketch, ((1,), (1,)))
    rows = lax.broadcasted_iota(jnp.int32, (rank, rank), 0)
    cols = lax.broadcasted_iota(jnp.int32, (rank, rank), 1)
    w_e[...] = jnp.where(rows == cols, 1.0, 0.0)
    own = jnp.where(lead, reduced[:, :rank], reduced[:, rank:])
    if has_path:
        own = split_dot(own, path_ref[...], natural)
    eliminate(w_k, w_e)
    inverse = w_e[...]
    mixed = split_dot(inverse, sketch, natural)
    if last:
        count = left_ref.shape[1]
        part = z_ref[:, pl.ds(pl.multiple_of(lax.axis_index("pu") * count, 128), count)]
        left_ref[...] = split_dot(mixed, part, natural)
    else:
        encode(split_dot(mixed, z_ref[...], natural), jnp.minimum(my_key, other_key), left_ref)
    new_path_ref[...] = split_dot(inverse, own, natural)


def merge(level, mine, other, sketch, path, last_rows):
    rank, cols = mine.shape
    whole = pl.BlockSpec(memory_space=pltpu.VMEM)
    paths = () if path is None else (path,)
    if last_rows:
        left = jax.ShapeDtypeStruct((rank, last_rows), jnp.float32)
    else:
        left = jax.ShapeDtypeStruct(mine.shape, jnp.int16)
    return pl.pallas_call(
        functools.partial(merge_kernel, bool(paths), bool(last_rows)),
        in_specs=[whole, whole, whole] + [whole] * len(paths),
        out_specs=[whole, whole],
        out_shape=[left, jax.ShapeDtypeStruct((rank, rank), jnp.float32)],
        scratch_shapes=[
            pltpu.VMEM((rank, rank), jnp.float32),
            pltpu.VMEM((rank, rank), jnp.float32),
            pltpu.VMEM((2 * rank, cols - tail_lanes), jnp.float32),
        ],
        cost_estimate=cost((9, 1.5)[level] if level < 2 else 0.5),
        compiler_params=pltpu.CompilerParams(vmem_limit_bytes=merge_vmem),
    )(mine, other, sketch, *paths)


def from_partner(value, axis, mask):
    pairs = [(source, source ^ mask) for source in range(lax.axis_size(axis))]
    return lax.ppermute(value, axis, pairs)


def summed(values):
    return functools.reduce(lambda a, b: a + b, values)


def swapped(value, axis, far):
    count = lax.axis_size(axis)
    pairs = []
    for low in range(int(far), count - 1, 2):
        pairs += [(low, low + 1), (low + 1, low)]
    return lax.ppermute(value, axis, pairs)


def tied(*values):
    return lax.optimization_barrier(values)


def per_device(density, near_blocks, neighbours, far_right, far_left, sketch, patch_order):
    pu_count = lax.axis_size("pu")
    pv_count = lax.axis_size("pv")
    pv_index = lax.axis_index("pv")
    rhs = density.shape[3]
    pv_levels = pv_count.bit_length() - 1
    pu_levels = pu_count.bit_length() - 1
    levels = pv_levels + pu_levels

    def partner(value, level):
        if level < pv_levels:
            return from_partner(value, "pv", 1 << level)
        return from_partner(value, "pu", 1 << level - pv_levels)

    def halved(share):
        bit = pv_index & 1
        pairs = share.reshape(share.shape[0] // 2, 2, *share.shape[1:])
        keep = lax.dynamic_index_in_dim(pairs, bit, 1, keepdims=False)
        give = lax.dynamic_index_in_dim(pairs, 1 - bit, 1, keepdims=False)
        return keep + from_partner(give, "pv", 1)

    rows = far_left.shape[2]
    left, sketch = coded_leaf(far_left, sketch, patch_order, (pu_count, pv_count))
    other = partner(left, 0)
    density, left = tied(density, left)
    beside, ends, mids, pu_near, pu_far = patch_edges(density)
    beside = swapped(beside, "pv", False)
    pu_near = swapped(pu_near, "pu", False)
    pu_far = swapped(pu_far, "pu", True)

    coefs = []
    corrected = share = None
    pv_path = pu_path = None
    for level in range(levels):
        last = level == levels - 1
        coef = None
        if level:
            other = partner(left, level)
        if level in (1, 2) or last:
            links, left = tied(neighbours, left)
        if level == 1:
            corrected, coef = near_rows(density, pu_near, pu_far, near_blocks, far_right, links, corrected)
            ends, coef = tied(ends, coef)
            ends = swapped(ends, "pv", True)
        elif level == 2:
            mids, left = tied(mids, left)
            mids = swapped(mids, "pv", True)
            ends, other = tied(ends, other)
            corrected, coef = near_middle(density, near_blocks, far_right, links, corrected)
        elif last:
            corner_near, corner_far = patch_corners(beside, ends)
            corner_near = swapped(corner_near, "pu", False)
            corner_far = swapped(corner_far, "pu", True)
            corrected, coef = near_columns(
                density,
                pu_near,
                pu_far,
                corner_near,
                corner_far,
                beside,
                ends,
                mids,
                near_blocks,
                far_right,
                links,
                corrected,
            )
        if coef is not None:
            other, coef = tied(other, coef)
            coefs.append(coef)
        if last:
            coef = summed(coefs)
            share = lax.dot_general(coef, pv_path, (((0,), (1,)), ((), ())), precision=high)
            share = share.reshape(pv_count, rhs // pv_count, -1)
            share, other = tied(halved(share), other)
            here = pv_index // 2
            parts = [lax.dynamic_index_in_dim(share, here, 0, keepdims=False)]
            for by in range(1, pv_count // 2):
                give = lax.dynamic_index_in_dim(share, here ^ by, 0, keepdims=False)
                parts.append(from_partner(give, "pv", 2 * by))
        path = pv_path if level < pv_levels else pu_path
        last_rows = rows // pu_count if last else 0
        left, path = merge(level, left, other, sketch, path, last_rows)
        if level < pv_levels:
            pv_path = path
        else:
            pu_path = path

    root_coef = lax.dot_general(summed(parts), pu_path, (((1,), (1,)), ((), ())), precision=high)
    root_coef = summed([root_coef] + [from_partner(root_coef, "pu", by) for by in range(1, pu_count)])
    far_field = lax.dot_general(left, root_coef, (((0,), (1,)), ((), ())), precision=high)
    return (corrected, far_field)


def solution(mesh):
    in_specs = (
        P("pu", "pv", None, None),
        P("pu", "pv", None, None, None),
        P("pu", "pv", None),
        P("pu", "pv", None, None),
        P("pu", "pv", None, None),
        P(),
        P(),
    )
    out_specs = (P("pu", "pv", None, None), P("pu", "pv"))
    return jax.shard_map(
        per_device, mesh=mesh, in_specs=in_specs, out_specs=out_specs, check_vma=False
    )
```

```python
import functools

import jax
import jax.numpy as jnp
from jax import lax
from jax.experimental import pallas as pl
from jax.experimental.pallas import tpu as pltpu
from jax.sharding import PartitionSpec as P

high = lax.Precision.HIGH
empty_slot = 9
near_vmem = 17 * 1024 * 1024
merge_vmem = 8 * 1024 * 1024


def dot_t(a, b, dims, precision=None):
    return lax.dot_general(
        a, b, (dims, ((), ())), precision=precision, preferred_element_type=jnp.float32
    )


def split_dot(a, b, dims):
    return dot_t(a, b, dims, high)


def in_hbm(value):
    return pltpu.with_memory_space_constraint(value, pltpu.HBM)


def cost(microseconds):
    return pl.CostEstimate(flops=int(microseconds * 1.1e9), bytes_accessed=0, transcendentals=0)


def near_kernel(plan, n_src, nb_hbm, near_hbm, right_hbm, *refs):
    steps, spans, parts = plan
    srcs = refs[:n_src]
    out_ref, coef_ref, nb_ref, ext_ref, near_ref, right_ref, stage_ref, sems, out_sems, nb_sem = refs[-10:]
    step = pl.program_id(0)
    count = len(parts)
    links = pltpu.make_async_copy(nb_hbm, nb_ref, nb_sem)

    def fetch(at_step):
        found = []
        for index, (needed, views) in enumerate(spans):
            if needed == at_step:
                source, target = views(srcs, ext_ref)
                found.append(pltpu.make_async_copy(source, target, sems.at[index]))
        for part, (row, by, col, *_) in enumerate(parts):
            at = len(spans) + 2 * (at_step * count + part)
            for offset, source, target in ((0, near_hbm, near_ref), (1, right_hbm, right_ref)):
                found.append(
                    pltpu.make_async_copy(
                        source.at[row + by * at_step, col()], target.at[at_step, part], sems.at[at + offset]
                    )
                )
        return found

    def send(place, at_step, part):
        row, by, col = parts[part][:3]
        return pltpu.make_async_copy(
            stage_ref.at[place, part], out_ref.at[row + by * at_step, col()], out_sems.at[place, part]
        )

    @pl.when(step == 0)
    def _():
        links.start()
        for at_step in range(steps):
            for copy in fetch(at_step):
                copy.start()
        links.wait()

    for at_step in range(steps):

        @pl.when(step == at_step)
        def _():
            for copy in fetch(at_step):
                copy.wait()

    place = lax.rem(step, 2)

    @pl.when(step >= 2)
    def _():
        for part in range(count):
            send(place, step - 2, part).wait()

    rhs = ext_ref.shape[-1]
    tile = 256 if rhs % 256 == 0 else rhs
    for part, (row, by, col, ext_row, ext_by, middle) in enumerate(parts):
        centre = ext_row + ext_by * step
        weights = []
        places = []
        for slot in range(near_ref.shape[2]):
            link = nb_ref[row + by * step, col(), slot]
            there = jnp.minimum(link, empty_slot - 1)
            weight = near_ref[step, part, slot]
            weights.append(jnp.where(link < empty_slot, weight, jnp.zeros_like(weight)))
            places.append((centre - 1 + lax.div(there, 3), middle - 1 + lax.rem(there, 3)))
        weights = jnp.concatenate(weights, axis=1)
        for at in range(0, rhs, tile):
            values = [ext_ref[i, j, :, at : at + tile] for i, j in places]
            total = jnp.dot(weights, jnp.concatenate(values, axis=0), preferred_element_type=jnp.float32)
            own = ext_ref[centre, middle, :, at : at + tile].astype(jnp.float32)
            stage_ref[place, part, :, at : at + tile] = (own + total).astype(jnp.bfloat16)
        send(place, step, part).start()
    rights = jnp.concatenate([right_ref[step, part] for part in range(count)], axis=0)
    blocks = jnp.concatenate([stage_ref[place, part] for part in range(count)], axis=0)
    coef = dot_t(rights, blocks, ((0,), (0,)))

    @pl.when(step == 0)
    def _():
        coef_ref[...] = coef

    @pl.when(step > 0)
    def _():
        coef_ref[...] += coef

    @pl.when(step == steps - 1)
    def _():
        for at_step in range(max(steps - 2, 0), steps):
            for part in range(count):
                send(at_step % 2, at_step, part).wait()


def near_part(sources, plan, ext_shape, near_blocks, far_right, neighbours, prior, time):
    steps, spans, parts = plan
    count = len(parts)
    gu, gv, slots, size, _ = near_blocks.shape
    rhs = sources[0].shape[-1]
    rank = far_right.shape[-1]
    args = [neighbours, near_blocks, far_right, *sources]
    args = [in_hbm(value) if at < 3 or value.ndim > 3 else value for at, value in enumerate(args)]
    aliases = {}
    if prior is not None:
        aliases = {len(args): 0}
        args.append(prior)
    held = pl.BlockSpec(memory_space=pltpu.HBM)
    return pl.pallas_call(
        functools.partial(near_kernel, plan, len(sources)),
        grid=(steps,),
        in_specs=[held] * 3
        + [held if source.ndim == 4 else pl.BlockSpec(memory_space=pl.ANY) for source in sources]
        + [held] * len(aliases),
        out_specs=[held, pl.BlockSpec((rank, rhs), lambda i: (0, 0))],
        scratch_shapes=[
            pltpu.SMEM(neighbours.shape, jnp.int32),
            pltpu.VMEM((*ext_shape, size, rhs), jnp.bfloat16),
            pltpu.VMEM((steps, count, slots, size, size), jnp.bfloat16),
            pltpu.VMEM((steps, count, size, rank), jnp.bfloat16),
            pltpu.VMEM((2, count, size, rhs), jnp.bfloat16),
            pltpu.SemaphoreType.DMA((len(spans) + 2 * steps * count,)),
            pltpu.SemaphoreType.DMA((2, count)),
            pltpu.SemaphoreType.DMA,
        ],
        out_shape=[
            jax.ShapeDtypeStruct((gu, gv, size, rhs), jnp.bfloat16),
            jax.ShapeDtypeStruct((rank, rhs), jnp.float32),
        ],
        input_output_aliases=aliases,
        cost_estimate=cost(time),
        compiler_params=pltpu.CompilerParams(
            dimension_semantics=("arbitrary",), vmem_limit_bytes=near_vmem
        ),
    )(*args)


def odd(axis):
    return lax.rem(lax.axis_index(axis), 2)


def row_span(row, ext_row):
    return lambda srcs, ext: (srcs[0].at[row], ext.at[ext_row])


def near_middle(density, near_blocks, far_right, neighbours, prior):
    gu, gv = density.shape[:2]
    spans = [(max(row - 2, 0), row_span(row, row)) for row in range(gu)]
    parts = [(1, 1, lambda col=col: col, 1, 1, col) for col in range(1, gv - 1)]
    plan = (gu - 2, spans, parts)
    return near_part((density,), plan, (gu, gv), near_blocks, far_right, neighbours, prior, 0.5)


def near_rows(density, pu_near, pu_far, near_blocks, far_right, neighbours, prior):
    gu, gv = density.shape[:2]
    spans = [(at, row_span(row, ext_row)) for at, row, ext_row in ((0, 0, 1), (0, 1, 2), (1, gu - 2, 3), (1, gu - 1, 4))]
    spans.append((0, lambda srcs, ext: (srcs[1], ext.at[5 * (1 - odd("pu"))])))
    spans.append((0, lambda srcs, ext: (srcs[2], ext.at[5 * odd("pu")])))
    parts = [(0, gu - 1, lambda col=col: col, 1, 3, col) for col in range(1, gv - 1)]
    plan = (2, spans, parts)
    return near_part((density, pu_near, pu_far), plan, (6, gv), near_blocks, far_right, neighbours, prior, 0.5)


def near_column(far, density, pu_near, pu_far, corner_near, corner_far, halo, near_blocks, far_right, neighbours, prior):
    gu, gv = density.shape[:2]
    per_step = 3
    spans = []

    def near_row():
        return (gu + 1) * (1 - odd("pu"))

    def far_row():
        return (gu + 1) * odd("pu")

    def left_side():
        return 1 - odd("pv") if far else odd("pv")

    def inner(source, at, ext_row):
        def views(srcs, ext):
            view = srcs[source]
            if at is not None:
                view = view.at[at]
            return view.at[pl.ds((gv - 2) * (1 - left_side()), 2)], ext.at[ext_row(), pl.ds(left_side(), 2)]

        return views

    def outer(source, at, ext_row):
        return lambda srcs, ext: (srcs[source].at[at], ext.at[ext_row(), 2 * (1 - left_side())])

    for row in range(gu):
        at = max((row - 1) // per_step, 0)
        here = lambda row=row: row + 1
        spans.append((at, inner(0, row, here)))
        if len(halo) == 1:
            spans.append((at, outer(5, row, here)))
        elif row in (0, gu - 1):
            spans.append((at, outer(5, min(row, 1), here)))
        else:
            spans.append((at, outer(6, row - 1, here)))
    spans.append((0, inner(1, None, near_row)))
    spans.append((0, inner(2, None, far_row)))
    spans.append((0, outer(3, far, near_row)))
    spans.append((0, outer(4, far, far_row)))
    col = lambda: (gv - 1) * (1 - left_side())
    parts = [(row, per_step, col, row + 1, per_step, 1) for row in range(per_step)]
    plan = (gu // per_step, spans, parts)
    sources = (density, pu_near, pu_far, corner_near, corner_far, *halo)
    return near_part(sources, plan, (gu + 2, 3), near_blocks, far_right, neighbours, prior, 0.5)


def run_copies(pairs, sems):
    copies = [
        pltpu.make_async_copy(source, target, sems.at[index])
        for index, (source, target) in enumerate(pairs)
    ]
    for copy in copies:
        copy.start()
    return copies


def corners_kernel(beside, ends, to_near, to_far, sems):
    low = odd("pu")
    rows = beside.shape[0]
    pairs = []
    for target, last in ((to_near, 1 - low), (to_far, low)):
        pairs += [(beside.at[(rows - 1) * last], target.at[0]), (ends.at[last], target.at[1])]
    for copy in run_copies(pairs, sems):
        copy.wait()


def patch_corners(beside, ends):
    return pl.pallas_call(
        corners_kernel,
        in_specs=[pl.BlockSpec(memory_space=pl.ANY)] * 2,
        out_specs=[pl.BlockSpec(memory_space=pltpu.VMEM)] * 2,
        out_shape=[jax.ShapeDtypeStruct(ends.shape, ends.dtype)] * 2,
        scratch_shapes=[pltpu.SemaphoreType.DMA((4,))],
        cost_estimate=cost(0.7),
        compiler_params=pltpu.CompilerParams(vmem_limit_bytes=merge_vmem),
    )(beside, ends)


def reciprocal(value):
    guess = pl.reciprocal(value, approx=True)
    return guess * (2.0 - value * guess)


def eliminate(w_k, w_e):
    size = w_k.shape[0]
    step = 32
    tile = 8
    sub = lax.broadcasted_iota(jnp.int32, (tile, size), 0)

    def spread(value, row):
        return jnp.broadcast_to(value[row : row + 1, :], (tile, size))

    for base in range(0, size, step):
        count = step // tile
        k_rows = [w_k[base + tile * r : base + tile * (r + 1), :] for r in range(count)]
        e_rows = [w_e[base + tile * r : base + tile * (r + 1), :] for r in range(count)]
        for q in range(count):
            at = base + tile * q
            cols = {
                (r, k): jnp.broadcast_to(k_rows[r][:, at + k : at + k + 1], (tile, size))
                for r in range(q, count)
                for k in range(tile)
            }
            k_done = k_rows[q]
            e_done = e_rows[q]
            for k in range(0, tile, 2):
                a = spread(cols[q, k], k)
                b = spread(cols[q, k], k + 1)
                c = spread(cols[q, k + 1], k + 1)
                det = a * c - b * b
                inverse = reciprocal(det)

                def solved(one, two):
                    return (c * one - b * two) * inverse, (a * two - b * one) * inverse

                k_one, k_two = spread(k_rows[q], k), spread(k_rows[q], k + 1)
                e_one, e_two = spread(e_rows[q], k), spread(e_rows[q], k + 1)
                k_solved = solved(k_one, k_two)
                e_solved = solved(e_one, e_two)
                links = {
                    m: solved(spread(cols[q, k], m), spread(cols[q, k + 1], m)) for m in range(k + 2, tile)
                }
                root = lax.rsqrt(a)
                second = lax.rsqrt(det) * a * root
                slope = b * root * root
                k_done = jnp.where(sub == k, k_one * root, k_done)
                e_done = jnp.where(sub == k, e_one * root, e_done)
                k_done = jnp.where(sub == k + 1, (k_two - slope * k_one) * second, k_done)
                e_done = jnp.where(sub == k + 1, (e_two - slope * e_one) * second, e_done)
                for r in range(q, count):
                    one, two = cols[r, k], cols[r, k + 1]
                    if r == q:
                        if k + 2 == tile:
                            continue
                        one = jnp.where(sub > k + 1, one, 0.0)
                        two = jnp.where(sub > k + 1, two, 0.0)
                    for m in range(k + 2, tile):
                        cols[r, m] = cols[r, m] - (one * links[m][0] + two * links[m][1])
                    k_rows[r] = k_rows[r] - (one * k_solved[0] + two * k_solved[1])
                    e_rows[r] = e_rows[r] - (one * e_solved[0] + two * e_solved[1])
            k_rows[q] = k_done
            e_rows[q] = e_done
        e_now = jnp.concatenate(e_rows, axis=0)
        w_e[base : base + step, :] = e_now
        if base + step < size:
            k_now = jnp.concatenate(k_rows, axis=0)
            k_hi = k_now.astype(jnp.bfloat16)
            k_lo = (k_now - k_hi.astype(jnp.float32)).astype(jnp.bfloat16)
            e_hi = e_now.astype(jnp.bfloat16)
            e_lo = (e_now - e_hi.astype(jnp.float32)).astype(jnp.bfloat16)
            lhs = jnp.concatenate([k_hi, k_hi, k_lo], axis=0)
            k_rhs = jnp.concatenate([k_hi, k_lo, k_hi], axis=0)
            e_rhs = jnp.concatenate([e_hi, e_lo, e_hi], axis=0)
            k_fall = dot_t(lhs, k_rhs, ((0,), (0,)))
            e_fall = dot_t(lhs, e_rhs, ((0,), (0,)))
            w_k[base + step :, :] -= k_fall[base + step :, :]
            w_e[base + step :, :] -= e_fall[base + step :, :]


tail_lanes = 128


def encode(value, key, out_ref):
    cols = value.shape[1]
    top = jnp.max(jnp.abs(value), axis=1, keepdims=True)
    power = jnp.clip(jnp.floor(jnp.log2(32000.0 / jnp.maximum(top, 1e-30))), -60.0, 60.0)
    scaled = jnp.floor(value * jnp.exp2(power) + 0.5)
    out_ref[:, :cols] = scaled.astype(jnp.int32).astype(jnp.int16)
    lanes = lax.broadcasted_iota(jnp.int32, (value.shape[0], tail_lanes), 1)
    out_ref[:, cols:] = jnp.where(lanes < tail_lanes // 2, power, key).astype(jnp.int32).astype(jnp.int16)


def decode(ref):
    cols = ref.shape[1] - tail_lanes
    tail = ref[:, cols:].astype(jnp.int32).astype(jnp.float32)
    value = ref[:, :cols].astype(jnp.int32).astype(jnp.float32) * jnp.exp2(-tail[:, :1])
    return value, tail[:, tail_lanes - 1 :]


def leaf_kernel(counts, order_hbm, value_hbm, sketch_hbm, code_ref, sketch_ref, order, value, sketch, sems):
    pairs = [(value_hbm.at[0, 0], value), (order_hbm, order), (sketch_hbm, sketch)]
    for copy in run_copies(pairs, sems):
        copy.wait()
    key = order[lax.axis_index("pu") * counts[1] + lax.axis_index("pv")]
    encode(jnp.transpose(value[...]), key.astype(jnp.float32), code_ref)
    sketch_ref[...] = jnp.transpose(sketch[...])


def coded_leaf(value, sketch, order, counts):
    rows, cols = value.shape[2:]
    whole = pl.BlockSpec(memory_space=pltpu.VMEM)
    held = pl.BlockSpec(memory_space=pltpu.HBM)
    return pl.pallas_call(
        functools.partial(leaf_kernel, counts),
        in_specs=[held] * 3,
        out_specs=[whole] * 2,
        out_shape=[
            jax.ShapeDtypeStruct((cols, rows + tail_lanes), jnp.int16),
            jax.ShapeDtypeStruct(sketch.shape[::-1], jnp.float32),
        ],
        scratch_shapes=[
            pltpu.SMEM(order.shape, jnp.int32),
            pltpu.VMEM((rows, cols), jnp.float32),
            pltpu.VMEM(sketch.shape, jnp.float32),
            pltpu.SemaphoreType.DMA((3,)),
        ],
        cost_estimate=cost(1.5),
        compiler_params=pltpu.CompilerParams(vmem_limit_bytes=merge_vmem),
    )(in_hbm(order), in_hbm(value), in_hbm(sketch))


def edges_kernel(density, beside, ends, mids, pu_near, pu_far, sems):
    gu, gv = density.shape[:2]
    near_col = (gv - 1) * (1 - odd("pv"))
    far_col = (gv - 1) * odd("pv")
    pairs = [(density.at[(gu - 1) * odd("pu"), col], pu_far.at[col]) for col in range(gv)]
    pairs += [(density.at[(gu - 1) * (1 - odd("pu")), col], pu_near.at[col]) for col in range(gv)]
    pairs += [(density.at[row, near_col], beside.at[row]) for row in range(gu)]
    pairs += [(density.at[(gu - 1) * row, far_col], ends.at[row]) for row in range(2)]
    pairs += [(density.at[row + 1, far_col], mids.at[row]) for row in range(gu - 2)]
    for copy in run_copies(pairs, sems):
        copy.wait()


def patch_edges(density):
    gu, gv, size, rhs = density.shape
    blocks = (gu, 2, gu - 2, gv, gv)
    return pl.pallas_call(
        edges_kernel,
        in_specs=[pl.BlockSpec(memory_space=pltpu.HBM)],
        out_specs=[pl.BlockSpec(memory_space=pltpu.VMEM)] * len(blocks),
        out_shape=[jax.ShapeDtypeStruct((count, size, rhs), density.dtype) for count in blocks],
        scratch_shapes=[pltpu.SemaphoreType.DMA((2 * gu + 2 * gv,))],
        cost_estimate=cost(2.5),
        compiler_params=pltpu.CompilerParams(vmem_limit_bytes=merge_vmem),
    )(in_hbm(density))


natural = ((1,), (0,))


def merge_kernel(has_path, last, mine_ref, other_ref, sketch_ref, *refs):
    if has_path:
        path_ref, *refs = refs
    left_ref, new_path_ref, w_k, w_e, z_ref = refs
    rank = mine_ref.shape[0]
    mine, my_key = decode(mine_ref)
    other, other_key = decode(other_ref)
    lead = my_key < other_key
    z_ref[:rank, :] = jnp.where(lead, mine, other)
    z_ref[rank:, :] = jnp.where(lead, other, mine)
    stacked = z_ref[...]
    sketch = sketch_ref[...]
    gram = split_dot(stacked, stacked, ((1,), (1,)))
    reduced = split_dot(sketch, gram, natural)
    w_k[...] = split_dot(reduced, sketch, ((1,), (1,)))
    rows = lax.broadcasted_iota(jnp.int32, (rank, rank), 0)
    cols = lax.broadcasted_iota(jnp.int32, (rank, rank), 1)
    w_e[...] = jnp.where(rows == cols, 1.0, 0.0)
    own = jnp.where(lead, reduced[:, :rank], reduced[:, rank:])
    if has_path:
        own = split_dot(own, path_ref[...], natural)
    eliminate(w_k, w_e)
    inverse = w_e[...]
    mixed = split_dot(inverse, sketch, natural)
    if last:
        count = left_ref.shape[1]
        part = z_ref[:, pl.ds(pl.multiple_of(lax.axis_index("pu") * count, 128), count)]
        left_ref[...] = split_dot(mixed, part, natural)
    else:
        encode(split_dot(mixed, z_ref[...], natural), jnp.minimum(my_key, other_key), left_ref)
    new_path_ref[...] = split_dot(inverse, own, natural)


def merge(level, mine, other, sketch, path, last_rows):
    rank, cols = mine.shape
    whole = pl.BlockSpec(memory_space=pltpu.VMEM)
    paths = () if path is None else (path,)
    if last_rows:
        left = jax.ShapeDtypeStruct((rank, last_rows), jnp.float32)
    else:
        left = jax.ShapeDtypeStruct(mine.shape, jnp.int16)
    return pl.pallas_call(
        functools.partial(merge_kernel, bool(paths), bool(last_rows)),
        in_specs=[whole, whole, whole] + [whole] * len(paths),
        out_specs=[whole, whole],
        out_shape=[left, jax.ShapeDtypeStruct((rank, rank), jnp.float32)],
        scratch_shapes=[
            pltpu.VMEM((rank, rank), jnp.float32),
            pltpu.VMEM((rank, rank), jnp.float32),
            pltpu.VMEM((2 * rank, cols - tail_lanes), jnp.float32),
        ],
        cost_estimate=cost((9, 1.5)[level] if level < 2 else 0.5),
        compiler_params=pltpu.CompilerParams(vmem_limit_bytes=merge_vmem),
    )(mine, other, sketch, *paths)


def from_partner(value, axis, mask):
    pairs = [(source, source ^ mask) for source in range(lax.axis_size(axis))]
    return lax.ppermute(value, axis, pairs)


def summed(values):
    return functools.reduce(lambda a, b: a + b, values)


def swapped(value, axis, far):
    count = lax.axis_size(axis)
    pairs = []
    for low in range(int(far), count - 1, 2):
        pairs += [(low, low + 1), (low + 1, low)]
    return lax.ppermute(value, axis, pairs)


def tied(*values):
    return lax.optimization_barrier(values)


def per_device(density, near_blocks, neighbours, far_right, far_left, sketch, patch_order):
    pu_count = lax.axis_size("pu")
    pv_count = lax.axis_size("pv")
    pv_index = lax.axis_index("pv")
    rhs = density.shape[3]
    pv_levels = pv_count.bit_length() - 1
    pu_levels = pu_count.bit_length() - 1
    levels = pv_levels + pu_levels

    def partner(value, level):
        if level < pv_levels:
            return from_partner(value, "pv", 1 << level)
        return from_partner(value, "pu", 1 << level - pv_levels)

    def halved(share):
        bit = pv_index & 1
        pairs = share.reshape(share.shape[0] // 2, 2, *share.shape[1:])
        keep = lax.dynamic_index_in_dim(pairs, bit, 1, keepdims=False)
        give = lax.dynamic_index_in_dim(pairs, 1 - bit, 1, keepdims=False)
        return keep + from_partner(give, "pv", 1)

    rows = far_left.shape[2]
    left, sketch = coded_leaf(far_left, sketch, patch_order, (pu_count, pv_count))
    other = partner(left, 0)
    density, left = tied(density, left)
    beside, ends, mids, pu_near, pu_far = patch_edges(density)
    beside = swapped(beside, "pv", False)
    pu_near = swapped(pu_near, "pu", False)
    pu_far = swapped(pu_far, "pu", True)

    coefs = []
    corrected = share = None
    pv_path = pu_path = None
    for level in range(levels):
        last = level == levels - 1
        coef = None
        if level:
            other = partner(left, level)
        if level in (1, 2) or last:
            links, left = tied(neighbours, left)
        if level == 1:
            corrected, coef = near_middle(density, near_blocks, far_right, links, corrected)
        elif level == 2:
            ends, mids, left = tied(ends, mids, left)
            ends = swapped(ends, "pv", True)
            mids = swapped(mids, "pv", True)
            corrected, coef = near_rows(density, pu_near, pu_far, near_blocks, far_right, links, corrected)
        elif last:
            corner_near, corner_far = patch_corners(beside, ends)
            corner_near = swapped(corner_near, "pu", False)
            corner_far = swapped(corner_far, "pu", True)
            halo = (density, pu_near, pu_far, corner_near, corner_far)
            corrected, coef = near_column(0, *halo, (beside,), near_blocks, far_right, links, corrected)
            coefs.append(coef)
            corrected, coef = near_column(1, *halo, (ends, mids), near_blocks, far_right, links, corrected)
        if coef is not None:
            other, coef = tied(other, coef)
            coefs.append(coef)
        if last:
            coef = summed(coefs)
            share = lax.dot_general(coef, pv_path, (((0,), (1,)), ((), ())), precision=high)
            share = share.reshape(pv_count, rhs // pv_count, -1)
            share, other = tied(share, other)
            share = halved(share)
        path = pv_path if level < pv_levels else pu_path
        last_rows = rows // pu_count if last else 0
        left, path = merge(level, left, other, sketch, path, last_rows)
        if level < pv_levels:
            pv_path = path
        else:
            pu_path = path

    share, left = tied(share, left)
    far_index = pv_index // 2
    mine = lax.dynamic_index_in_dim(share, far_index, 0, keepdims=False)
    parts = [mine]
    for by in range(1, pv_count // 2):
        give = lax.dynamic_index_in_dim(share, far_index ^ by, 0, keepdims=False)
        parts.append(from_partner(give, "pv", 2 * by))
    root_coef = lax.dot_general(summed(parts), pu_path, (((1,), (1,)), ((), ())), precision=high)
    root_coef = summed([root_coef] + [from_partner(root_coef, "pu", by) for by in range(1, pu_count)])
    far_field = lax.dot_general(left, root_coef, (((0,), (1,)), ((), ())), precision=high)
    return (corrected, far_field)


def solution(mesh):
    in_specs = (
        P("pu", "pv", None, None),
        P("pu", "pv", None, None, None),
        P("pu", "pv", None),
        P("pu", "pv", None, None),
        P("pu", "pv", None, None),
        P(),
        P(),
    )
    out_specs = (P("pu", "pv", None, None), P("pu", "pv"))
    return jax.shard_map(
        per_device, mesh=mesh, in_specs=in_specs, out_specs=out_specs, check_vma=False
    )
```

```python
import functools

import jax
import jax.numpy as jnp
from jax import lax
from jax.experimental import pallas as pl
from jax.experimental.pallas import tpu as pltpu
from jax.sharding import PartitionSpec as P

high = lax.Precision.HIGH
empty_slot = 9
spare_vmem = 2 * 1024 * 1024
merge_vmem = 8 * 1024 * 1024


def dot_t(a, b, dims, precision=None):
    return lax.dot_general(
        a, b, (dims, ((), ())), precision=precision, preferred_element_type=jnp.float32
    )


def split_dot(a, b, dims):
    return dot_t(a, b, dims, high)


def in_hbm(value):
    return pltpu.with_memory_space_constraint(value, pltpu.HBM)


def cost(microseconds):
    return pl.CostEstimate(flops=int(microseconds * 1.1e9), bytes_accessed=0, transcendentals=0)


def near_kernel(plan, n_src, nb_hbm, near_hbm, right_hbm, *refs):
    steps, spans, parts = plan
    srcs = refs[:n_src]
    out_ref, coef_ref, nb_ref, ext_ref, near_ref, right_ref, stage_ref, sems, out_sems, nb_sem = refs[-10:]
    step = pl.program_id(0)
    count = len(parts)
    links = pltpu.make_async_copy(nb_hbm, nb_ref, nb_sem)

    def fetch(at_step):
        found = []
        for index, (needed, views) in enumerate(spans):
            if needed == at_step:
                source, target = views(srcs, ext_ref)
                found.append(pltpu.make_async_copy(source, target, sems.at[index]))
        for part, (row, by, col, *_) in enumerate(parts):
            at = len(spans) + 2 * (at_step * count + part)
            for offset, source, target in ((0, near_hbm, near_ref), (1, right_hbm, right_ref)):
                found.append(
                    pltpu.make_async_copy(
                        source.at[row + by * at_step, col()], target.at[at_step, part], sems.at[at + offset]
                    )
                )
        return found

    def send(place, at_step, part):
        row, by, col = parts[part][:3]
        return pltpu.make_async_copy(
            stage_ref.at[place, part], out_ref.at[row + by * at_step, col()], out_sems.at[place, part]
        )

    @pl.when(step == 0)
    def _():
        links.start()
        for at_step in range(steps):
            for copy in fetch(at_step):
                copy.start()
        links.wait()

    for at_step in range(steps):

        @pl.when(step == at_step)
        def _():
            for copy in fetch(at_step):
                copy.wait()

    place = lax.rem(step, 2)

    @pl.when(step >= 2)
    def _():
        for part in range(count):
            send(place, step - 2, part).wait()

    rhs = ext_ref.shape[-1]
    tile = 256 if rhs % 256 == 0 else rhs
    for part, (row, by, col, ext_row, ext_by, middle) in enumerate(parts):
        centre = ext_row + ext_by * step
        weights = []
        places = []
        for slot in range(near_ref.shape[2]):
            link = nb_ref[row + by * step, col(), slot]
            there = jnp.minimum(link, empty_slot - 1)
            weight = near_ref[step, part, slot]
            weights.append(jnp.where(link < empty_slot, weight, jnp.zeros_like(weight)))
            places.append((centre - 1 + lax.div(there, 3), middle - 1 + lax.rem(there, 3)))
        weights = jnp.concatenate(weights, axis=1)
        for at in range(0, rhs, tile):
            values = [ext_ref[i, j, :, at : at + tile] for i, j in places]
            total = jnp.dot(weights, jnp.concatenate(values, axis=0), preferred_element_type=jnp.float32)
            own = ext_ref[centre, middle, :, at : at + tile].astype(jnp.float32)
            stage_ref[place, part, :, at : at + tile] = (own + total).astype(jnp.bfloat16)
        send(place, step, part).start()
    rights = jnp.concatenate([right_ref[step, part] for part in range(count)], axis=0)
    blocks = jnp.concatenate([stage_ref[place, part] for part in range(count)], axis=0)
    coef = dot_t(rights, blocks, ((0,), (0,)))

    @pl.when(step == 0)
    def _():
        coef_ref[...] = coef

    @pl.when(step > 0)
    def _():
        coef_ref[...] += coef

    @pl.when(step == steps - 1)
    def _():
        for at_step in range(max(steps - 2, 0), steps):
            for part in range(count):
                send(at_step % 2, at_step, part).wait()


def near_part(sources, plan, ext_shape, near_blocks, far_right, neighbours, prior, time):
    steps, spans, parts = plan
    count = len(parts)
    gu, gv, slots, size, _ = near_blocks.shape
    rhs = sources[0].shape[-1]
    rank = far_right.shape[-1]
    args = [neighbours, near_blocks, far_right, *sources]
    args = [in_hbm(value) if at < 3 or value.ndim > 3 else value for at, value in enumerate(args)]
    aliases = {}
    if prior is not None:
        aliases = {len(args): 0}
        args.append(prior)
    held = pl.BlockSpec(memory_space=pltpu.HBM)
    blocks = ext_shape[0] * ext_shape[1] + 2 * count + 2
    scratch = 2 * size * (blocks * rhs + steps * count * (slots * size + rank)) + 8 * rank * rhs
    return pl.pallas_call(
        functools.partial(near_kernel, plan, len(sources)),
        grid=(steps,),
        in_specs=[held] * 3
        + [held if source.ndim == 4 else pl.BlockSpec(memory_space=pl.ANY) for source in sources]
        + [held] * len(aliases),
        out_specs=[held, pl.BlockSpec((rank, rhs), lambda i: (0, 0))],
        scratch_shapes=[
            pltpu.SMEM(neighbours.shape, jnp.int32),
            pltpu.VMEM((*ext_shape, size, rhs), jnp.bfloat16),
            pltpu.VMEM((steps, count, slots, size, size), jnp.bfloat16),
            pltpu.VMEM((steps, count, size, rank), jnp.bfloat16),
            pltpu.VMEM((2, count, size, rhs), jnp.bfloat16),
            pltpu.SemaphoreType.DMA((len(spans) + 2 * steps * count,)),
            pltpu.SemaphoreType.DMA((2, count)),
            pltpu.SemaphoreType.DMA,
        ],
        out_shape=[
            jax.ShapeDtypeStruct((gu, gv, size, rhs), jnp.bfloat16),
            jax.ShapeDtypeStruct((rank, rhs), jnp.float32),
        ],
        input_output_aliases=aliases,
        cost_estimate=cost(time),
        compiler_params=pltpu.CompilerParams(
            dimension_semantics=("arbitrary",), vmem_limit_bytes=scratch + spare_vmem
        ),
    )(*args)


def odd(axis):
    return lax.rem(lax.axis_index(axis), 2)


def row_span(row, ext_row):
    return lambda srcs, ext: (srcs[0].at[row], ext.at[ext_row])


def near_middle(density, near_blocks, far_right, neighbours, prior):
    gu, gv = density.shape[:2]
    spans = [(max(row - 2, 0), row_span(row, row)) for row in range(gu)]
    parts = [(1, 1, lambda col=col: col, 1, 1, col) for col in range(1, gv - 1)]
    plan = (gu - 2, spans, parts)
    return near_part((density,), plan, (gu, gv), near_blocks, far_right, neighbours, prior, 0.5)


def near_rows(density, pu_near, pu_far, near_blocks, far_right, neighbours, prior):
    gu, gv = density.shape[:2]
    spans = [(at, row_span(row, ext_row)) for at, row, ext_row in ((0, 0, 1), (0, 1, 2), (1, gu - 2, 3), (1, gu - 1, 4))]
    spans.append((0, lambda srcs, ext: (srcs[1], ext.at[5 * (1 - odd("pu"))])))
    spans.append((0, lambda srcs, ext: (srcs[2], ext.at[5 * odd("pu")])))
    parts = [(0, gu - 1, lambda col=col: col, 1, 3, col) for col in range(1, gv - 1)]
    plan = (2, spans, parts)
    return near_part((density, pu_near, pu_far), plan, (6, gv), near_blocks, far_right, neighbours, prior, 0.5)


def near_column(far, density, pu_near, pu_far, corner_near, corner_far, halo, near_blocks, far_right, neighbours, prior):
    gu, gv = density.shape[:2]
    per_step = 3
    spans = []

    def near_row():
        return (gu + 1) * (1 - odd("pu"))

    def far_row():
        return (gu + 1) * odd("pu")

    def left_side():
        return 1 - odd("pv") if far else odd("pv")

    def inner(source, at, ext_row):
        def views(srcs, ext):
            view = srcs[source]
            if at is not None:
                view = view.at[at]
            return view.at[pl.ds((gv - 2) * (1 - left_side()), 2)], ext.at[ext_row(), pl.ds(left_side(), 2)]

        return views

    def outer(source, at, ext_row):
        return lambda srcs, ext: (srcs[source].at[at], ext.at[ext_row(), 2 * (1 - left_side())])

    for row in range(gu):
        at = max((row - 1) // per_step, 0)
        here = lambda row=row: row + 1
        spans.append((at, inner(0, row, here)))
        if len(halo) == 1:
            spans.append((at, outer(5, row, here)))
        else:
            order = far_order(gu).index(row)
            sent = halo[0].shape[0]
            spans.append((at, outer(5, order, here) if order < sent else outer(6, order - sent, here)))
    spans.append((0, inner(1, None, near_row)))
    spans.append((0, inner(2, None, far_row)))
    spans.append((0, outer(3, 0, near_row)))
    spans.append((0, outer(4, 0, far_row)))
    col = lambda: (gv - 1) * (1 - left_side())
    parts = [(row, per_step, col, row + 1, per_step, 1) for row in range(per_step)]
    plan = (gu // per_step, spans, parts)
    sources = (density, pu_near, pu_far, corner_near, corner_far, *halo)
    return near_part(sources, plan, (gu + 2, 3), near_blocks, far_right, neighbours, prior, 0.5)


def run_copies(pairs, sems):
    copies = [
        pltpu.make_async_copy(source, target, sems.at[index])
        for index, (source, target) in enumerate(pairs)
    ]
    for copy in copies:
        copy.start()
    return copies


def corners_kernel(last, column, to_near, to_far):
    low = odd("pu")
    to_near[0] = column[last * (1 - low)]
    to_far[0] = column[last * low]


def swapped_corners(column, last):
    whole = pl.BlockSpec(memory_space=pltpu.VMEM)
    to_near, to_far = pl.pallas_call(
        functools.partial(corners_kernel, last),
        in_specs=[whole],
        out_specs=[whole, whole],
        out_shape=[jax.ShapeDtypeStruct((1, *column.shape[1:]), column.dtype)] * 2,
        cost_estimate=cost(0.5),
        compiler_params=pltpu.CompilerParams(vmem_limit_bytes=merge_vmem),
    )(column)
    return swapped(to_near, "pu", False), swapped(to_far, "pu", True)


def reciprocal(value):
    guess = pl.reciprocal(value, approx=True)
    return guess * (2.0 - value * guess)


def eliminate(w_k, w_e):
    size = w_k.shape[0]
    step = 32
    tile = 8
    sub = lax.broadcasted_iota(jnp.int32, (tile, size), 0)

    def spread(value, row):
        return jnp.broadcast_to(value[row : row + 1, :], (tile, size))

    for base in range(0, size, step):
        count = step // tile
        k_rows = [w_k[base + tile * r : base + tile * (r + 1), :] for r in range(count)]
        e_rows = [w_e[base + tile * r : base + tile * (r + 1), :] for r in range(count)]
        for q in range(count):
            at = base + tile * q
            cols = {
                (r, k): jnp.broadcast_to(k_rows[r][:, at + k : at + k + 1], (tile, size))
                for r in range(q, count)
                for k in range(tile)
            }
            k_done = k_rows[q]
            e_done = e_rows[q]
            for k in range(0, tile, 2):
                a = spread(cols[q, k], k)
                b = spread(cols[q, k], k + 1)
                c = spread(cols[q, k + 1], k + 1)
                det = a * c - b * b
                inverse = reciprocal(det)

                def solved(one, two):
                    return (c * one - b * two) * inverse, (a * two - b * one) * inverse

                k_one, k_two = spread(k_rows[q], k), spread(k_rows[q], k + 1)
                e_one, e_two = spread(e_rows[q], k), spread(e_rows[q], k + 1)
                k_solved = solved(k_one, k_two)
                e_solved = solved(e_one, e_two)
                links = {
                    m: solved(spread(cols[q, k], m), spread(cols[q, k + 1], m)) for m in range(k + 2, tile)
                }
                root = lax.rsqrt(a)
                second = lax.rsqrt(det) * a * root
                slope = b * root * root
                k_done = jnp.where(sub == k, k_one * root, k_done)
                e_done = jnp.where(sub == k, e_one * root, e_done)
                k_done = jnp.where(sub == k + 1, (k_two - slope * k_one) * second, k_done)
                e_done = jnp.where(sub == k + 1, (e_two - slope * e_one) * second, e_done)
                for r in range(q, count):
                    one, two = cols[r, k], cols[r, k + 1]
                    if r == q:
                        if k + 2 == tile:
                            continue
                        one = jnp.where(sub > k + 1, one, 0.0)
                        two = jnp.where(sub > k + 1, two, 0.0)
                    for m in range(k + 2, tile):
                        cols[r, m] = cols[r, m] - (one * links[m][0] + two * links[m][1])
                    k_rows[r] = k_rows[r] - (one * k_solved[0] + two * k_solved[1])
                    e_rows[r] = e_rows[r] - (one * e_solved[0] + two * e_solved[1])
            k_rows[q] = k_done
            e_rows[q] = e_done
        e_now = jnp.concatenate(e_rows, axis=0)
        w_e[base : base + step, :] = e_now
        if base + step < size:
            k_now = jnp.concatenate(k_rows, axis=0)
            k_hi = k_now.astype(jnp.bfloat16)
            k_lo = (k_now - k_hi.astype(jnp.float32)).astype(jnp.bfloat16)
            e_hi = e_now.astype(jnp.bfloat16)
            e_lo = (e_now - e_hi.astype(jnp.float32)).astype(jnp.bfloat16)
            lhs = jnp.concatenate([k_hi, k_hi, k_lo], axis=0)
            k_rhs = jnp.concatenate([k_hi, k_lo, k_hi], axis=0)
            e_rhs = jnp.concatenate([e_hi, e_lo, e_hi], axis=0)
            k_fall = dot_t(lhs, k_rhs, ((0,), (0,)))
            e_fall = dot_t(lhs, e_rhs, ((0,), (0,)))
            w_k[base + step :, :] -= k_fall[base + step :, :]
            w_e[base + step :, :] -= e_fall[base + step :, :]


tail_lanes = 128


def encode(value, key, out_ref):
    cols = value.shape[1]
    top = jnp.max(jnp.abs(value), axis=1, keepdims=True)
    power = jnp.clip(jnp.floor(jnp.log2(32000.0 / jnp.maximum(top, 1e-30))), -60.0, 60.0)
    scaled = jnp.floor(value * jnp.exp2(power) + 0.5)
    out_ref[:, :cols] = scaled.astype(jnp.int32).astype(jnp.int16)
    lanes = lax.broadcasted_iota(jnp.int32, (value.shape[0], tail_lanes), 1)
    out_ref[:, cols:] = jnp.where(lanes < tail_lanes // 2, power, key).astype(jnp.int32).astype(jnp.int16)


def decode(ref):
    cols = ref.shape[1] - tail_lanes
    tail = ref[:, cols:].astype(jnp.int32).astype(jnp.float32)
    value = ref[:, :cols].astype(jnp.int32).astype(jnp.float32) * jnp.exp2(-tail[:, :1])
    return value, tail[:, tail_lanes - 1 :]


def run_copies(pairs, sems):
    copies = [
        pltpu.make_async_copy(source, target, sems.at[index])
        for index, (source, target) in enumerate(pairs)
    ]
    for copy in copies:
        copy.start()
    return copies


def leaf_kernel(counts, order_hbm, value_hbm, sketch_hbm, code_ref, sketch_ref, order, value, sketch, sems):
    pairs = [(value_hbm.at[0, 0], value), (order_hbm, order), (sketch_hbm, sketch)]
    for copy in run_copies(pairs, sems):
        copy.wait()
    key = order[lax.axis_index("pu") * counts[1] + lax.axis_index("pv")]
    encode(jnp.transpose(value[...]), key.astype(jnp.float32), code_ref)
    sketch_ref[...] = jnp.transpose(sketch[...])


def coded_leaf(value, sketch, order, counts):
    rows, cols = value.shape[2:]
    whole = pl.BlockSpec(memory_space=pltpu.VMEM)
    held = pl.BlockSpec(memory_space=pltpu.HBM)
    return pl.pallas_call(
        functools.partial(leaf_kernel, counts),
        in_specs=[held] * 3,
        out_specs=[whole] * 2,
        out_shape=[
            jax.ShapeDtypeStruct((cols, rows + tail_lanes), jnp.int16),
            jax.ShapeDtypeStruct(sketch.shape[::-1], jnp.float32),
        ],
        scratch_shapes=[
            pltpu.SMEM(order.shape, jnp.int32),
            pltpu.VMEM((rows, cols), jnp.float32),
            pltpu.VMEM(sketch.shape, jnp.float32),
            pltpu.SemaphoreType.DMA((3,)),
        ],
        cost_estimate=cost(1.5),
        compiler_params=pltpu.CompilerParams(vmem_limit_bytes=merge_vmem),
    )(in_hbm(order), in_hbm(value), in_hbm(sketch))


def far_order(gu):
    return [0, gu - 1, *range(1, gu - 1)]


def edges_kernel(density, beside, ends, mids, pu_near, pu_far, sems):
    gu, gv = density.shape[:2]
    near_col = (gv - 1) * (1 - odd("pv"))
    far_col = (gv - 1) * odd("pv")
    pairs = [(density.at[row, near_col], beside.at[row]) for row in range(gu)]
    for at, row in enumerate(far_order(gu)):
        target = ends.at[at] if at < ends.shape[0] else mids.at[at - ends.shape[0]]
        pairs.append((density.at[row, far_col], target))
    pairs.append((density.at[(gu - 1) * (1 - odd("pu"))], pu_near))
    pairs.append((density.at[(gu - 1) * odd("pu")], pu_far))
    for copy in run_copies(pairs, sems):
        copy.wait()


def patch_edges(density):
    gu, gv, size, rhs = density.shape
    blocks = (gu, 3, gu - 3, gv, gv)
    return pl.pallas_call(
        edges_kernel,
        in_specs=[pl.BlockSpec(memory_space=pltpu.HBM)],
        out_specs=[pl.BlockSpec(memory_space=pltpu.VMEM)] * len(blocks),
        out_shape=[jax.ShapeDtypeStruct((count, size, rhs), density.dtype) for count in blocks],
        scratch_shapes=[pltpu.SemaphoreType.DMA((2 * gu + 2,))],
        cost_estimate=cost(2.5),
        compiler_params=pltpu.CompilerParams(vmem_limit_bytes=merge_vmem),
    )(in_hbm(density))


natural = ((1,), (0,))


def merge_kernel(has_path, last, mine_ref, other_ref, sketch_ref, *refs):
    if has_path:
        path_ref, *refs = refs
    left_ref, new_path_ref, w_k, w_e, z_ref = refs
    rank = mine_ref.shape[0]
    mine, my_key = decode(mine_ref)
    other, other_key = decode(other_ref)
    lead = my_key < other_key
    z_ref[:rank, :] = jnp.where(lead, mine, other)
    z_ref[rank:, :] = jnp.where(lead, other, mine)
    stacked = z_ref[...]
    sketch = sketch_ref[...]
    gram = split_dot(stacked, stacked, ((1,), (1,)))
    reduced = split_dot(sketch, gram, natural)
    w_k[...] = split_dot(reduced, sketch, ((1,), (1,)))
    rows = lax.broadcasted_iota(jnp.int32, (rank, rank), 0)
    cols = lax.broadcasted_iota(jnp.int32, (rank, rank), 1)
    w_e[...] = jnp.where(rows == cols, 1.0, 0.0)
    own = jnp.where(lead, reduced[:, :rank], reduced[:, rank:])
    if has_path:
        own = split_dot(own, path_ref[...], natural)
    eliminate(w_k, w_e)
    inverse = w_e[...]
    mixed = split_dot(inverse, sketch, natural)
    if last:
        count = left_ref.shape[1]
        part = z_ref[:, pl.ds(pl.multiple_of(lax.axis_index("pu") * count, 128), count)]
        left_ref[...] = split_dot(mixed, part, natural)
    else:
        encode(split_dot(mixed, z_ref[...], natural), jnp.minimum(my_key, other_key), left_ref)
    new_path_ref[...] = split_dot(inverse, own, natural)


def merge(level, mine, other, sketch, path, last_rows):
    rank, cols = mine.shape
    whole = pl.BlockSpec(memory_space=pltpu.VMEM)
    paths = () if path is None else (path,)
    if last_rows:
        left = jax.ShapeDtypeStruct((rank, last_rows), jnp.float32)
    else:
        left = jax.ShapeDtypeStruct(mine.shape, jnp.int16)
    return pl.pallas_call(
        functools.partial(merge_kernel, bool(paths), bool(last_rows)),
        in_specs=[whole, whole, whole] + [whole] * len(paths),
        out_specs=[whole, whole],
        out_shape=[left, jax.ShapeDtypeStruct((rank, rank), jnp.float32)],
        scratch_shapes=[
            pltpu.VMEM((rank, rank), jnp.float32),
            pltpu.VMEM((rank, rank), jnp.float32),
            pltpu.VMEM((2 * rank, cols - tail_lanes), jnp.float32),
        ],
        cost_estimate=cost((9, 1.5)[level] if level < 2 else 0.5),
        compiler_params=pltpu.CompilerParams(vmem_limit_bytes=merge_vmem),
    )(mine, other, sketch, *paths)


def from_partner(value, axis, mask):
    pairs = [(source, source ^ mask) for source in range(lax.axis_size(axis))]
    return lax.ppermute(value, axis, pairs)


def summed(values):
    return functools.reduce(lambda a, b: a + b, values)


def swapped(value, axis, far):
    count = lax.axis_size(axis)
    pairs = []
    for low in range(int(far), count - 1, 2):
        pairs += [(low, low + 1), (low + 1, low)]
    return lax.ppermute(value, axis, pairs)


def tied(*values):
    return lax.optimization_barrier(values)


def per_device(density, near_blocks, neighbours, far_right, far_left, sketch, patch_order):
    pu_count = lax.axis_size("pu")
    pv_count = lax.axis_size("pv")
    pv_index = lax.axis_index("pv")
    rhs = density.shape[3]
    pv_levels = pv_count.bit_length() - 1
    pu_levels = pu_count.bit_length() - 1
    levels = pv_levels + pu_levels

    def partner(value, level):
        if level < pv_levels:
            return from_partner(value, "pv", 1 << level)
        return from_partner(value, "pu", 1 << level - pv_levels)

    def halved(share):
        bit = pv_index & 1
        pairs = share.reshape(share.shape[0] // 2, 2, *share.shape[1:])
        keep = lax.dynamic_index_in_dim(pairs, bit, 1, keepdims=False)
        give = lax.dynamic_index_in_dim(pairs, 1 - bit, 1, keepdims=False)
        return keep + from_partner(give, "pv", 1)

    rows = far_left.shape[2]
    left, sketch = coded_leaf(far_left, sketch, patch_order, (pu_count, pv_count))
    other = partner(left, 0)
    density, left = tied(density, left)
    beside, ends, mids, pu_near, pu_far = patch_edges(density)
    beside = swapped(beside, "pv", False)
    pu_near = swapped(pu_near, "pu", False)
    pu_far = swapped(pu_far, "pu", True)

    coefs = []
    corrected = share = None
    pv_path = pu_path = None
    for level in range(levels):
        last = level == levels - 1
        coef = None
        if level:
            other = partner(left, level)
        if level in (1, 2) or last:
            links, left = tied(neighbours, left)
        if level == 1:
            corrected, coef = near_middle(density, near_blocks, far_right, links, corrected)
        elif level == 2:
            ends, mids, left = tied(ends, mids, left)
            ends = swapped(ends, "pv", True)
            mids = swapped(mids, "pv", True)
            corrected, coef = near_rows(density, pu_near, pu_far, near_blocks, far_right, links, corrected)
            beside, coef = tied(beside, coef)
            near_corners = swapped_corners(beside, density.shape[0] - 1)
        elif last:
            ends, left = tied(ends, left)
            far_corners = swapped_corners(ends, 1)
            halo = (density, pu_near, pu_far)
            corrected, coef = near_column(
                0, *halo, *near_corners, (beside,), near_blocks, far_right, links, corrected
            )
            coefs.append(coef)
            corrected, coef = near_column(
                1, *halo, *far_corners, (ends, mids), near_blocks, far_right, links, corrected
            )
        if coef is not None:
            other, coef = tied(other, coef)
            coefs.append(coef)
        if last:
            coef = summed(coefs)
            share = lax.dot_general(coef, pv_path, (((0,), (1,)), ((), ())), precision=high)
            share = share.reshape(pv_count, rhs // pv_count, -1)
            share, other = tied(share, other)
            share = halved(share)
        path = pv_path if level < pv_levels else pu_path
        last_rows = rows // pu_count if last else 0
        left, path = merge(level, left, other, sketch, path, last_rows)
        if level < pv_levels:
            pv_path = path
        else:
            pu_path = path

    share, left = tied(share, left)
    far_index = pv_index // 2
    mine = lax.dynamic_index_in_dim(share, far_index, 0, keepdims=False)
    parts = [mine]
    for by in range(1, pv_count // 2):
        give = lax.dynamic_index_in_dim(share, far_index ^ by, 0, keepdims=False)
        parts.append(from_partner(give, "pv", 2 * by))
    root_coef = lax.dot_general(summed(parts), pu_path, (((1,), (1,)), ((), ())), precision=high)
    root_coef = summed([root_coef] + [from_partner(root_coef, "pu", by) for by in range(1, pu_count)])
    far_field = lax.dot_general(left, root_coef, (((0,), (1,)), ((), ())), precision=high)
    return (corrected, far_field)


def solution(mesh):
    in_specs = (
        P("pu", "pv", None, None),
        P("pu", "pv", None, None, None),
        P("pu", "pv", None),
        P("pu", "pv", None, None),
        P("pu", "pv", None, None),
        P(),
        P(),
    )
    out_specs = (P("pu", "pv", None, None), P("pu", "pv"))
    return jax.shard_map(
        per_device, mesh=mesh, in_specs=in_specs, out_specs=out_specs, check_vma=False
    )
```

```python
import functools

import jax
import jax.numpy as jnp
from jax import lax
from jax.experimental import pallas as pl
from jax.experimental.pallas import tpu as pltpu
from jax.sharding import PartitionSpec as P

high = lax.Precision.HIGH
empty_slot = 9
near_vmem = 17 * 1024 * 1024
merge_vmem = 8 * 1024 * 1024


def dot_t(a, b, dims, precision=None):
    return lax.dot_general(
        a, b, (dims, ((), ())), precision=precision, preferred_element_type=jnp.float32
    )


def split_dot(a, b, dims):
    return dot_t(a, b, dims, high)


def in_hbm(value):
    return pltpu.with_memory_space_constraint(value, pltpu.HBM)


def cost(microseconds):
    return pl.CostEstimate(flops=int(microseconds * 1.1e9), bytes_accessed=0, transcendentals=0)


def near_kernel(plan, n_src, nb_hbm, near_hbm, right_hbm, *refs):
    steps, spans, parts = plan
    srcs = refs[:n_src]
    out_ref, coef_ref, nb_ref, ext_ref, near_ref, right_ref, stage_ref, sems, out_sems, nb_sem = refs[-10:]
    step = pl.program_id(0)
    count = len(parts)
    links = pltpu.make_async_copy(nb_hbm, nb_ref, nb_sem)

    def fetch(at_step):
        found = []
        for index, (needed, views) in enumerate(spans):
            if needed == at_step:
                source, target = views(srcs, ext_ref)
                found.append(pltpu.make_async_copy(source, target, sems.at[index]))
        for part, (row, by, col, *_) in enumerate(parts):
            at = len(spans) + 2 * (at_step * count + part)
            for offset, source, target in ((0, near_hbm, near_ref), (1, right_hbm, right_ref)):
                found.append(
                    pltpu.make_async_copy(
                        source.at[row + by * at_step, col()], target.at[at_step, part], sems.at[at + offset]
                    )
                )
        return found

    def send(place, at_step, part):
        row, by, col = parts[part][:3]
        return pltpu.make_async_copy(
            stage_ref.at[place, part], out_ref.at[row + by * at_step, col()], out_sems.at[place, part]
        )

    @pl.when(step == 0)
    def _():
        links.start()
        for at_step in range(steps):
            for copy in fetch(at_step):
                copy.start()
        links.wait()

    for at_step in range(steps):

        @pl.when(step == at_step)
        def _():
            for copy in fetch(at_step):
                copy.wait()

    place = lax.rem(step, 2)

    @pl.when(step >= 2)
    def _():
        for part in range(count):
            send(place, step - 2, part).wait()

    rhs = ext_ref.shape[-1]
    tile = 256 if rhs % 256 == 0 else rhs
    for part, (row, by, col, ext_row, ext_by, middle) in enumerate(parts):
        centre = ext_row + ext_by * step
        weights = []
        places = []
        for slot in range(near_ref.shape[2]):
            link = nb_ref[row + by * step, col(), slot]
            there = jnp.minimum(link, empty_slot - 1)
            weight = near_ref[step, part, slot]
            weights.append(jnp.where(link < empty_slot, weight, jnp.zeros_like(weight)))
            places.append((centre - 1 + lax.div(there, 3), middle - 1 + lax.rem(there, 3)))
        weights = jnp.concatenate(weights, axis=1)
        for at in range(0, rhs, tile):
            values = [ext_ref[i, j, :, at : at + tile] for i, j in places]
            total = jnp.dot(weights, jnp.concatenate(values, axis=0), preferred_element_type=jnp.float32)
            own = ext_ref[centre, middle, :, at : at + tile].astype(jnp.float32)
            stage_ref[place, part, :, at : at + tile] = (own + total).astype(jnp.bfloat16)
        send(place, step, part).start()
    rights = jnp.concatenate([right_ref[step, part] for part in range(count)], axis=0)
    blocks = jnp.concatenate([stage_ref[place, part] for part in range(count)], axis=0)
    coef = dot_t(rights, blocks, ((0,), (0,)))

    @pl.when(step == 0)
    def _():
        coef_ref[...] = coef

    @pl.when(step > 0)
    def _():
        coef_ref[...] += coef

    @pl.when(step == steps - 1)
    def _():
        for at_step in range(max(steps - 2, 0), steps):
            for part in range(count):
                send(at_step % 2, at_step, part).wait()


def near_part(sources, plan, ext_shape, near_blocks, far_right, neighbours, prior, time):
    steps, spans, parts = plan
    count = len(parts)
    gu, gv, slots, size, _ = near_blocks.shape
    rhs = sources[0].shape[-1]
    rank = far_right.shape[-1]
    args = [neighbours, near_blocks, far_right, *sources]
    args = [in_hbm(value) if at < 3 or value.ndim > 3 else value for at, value in enumerate(args)]
    aliases = {}
    if prior is not None:
        aliases = {len(args): 0}
        args.append(prior)
    held = pl.BlockSpec(memory_space=pltpu.HBM)
    return pl.pallas_call(
        functools.partial(near_kernel, plan, len(sources)),
        grid=(steps,),
        in_specs=[held] * 3
        + [held if source.ndim == 4 else pl.BlockSpec(memory_space=pl.ANY) for source in sources]
        + [held] * len(aliases),
        out_specs=[held, pl.BlockSpec((rank, rhs), lambda i: (0, 0))],
        scratch_shapes=[
            pltpu.SMEM(neighbours.shape, jnp.int32),
            pltpu.VMEM((*ext_shape, size, rhs), jnp.bfloat16),
            pltpu.VMEM((steps, count, slots, size, size), jnp.bfloat16),
            pltpu.VMEM((steps, count, size, rank), jnp.bfloat16),
            pltpu.VMEM((2, count, size, rhs), jnp.bfloat16),
            pltpu.SemaphoreType.DMA((len(spans) + 2 * steps * count,)),
            pltpu.SemaphoreType.DMA((2, count)),
            pltpu.SemaphoreType.DMA,
        ],
        out_shape=[
            jax.ShapeDtypeStruct((gu, gv, size, rhs), jnp.bfloat16),
            jax.ShapeDtypeStruct((rank, rhs), jnp.float32),
        ],
        input_output_aliases=aliases,
        cost_estimate=cost(time),
        compiler_params=pltpu.CompilerParams(
            dimension_semantics=("arbitrary",), vmem_limit_bytes=near_vmem
        ),
    )(*args)


def odd(axis):
    return lax.rem(lax.axis_index(axis), 2)


def row_span(row, ext_row):
    return lambda srcs, ext: (srcs[0].at[row], ext.at[ext_row])


def near_middle(density, near_blocks, far_right, neighbours, prior):
    gu, gv = density.shape[:2]
    spans = [(max(row - 2, 0), row_span(row, row)) for row in range(gu)]
    parts = [(1, 1, lambda col=col: col, 1, 1, col) for col in range(1, gv - 1)]
    plan = (gu - 2, spans, parts)
    return near_part((density,), plan, (gu, gv), near_blocks, far_right, neighbours, prior, 0.5)


def near_rows(density, pu_near, pu_far, near_blocks, far_right, neighbours, prior):
    gu, gv = density.shape[:2]
    spans = [(at, row_span(row, ext_row)) for at, row, ext_row in ((0, 0, 1), (0, 1, 2), (1, gu - 2, 3), (1, gu - 1, 4))]
    spans.append((0, lambda srcs, ext: (srcs[1], ext.at[5 * (1 - odd("pu"))])))
    spans.append((0, lambda srcs, ext: (srcs[2], ext.at[5 * odd("pu")])))
    parts = [(0, gu - 1, lambda col=col: col, 1, 3, col) for col in range(1, gv - 1)]
    plan = (2, spans, parts)
    return near_part((density, pu_near, pu_far), plan, (6, gv), near_blocks, far_right, neighbours, prior, 0.5)


def near_columns(density, pu_near, pu_far, corner_near, corner_far, beside, ends, mids, near_blocks, far_right, neighbours, prior):
    gu, gv = density.shape[:2]
    per_step = 2
    spans = []
    parts = []

    def near_row():
        return (gu + 1) * (1 - odd("pu"))

    def far_row():
        return (gu + 1) * odd("pu")

    for far in (0, 1):

        def left_side(far=far):
            return 1 - odd("pv") if far else odd("pv")

        def inner(source, at, ext_row, far=far, left_side=left_side):
            def views(srcs, ext):
                view = srcs[source]
                if at is not None:
                    view = view.at[at]
                from_cols = pl.ds((gv - 2) * (1 - left_side()), 2)
                return view.at[from_cols], ext.at[ext_row(), pl.ds(3 * far + left_side(), 2)]

            return views

        def outer(source, at, ext_row, far=far, left_side=left_side):
            return lambda srcs, ext: (srcs[source].at[at], ext.at[ext_row(), 3 * far + 2 * (1 - left_side())])

        for row in range(gu):
            at = max((row - 1) // per_step, 0)
            here = lambda row=row: row + 1
            spans.append((at, inner(0, row, here)))
            if not far:
                spans.append((at, outer(5, row, here)))
            elif row in (0, gu - 1):
                spans.append((at, outer(6, min(row, 1), here)))
            else:
                spans.append((at, outer(7, row - 1, here)))
        spans.append((0, inner(1, None, near_row)))
        spans.append((0, inner(2, None, far_row)))
        spans.append((0, outer(3, far, near_row)))
        spans.append((0, outer(4, far, far_row)))
        col = lambda left_side=left_side: (gv - 1) * (1 - left_side())
        parts += [(row, per_step, col, row + 1, per_step, 3 * far + 1) for row in range(per_step)]
    plan = (gu // per_step, spans, parts)
    sources = (density, pu_near, pu_far, corner_near, corner_far, beside, ends, mids)
    return near_part(sources, plan, (gu + 2, 6), near_blocks, far_right, neighbours, prior, 0.5)


def run_copies(pairs, sems):
    copies = [
        pltpu.make_async_copy(source, target, sems.at[index])
        for index, (source, target) in enumerate(pairs)
    ]
    for copy in copies:
        copy.start()
    return copies


def corners_kernel(beside, ends, to_near, to_far):
    low = odd("pu")
    rows = beside.shape[0]
    for target, last in ((to_near, 1 - low), (to_far, low)):
        target[0] = beside[(rows - 1) * last]
        target[1] = ends[last]


def patch_corners(beside, ends):
    whole = pl.BlockSpec(memory_space=pltpu.VMEM)
    return pl.pallas_call(
        corners_kernel,
        in_specs=[whole, whole],
        out_specs=[whole, whole],
        out_shape=[jax.ShapeDtypeStruct(ends.shape, ends.dtype)] * 2,
        cost_estimate=cost(0.7),
        compiler_params=pltpu.CompilerParams(vmem_limit_bytes=merge_vmem),
    )(beside, ends)


def reciprocal(value):
    guess = pl.reciprocal(value, approx=True)
    return guess * (2.0 - value * guess)


def eliminate(w_k, w_e):
    size = w_k.shape[0]
    step = 32
    tile = 8
    sub = lax.broadcasted_iota(jnp.int32, (tile, size), 0)

    def spread(value, row):
        return jnp.broadcast_to(value[row : row + 1, :], (tile, size))

    for base in range(0, size, step):
        count = step // tile
        k_rows = [w_k[base + tile * r : base + tile * (r + 1), :] for r in range(count)]
        e_rows = [w_e[base + tile * r : base + tile * (r + 1), :] for r in range(count)]
        for q in range(count):
            at = base + tile * q
            cols = {
                (r, k): jnp.broadcast_to(k_rows[r][:, at + k : at + k + 1], (tile, size))
                for r in range(q, count)
                for k in range(tile)
            }
            k_done = k_rows[q]
            e_done = e_rows[q]
            for k in range(0, tile, 2):
                a = spread(cols[q, k], k)
                b = spread(cols[q, k], k + 1)
                c = spread(cols[q, k + 1], k + 1)
                det = a * c - b * b
                inverse = reciprocal(det)

                def solved(one, two):
                    return (c * one - b * two) * inverse, (a * two - b * one) * inverse

                k_one, k_two = spread(k_rows[q], k), spread(k_rows[q], k + 1)
                e_one, e_two = spread(e_rows[q], k), spread(e_rows[q], k + 1)
                k_solved = solved(k_one, k_two)
                e_solved = solved(e_one, e_two)
                links = {
                    m: solved(spread(cols[q, k], m), spread(cols[q, k + 1], m)) for m in range(k + 2, tile)
                }
                root = lax.rsqrt(a)
                second = lax.rsqrt(det) * a * root
                slope = b * root * root
                k_done = jnp.where(sub == k, k_one * root, k_done)
                e_done = jnp.where(sub == k, e_one * root, e_done)
                k_done = jnp.where(sub == k + 1, (k_two - slope * k_one) * second, k_done)
                e_done = jnp.where(sub == k + 1, (e_two - slope * e_one) * second, e_done)
                for r in range(q, count):
                    one, two = cols[r, k], cols[r, k + 1]
                    if r == q:
                        if k + 2 == tile:
                            continue
                        one = jnp.where(sub > k + 1, one, 0.0)
                        two = jnp.where(sub > k + 1, two, 0.0)
                    for m in range(k + 2, tile):
                        cols[r, m] = cols[r, m] - (one * links[m][0] + two * links[m][1])
                    k_rows[r] = k_rows[r] - (one * k_solved[0] + two * k_solved[1])
                    e_rows[r] = e_rows[r] - (one * e_solved[0] + two * e_solved[1])
            k_rows[q] = k_done
            e_rows[q] = e_done
        e_now = jnp.concatenate(e_rows, axis=0)
        w_e[base : base + step, :] = e_now
        if base + step < size:
            k_now = jnp.concatenate(k_rows, axis=0)
            k_hi = k_now.astype(jnp.bfloat16)
            k_lo = (k_now - k_hi.astype(jnp.float32)).astype(jnp.bfloat16)
            e_hi = e_now.astype(jnp.bfloat16)
            e_lo = (e_now - e_hi.astype(jnp.float32)).astype(jnp.bfloat16)
            lhs = jnp.concatenate([k_hi, k_hi, k_lo], axis=0)
            hi = jnp.concatenate([k_hi, e_hi], axis=1)
            lo = jnp.concatenate([k_lo, e_lo], axis=1)
            fall = dot_t(lhs, jnp.concatenate([hi, lo, hi], axis=0), ((0,), (0,)))
            w_k[base + step :, :] -= fall[base + step :, :size]
            w_e[base + step :, :] -= fall[base + step :, size:]


tail_lanes = 128


def encode(value, key, out_ref):
    cols = value.shape[1]
    top = jnp.max(jnp.abs(value), axis=1, keepdims=True)
    power = jnp.clip(jnp.floor(jnp.log2(32000.0 / jnp.maximum(top, 1e-30))), -60.0, 60.0)
    scaled = jnp.floor(value * jnp.exp2(power) + 0.5)
    out_ref[:, :cols] = scaled.astype(jnp.int32).astype(jnp.int16)
    lanes = lax.broadcasted_iota(jnp.int32, (value.shape[0], tail_lanes), 1)
    out_ref[:, cols:] = jnp.where(lanes < tail_lanes // 2, power, key).astype(jnp.int32).astype(jnp.int16)


def decode(ref):
    cols = ref.shape[1] - tail_lanes
    tail = ref[:, cols:].astype(jnp.int32).astype(jnp.float32)
    value = ref[:, :cols].astype(jnp.int32).astype(jnp.float32) * jnp.exp2(-tail[:, :1])
    return value, tail[:, tail_lanes - 1 :]


def leaf_kernel(counts, order_hbm, value_hbm, sketch_hbm, code_ref, sketch_ref, order, value, sketch, sems):
    pairs = [(value_hbm.at[0, 0], value), (order_hbm, order), (sketch_hbm, sketch)]
    for copy in run_copies(pairs, sems):
        copy.wait()
    key = order[lax.axis_index("pu") * counts[1] + lax.axis_index("pv")]
    encode(jnp.transpose(value[...]), key.astype(jnp.float32), code_ref)
    sketch_ref[...] = jnp.transpose(sketch[...])


def coded_leaf(value, sketch, order, counts):
    rows, cols = value.shape[2:]
    whole = pl.BlockSpec(memory_space=pltpu.VMEM)
    held = pl.BlockSpec(memory_space=pltpu.HBM)
    return pl.pallas_call(
        functools.partial(leaf_kernel, counts),
        in_specs=[held] * 3,
        out_specs=[whole] * 2,
        out_shape=[
            jax.ShapeDtypeStruct((cols, rows + tail_lanes), jnp.int16),
            jax.ShapeDtypeStruct(sketch.shape[::-1], jnp.float32),
        ],
        scratch_shapes=[
            pltpu.SMEM(order.shape, jnp.int32),
            pltpu.VMEM((rows, cols), jnp.float32),
            pltpu.VMEM(sketch.shape, jnp.float32),
            pltpu.SemaphoreType.DMA((3,)),
        ],
        cost_estimate=cost(1.5),
        compiler_params=pltpu.CompilerParams(vmem_limit_bytes=merge_vmem),
    )(in_hbm(order), in_hbm(value), in_hbm(sketch))


def edges_kernel(density, beside, ends, mids, pu_near, pu_far, sems):
    gu, gv = density.shape[:2]
    near_col = (gv - 1) * (1 - odd("pv"))
    far_col = (gv - 1) * odd("pv")
    pairs = [(density.at[(gu - 1) * odd("pu"), col], pu_far.at[col]) for col in range(gv)]
    pairs += [(density.at[(gu - 1) * (1 - odd("pu")), col], pu_near.at[col]) for col in range(gv)]
    pairs += [(density.at[row, near_col], beside.at[row]) for row in range(gu)]
    pairs += [(density.at[(gu - 1) * row, far_col], ends.at[row]) for row in range(2)]
    pairs += [(density.at[row + 1, far_col], mids.at[row]) for row in range(gu - 2)]
    for copy in run_copies(pairs, sems):
        copy.wait()


def patch_edges(density):
    gu, gv, size, rhs = density.shape
    blocks = (gu, 2, gu - 2, gv, gv)
    return pl.pallas_call(
        edges_kernel,
        in_specs=[pl.BlockSpec(memory_space=pltpu.HBM)],
        out_specs=[pl.BlockSpec(memory_space=pltpu.VMEM)] * len(blocks),
        out_shape=[jax.ShapeDtypeStruct((count, size, rhs), density.dtype) for count in blocks],
        scratch_shapes=[pltpu.SemaphoreType.DMA((2 * gu + 2 * gv,))],
        cost_estimate=cost(2.5),
        compiler_params=pltpu.CompilerParams(vmem_limit_bytes=merge_vmem),
    )(in_hbm(density))


natural = ((1,), (0,))


def merge_kernel(has_path, last, mine_ref, other_ref, sketch_ref, *refs):
    if has_path:
        path_ref, *refs = refs
    left_ref, new_path_ref, w_k, w_e, z_ref = refs
    rank = mine_ref.shape[0]
    mine, my_key = decode(mine_ref)
    other, other_key = decode(other_ref)
    lead = my_key < other_key
    z_ref[:rank, :] = jnp.where(lead, mine, other)
    z_ref[rank:, :] = jnp.where(lead, other, mine)
    stacked = z_ref[...]
    sketch = sketch_ref[...]
    gram = split_dot(stacked, stacked, ((1,), (1,)))
    reduced = split_dot(sketch, gram, natural)
    w_k[...] = split_dot(reduced, sketch, ((1,), (1,)))
    rows = lax.broadcasted_iota(jnp.int32, (rank, rank), 0)
    cols = lax.broadcasted_iota(jnp.int32, (rank, rank), 1)
    w_e[...] = jnp.where(rows == cols, 1.0, 0.0)
    own = jnp.where(lead, reduced[:, :rank], reduced[:, rank:])
    if has_path:
        own = split_dot(own, path_ref[...], natural)
    eliminate(w_k, w_e)
    inverse = w_e[...]
    mixed = split_dot(inverse, sketch, natural)
    if last:
        count = left_ref.shape[1]
        part = z_ref[:, pl.ds(pl.multiple_of(lax.axis_index("pu") * count, 128), count)]
        left_ref[...] = split_dot(mixed, part, natural)
    else:
        encode(split_dot(mixed, z_ref[...], natural), jnp.minimum(my_key, other_key), left_ref)
    new_path_ref[...] = split_dot(inverse, own, natural)


def merge(level, mine, other, sketch, path, last_rows):
    rank, cols = mine.shape
    whole = pl.BlockSpec(memory_space=pltpu.VMEM)
    paths = () if path is None else (path,)
    if last_rows:
        left = jax.ShapeDtypeStruct((rank, last_rows), jnp.float32)
    else:
        left = jax.ShapeDtypeStruct(mine.shape, jnp.int16)
    return pl.pallas_call(
        functools.partial(merge_kernel, bool(paths), bool(last_rows)),
        in_specs=[whole, whole, whole] + [whole] * len(paths),
        out_specs=[whole, whole],
        out_shape=[left, jax.ShapeDtypeStruct((rank, rank), jnp.float32)],
        scratch_shapes=[
            pltpu.VMEM((rank, rank), jnp.float32),
            pltpu.VMEM((rank, rank), jnp.float32),
            pltpu.VMEM((2 * rank, cols - tail_lanes), jnp.float32),
        ],
        cost_estimate=cost((9, 1.5)[level] if level < 2 else 0.5),
        compiler_params=pltpu.CompilerParams(vmem_limit_bytes=merge_vmem),
    )(mine, other, sketch, *paths)


def from_partner(value, axis, mask):
    pairs = [(source, source ^ mask) for source in range(lax.axis_size(axis))]
    return lax.ppermute(value, axis, pairs)


def summed(values):
    return functools.reduce(lambda a, b: a + b, values)


def swapped(value, axis, far):
    count = lax.axis_size(axis)
    pairs = []
    for low in range(int(far), count - 1, 2):
        pairs += [(low, low + 1), (low + 1, low)]
    return lax.ppermute(value, axis, pairs)


def tied(*values):
    return lax.optimization_barrier(values)


def per_device(density, near_blocks, neighbours, far_right, far_left, sketch, patch_order):
    pu_count = lax.axis_size("pu")
    pv_count = lax.axis_size("pv")
    pv_index = lax.axis_index("pv")
    rhs = density.shape[3]
    pv_levels = pv_count.bit_length() - 1
    pu_levels = pu_count.bit_length() - 1
    levels = pv_levels + pu_levels

    def partner(value, level):
        if level < pv_levels:
            return from_partner(value, "pv", 1 << level)
        return from_partner(value, "pu", 1 << level - pv_levels)

    def halved(share):
        bit = pv_index & 1
        pairs = share.reshape(share.shape[0] // 2, 2, *share.shape[1:])
        keep = lax.dynamic_index_in_dim(pairs, bit, 1, keepdims=False)
        give = lax.dynamic_index_in_dim(pairs, 1 - bit, 1, keepdims=False)
        return keep + from_partner(give, "pv", 1)

    rows = far_left.shape[2]
    left, sketch = coded_leaf(far_left, sketch, patch_order, (pu_count, pv_count))
    other = partner(left, 0)
    density, left = tied(density, left)
    beside, ends, mids, pu_near, pu_far = patch_edges(density)
    beside = swapped(beside, "pv", False)
    pu_near = swapped(pu_near, "pu", False)
    pu_far = swapped(pu_far, "pu", True)

    coefs = []
    corrected = share = None
    pv_path = pu_path = None
    for level in range(levels):
        last = level == levels - 1
        coef = None
        if level:
            other = partner(left, level)
        if level in (1, 2) or last:
            links, left = tied(neighbours, left)
        if level == 1:
            corrected, coef = near_middle(density, near_blocks, far_right, links, corrected)
        elif level == 2:
            ends, mids, left = tied(ends, mids, left)
            ends = swapped(ends, "pv", True)
            mids = swapped(mids, "pv", True)
            corrected, coef = near_rows(density, pu_near, pu_far, near_blocks, far_right, links, corrected)
        elif last:
            corner_near, corner_far = patch_corners(beside, ends)
            corner_near = swapped(corner_near, "pu", False)
            corner_far = swapped(corner_far, "pu", True)
            corrected, coef = near_columns(
                density,
                pu_near,
                pu_far,
                corner_near,
                corner_far,
                beside,
                ends,
                mids,
                near_blocks,
                far_right,
                links,
                corrected,
            )
        if coef is not None:
            other, coef = tied(other, coef)
            coefs.append(coef)
        if last:
            coef = summed(coefs)
            share = lax.dot_general(coef, pv_path, (((0,), (1,)), ((), ())), precision=high)
            share = share.reshape(pv_count, rhs // pv_count, -1)
            share, other = tied(share, other)
            share = halved(share)
        path = pv_path if level < pv_levels else pu_path
        last_rows = rows // pu_count if last else 0
        left, path = merge(level, left, other, sketch, path, last_rows)
        if level < pv_levels:
            pv_path = path
        else:
            pu_path = path

    share, left = tied(share, left)
    far_index = pv_index // 2
    mine = lax.dynamic_index_in_dim(share, far_index, 0, keepdims=False)
    parts = [mine]
    for by in range(1, pv_count // 2):
        give = lax.dynamic_index_in_dim(share, far_index ^ by, 0, keepdims=False)
        parts.append(from_partner(give, "pv", 2 * by))
    root_coef = lax.dot_general(summed(parts), pu_path, (((1,), (1,)), ((), ())), precision=high)
    root_coef = summed([root_coef] + [from_partner(root_coef, "pu", by) for by in range(1, pu_count)])
    far_field = lax.dot_general(left, root_coef, (((0,), (1,)), ((), ())), precision=high)
    return (corrected, far_field)


def solution(mesh):
    in_specs = (
        P("pu", "pv", None, None),
        P("pu", "pv", None, None, None),
        P("pu", "pv", None),
        P("pu", "pv", None, None),
        P("pu", "pv", None, None),
        P(),
        P(),
    )
    out_specs = (P("pu", "pv", None, None), P("pu", "pv"))
    return jax.shard_map(
        per_device, mesh=mesh, in_specs=in_specs, out_specs=out_specs, check_vma=False
    )
```

```python
import functools

import jax
import jax.numpy as jnp
from jax import lax
from jax.experimental import pallas as pl
from jax.experimental.pallas import tpu as pltpu
from jax.sharding import PartitionSpec as P

high = lax.Precision.HIGH
empty_slot = 9
near_vmem = 17 * 1024 * 1024
merge_vmem = 8 * 1024 * 1024


def dot_t(a, b, dims, precision=None):
    return lax.dot_general(
        a, b, (dims, ((), ())), precision=precision, preferred_element_type=jnp.float32
    )


def split_dot(a, b, dims):
    return dot_t(a, b, dims, high)


def in_hbm(value):
    return pltpu.with_memory_space_constraint(value, pltpu.HBM)


def cost(microseconds):
    return pl.CostEstimate(flops=int(microseconds * 1.1e9), bytes_accessed=0, transcendentals=0)


def near_kernel(plan, n_src, nb_hbm, near_hbm, right_hbm, *refs):
    steps, spans, parts = plan
    srcs = refs[:n_src]
    out_ref, coef_ref, nb_ref, ext_ref, near_ref, right_ref, stage_ref, sems, out_sems, nb_sem = refs[-10:]
    step = pl.program_id(0)
    count = len(parts)
    links = pltpu.make_async_copy(nb_hbm, nb_ref, nb_sem)

    def fetch(at_step):
        found = []
        for index, (needed, views) in enumerate(spans):
            if needed == at_step:
                source, target = views(srcs, ext_ref)
                found.append(pltpu.make_async_copy(source, target, sems.at[index]))
        for part, (row, by, col, *_) in enumerate(parts):
            at = len(spans) + 2 * (at_step * count + part)
            for offset, source, target in ((0, near_hbm, near_ref), (1, right_hbm, right_ref)):
                found.append(
                    pltpu.make_async_copy(
                        source.at[row + by * at_step, col()], target.at[at_step, part], sems.at[at + offset]
                    )
                )
        return found

    def send(place, at_step, part):
        row, by, col = parts[part][:3]
        return pltpu.make_async_copy(
            stage_ref.at[place, part], out_ref.at[row + by * at_step, col()], out_sems.at[place, part]
        )

    @pl.when(step == 0)
    def _():
        links.start()
        for at_step in range(steps):
            for copy in fetch(at_step):
                copy.start()
        links.wait()

    for at_step in range(steps):

        @pl.when(step == at_step)
        def _():
            for copy in fetch(at_step):
                copy.wait()

    place = lax.rem(step, 2)

    @pl.when(step >= 2)
    def _():
        for part in range(count):
            send(place, step - 2, part).wait()

    rhs = ext_ref.shape[-1]
    tile = 256 if rhs % 256 == 0 else rhs
    for part, (row, by, col, ext_row, ext_by, middle) in enumerate(parts):
        centre = ext_row + ext_by * step
        weights = []
        places = []
        for slot in range(near_ref.shape[2]):
            link = nb_ref[row + by * step, col(), slot]
            there = jnp.minimum(link, empty_slot - 1)
            weight = near_ref[step, part, slot]
            weights.append(jnp.where(link < empty_slot, weight, jnp.zeros_like(weight)))
            places.append((centre - 1 + lax.div(there, 3), middle - 1 + lax.rem(there, 3)))
        weights = jnp.concatenate(weights, axis=1)
        for at in range(0, rhs, tile):
            values = [ext_ref[i, j, :, at : at + tile] for i, j in places]
            total = jnp.dot(weights, jnp.concatenate(values, axis=0), preferred_element_type=jnp.float32)
            own = ext_ref[centre, middle, :, at : at + tile].astype(jnp.float32)
            stage_ref[place, part, :, at : at + tile] = (own + total).astype(jnp.bfloat16)
        send(place, step, part).start()
    rights = jnp.concatenate([right_ref[step, part] for part in range(count)], axis=0)
    blocks = jnp.concatenate([stage_ref[place, part] for part in range(count)], axis=0)
    coef = dot_t(rights, blocks, ((0,), (0,)))

    @pl.when(step == 0)
    def _():
        coef_ref[...] = coef

    @pl.when(step > 0)
    def _():
        coef_ref[...] += coef

    @pl.when(step == steps - 1)
    def _():
        for at_step in range(max(steps - 2, 0), steps):
            for part in range(count):
                send(at_step % 2, at_step, part).wait()


def near_part(sources, plan, ext_shape, near_blocks, far_right, neighbours, prior, time):
    steps, spans, parts = plan
    count = len(parts)
    gu, gv, slots, size, _ = near_blocks.shape
    rhs = sources[0].shape[-1]
    rank = far_right.shape[-1]
    args = [neighbours, near_blocks, far_right, *sources]
    args = [in_hbm(value) if at < 3 or value.ndim > 3 else value for at, value in enumerate(args)]
    aliases = {}
    if prior is not None:
        aliases = {len(args): 0}
        args.append(prior)
    held = pl.BlockSpec(memory_space=pltpu.HBM)
    return pl.pallas_call(
        functools.partial(near_kernel, plan, len(sources)),
        grid=(steps,),
        in_specs=[held] * 3
        + [held if source.ndim == 4 else pl.BlockSpec(memory_space=pl.ANY) for source in sources]
        + [held] * len(aliases),
        out_specs=[held, pl.BlockSpec((rank, rhs), lambda i: (0, 0))],
        scratch_shapes=[
            pltpu.SMEM(neighbours.shape, jnp.int32),
            pltpu.VMEM((*ext_shape, size, rhs), jnp.bfloat16),
            pltpu.VMEM((steps, count, slots, size, size), jnp.bfloat16),
            pltpu.VMEM((steps, count, size, rank), jnp.bfloat16),
            pltpu.VMEM((2, count, size, rhs), jnp.bfloat16),
            pltpu.SemaphoreType.DMA((len(spans) + 2 * steps * count,)),
            pltpu.SemaphoreType.DMA((2, count)),
            pltpu.SemaphoreType.DMA,
        ],
        out_shape=[
            jax.ShapeDtypeStruct((gu, gv, size, rhs), jnp.bfloat16),
            jax.ShapeDtypeStruct((rank, rhs), jnp.float32),
        ],
        input_output_aliases=aliases,
        cost_estimate=cost(time),
        compiler_params=pltpu.CompilerParams(
            dimension_semantics=("arbitrary",), vmem_limit_bytes=near_vmem
        ),
    )(*args)


def odd(axis):
    return lax.rem(lax.axis_index(axis), 2)


def row_span(row, ext_row):
    return lambda srcs, ext: (srcs[0].at[row], ext.at[ext_row])


def near_middle(density, near_blocks, far_right, neighbours, prior):
    gu, gv = density.shape[:2]
    spans = [(max(row - 2, 0), row_span(row, row)) for row in range(gu)]
    parts = [(1, 1, lambda col=col: col, 1, 1, col) for col in range(1, gv - 1)]
    plan = (gu - 2, spans, parts)
    return near_part((density,), plan, (gu, gv), near_blocks, far_right, neighbours, prior, 0.5)


def near_rows(density, pu_near, pu_far, near_blocks, far_right, neighbours, prior):
    gu, gv = density.shape[:2]
    spans = [(at, row_span(row, ext_row)) for at, row, ext_row in ((0, 0, 1), (0, 1, 2), (1, gu - 2, 3), (1, gu - 1, 4))]
    spans.append((0, lambda srcs, ext: (srcs[1], ext.at[5 * (1 - odd("pu"))])))
    spans.append((0, lambda srcs, ext: (srcs[2], ext.at[5 * odd("pu")])))
    parts = [(0, gu - 1, lambda col=col: col, 1, 3, col) for col in range(1, gv - 1)]
    plan = (2, spans, parts)
    return near_part((density, pu_near, pu_far), plan, (6, gv), near_blocks, far_right, neighbours, prior, 0.5)


def near_column(far, density, pu_near, pu_far, corner_near, corner_far, halo, near_blocks, far_right, neighbours, prior):
    gu, gv = density.shape[:2]
    per_step = 3
    spans = []

    def near_row():
        return (gu + 1) * (1 - odd("pu"))

    def far_row():
        return (gu + 1) * odd("pu")

    def left_side():
        return 1 - odd("pv") if far else odd("pv")

    def inner(source, at, ext_row):
        def views(srcs, ext):
            view = srcs[source]
            if at is not None:
                view = view.at[at]
            return view.at[pl.ds((gv - 2) * (1 - left_side()), 2)], ext.at[ext_row(), pl.ds(left_side(), 2)]

        return views

    def outer(source, at, ext_row):
        return lambda srcs, ext: (srcs[source].at[at], ext.at[ext_row(), 2 * (1 - left_side())])

    for row in range(gu):
        at = max((row - 1) // per_step, 0)
        here = lambda row=row: row + 1
        spans.append((at, inner(0, row, here)))
        if len(halo) == 1:
            spans.append((at, outer(5, row, here)))
        elif row in (0, gu - 1):
            spans.append((at, outer(5, min(row, 1), here)))
        else:
            spans.append((at, outer(6, row - 1, here)))
    spans.append((0, inner(1, None, near_row)))
    spans.append((0, inner(2, None, far_row)))
    spans.append((0, outer(3, far, near_row)))
    spans.append((0, outer(4, far, far_row)))
    col = lambda: (gv - 1) * (1 - left_side())
    parts = [(row, per_step, col, row + 1, per_step, 1) for row in range(per_step)]
    plan = (gu // per_step, spans, parts)
    sources = (density, pu_near, pu_far, corner_near, corner_far, *halo)
    return near_part(sources, plan, (gu + 2, 3), near_blocks, far_right, neighbours, prior, 0.5)


def run_copies(pairs, sems):
    copies = [
        pltpu.make_async_copy(source, target, sems.at[index])
        for index, (source, target) in enumerate(pairs)
    ]
    for copy in copies:
        copy.start()
    return copies


def corners_kernel(beside, ends, to_near, to_far):
    low = odd("pu")
    rows = beside.shape[0]
    for target, last in ((to_near, 1 - low), (to_far, low)):
        target[0] = beside[(rows - 1) * last]
        target[1] = ends[last]


def patch_corners(beside, ends):
    whole = pl.BlockSpec(memory_space=pltpu.VMEM)
    return pl.pallas_call(
        corners_kernel,
        in_specs=[whole, whole],
        out_specs=[whole, whole],
        out_shape=[jax.ShapeDtypeStruct(ends.shape, ends.dtype)] * 2,
        cost_estimate=cost(0.7),
        compiler_params=pltpu.CompilerParams(vmem_limit_bytes=merge_vmem),
    )(beside, ends)


def reciprocal(value):
    guess = pl.reciprocal(value, approx=True)
    return guess * (2.0 - value * guess)


def eliminate(w_k, w_e):
    size = w_k.shape[0]
    step = 32
    tile = 8
    sub = lax.broadcasted_iota(jnp.int32, (tile, size), 0)

    def spread(value, row):
        return jnp.broadcast_to(value[row : row + 1, :], (tile, size))

    for base in range(0, size, step):
        count = step // tile
        k_rows = [w_k[base + tile * r : base + tile * (r + 1), :] for r in range(count)]
        e_rows = [w_e[base + tile * r : base + tile * (r + 1), :] for r in range(count)]
        for q in range(count):
            at = base + tile * q
            cols = {
                (r, k): jnp.broadcast_to(k_rows[r][:, at + k : at + k + 1], (tile, size))
                for r in range(q, count)
                for k in range(tile)
            }
            k_done = k_rows[q]
            e_done = e_rows[q]
            for k in range(0, tile, 2):
                a = spread(cols[q, k], k)
                b = spread(cols[q, k], k + 1)
                c = spread(cols[q, k + 1], k + 1)
                det = a * c - b * b
                inverse = reciprocal(det)

                def solved(one, two):
                    return (c * one - b * two) * inverse, (a * two - b * one) * inverse

                k_one, k_two = spread(k_rows[q], k), spread(k_rows[q], k + 1)
                e_one, e_two = spread(e_rows[q], k), spread(e_rows[q], k + 1)
                k_solved = solved(k_one, k_two)
                e_solved = solved(e_one, e_two)
                links = {
                    m: solved(spread(cols[q, k], m), spread(cols[q, k + 1], m)) for m in range(k + 2, tile)
                }
                root = lax.rsqrt(a)
                second = lax.rsqrt(det) * a * root
                slope = b * root * root
                k_done = jnp.where(sub == k, k_one * root, k_done)
                e_done = jnp.where(sub == k, e_one * root, e_done)
                k_done = jnp.where(sub == k + 1, (k_two - slope * k_one) * second, k_done)
                e_done = jnp.where(sub == k + 1, (e_two - slope * e_one) * second, e_done)
                for r in range(q, count):
                    one, two = cols[r, k], cols[r, k + 1]
                    if r == q:
                        if k + 2 == tile:
                            continue
                        one = jnp.where(sub > k + 1, one, 0.0)
                        two = jnp.where(sub > k + 1, two, 0.0)
                    for m in range(k + 2, tile):
                        cols[r, m] = cols[r, m] - (one * links[m][0] + two * links[m][1])
                    k_rows[r] = k_rows[r] - (one * k_solved[0] + two * k_solved[1])
                    e_rows[r] = e_rows[r] - (one * e_solved[0] + two * e_solved[1])
            k_rows[q] = k_done
            e_rows[q] = e_done
        e_now = jnp.concatenate(e_rows, axis=0)
        w_e[base : base + step, :] = e_now
        if base + step < size:
            k_now = jnp.concatenate(k_rows, axis=0)
            k_hi = k_now.astype(jnp.bfloat16)
            k_lo = (k_now - k_hi.astype(jnp.float32)).astype(jnp.bfloat16)
            e_hi = e_now.astype(jnp.bfloat16)
            e_lo = (e_now - e_hi.astype(jnp.float32)).astype(jnp.bfloat16)
            lhs = jnp.concatenate([k_hi, k_hi, k_lo], axis=0)
            k_rhs = jnp.concatenate([k_hi, k_lo, k_hi], axis=0)
            e_rhs = jnp.concatenate([e_hi, e_lo, e_hi], axis=0)
            k_fall = dot_t(lhs, k_rhs, ((0,), (0,)))
            e_fall = dot_t(lhs, e_rhs, ((0,), (0,)))
            w_k[base + step :, :] -= k_fall[base + step :, :]
            w_e[base + step :, :] -= e_fall[base + step :, :]


tail_lanes = 128


def encode(value, key, out_ref):
    cols = value.shape[1]
    top = jnp.max(jnp.abs(value), axis=1, keepdims=True)
    power = jnp.clip(jnp.floor(jnp.log2(32000.0 / jnp.maximum(top, 1e-30))), -60.0, 60.0)
    scaled = jnp.floor(value * jnp.exp2(power) + 0.5)
    out_ref[:, :cols] = scaled.astype(jnp.int32).astype(jnp.int16)
    lanes = lax.broadcasted_iota(jnp.int32, (value.shape[0], tail_lanes), 1)
    out_ref[:, cols:] = jnp.where(lanes < tail_lanes // 2, power, key).astype(jnp.int32).astype(jnp.int16)


def decode(ref):
    cols = ref.shape[1] - tail_lanes
    tail = ref[:, cols:].astype(jnp.int32).astype(jnp.float32)
    value = ref[:, :cols].astype(jnp.int32).astype(jnp.float32) * jnp.exp2(-tail[:, :1])
    return value, tail[:, tail_lanes - 1 :]


def leaf_kernel(counts, order_hbm, value_hbm, sketch_hbm, code_ref, sketch_ref, order, value, sketch, sems):
    pairs = [(value_hbm.at[0, 0], value), (order_hbm, order), (sketch_hbm, sketch)]
    for copy in run_copies(pairs, sems):
        copy.wait()
    key = order[lax.axis_index("pu") * counts[1] + lax.axis_index("pv")]
    encode(jnp.transpose(value[...]), key.astype(jnp.float32), code_ref)
    sketch_ref[...] = jnp.transpose(sketch[...])


def coded_leaf(value, sketch, order, counts):
    rows, cols = value.shape[2:]
    whole = pl.BlockSpec(memory_space=pltpu.VMEM)
    held = pl.BlockSpec(memory_space=pltpu.HBM)
    return pl.pallas_call(
        functools.partial(leaf_kernel, counts),
        in_specs=[held] * 3,
        out_specs=[whole] * 2,
        out_shape=[
            jax.ShapeDtypeStruct((cols, rows + tail_lanes), jnp.int16),
            jax.ShapeDtypeStruct(sketch.shape[::-1], jnp.float32),
        ],
        scratch_shapes=[
            pltpu.SMEM(order.shape, jnp.int32),
            pltpu.VMEM((rows, cols), jnp.float32),
            pltpu.VMEM(sketch.shape, jnp.float32),
            pltpu.SemaphoreType.DMA((3,)),
        ],
        cost_estimate=cost(1.5),
        compiler_params=pltpu.CompilerParams(vmem_limit_bytes=merge_vmem),
    )(in_hbm(order), in_hbm(value), in_hbm(sketch))


def edges_kernel(density, beside, ends, mids, pu_near, pu_far, sems):
    gu, gv = density.shape[:2]
    near_col = (gv - 1) * (1 - odd("pv"))
    far_col = (gv - 1) * odd("pv")
    pairs = [(density.at[(gu - 1) * odd("pu"), col], pu_far.at[col]) for col in range(gv)]
    pairs += [(density.at[(gu - 1) * (1 - odd("pu")), col], pu_near.at[col]) for col in range(gv)]
    pairs += [(density.at[row, near_col], beside.at[row]) for row in range(gu)]
    pairs += [(density.at[(gu - 1) * row, far_col], ends.at[row]) for row in range(2)]
    pairs += [(density.at[row + 1, far_col], mids.at[row]) for row in range(gu - 2)]
    for copy in run_copies(pairs, sems):
        copy.wait()


def patch_edges(density):
    gu, gv, size, rhs = density.shape
    blocks = (gu, 2, gu - 2, gv, gv)
    return pl.pallas_call(
        edges_kernel,
        in_specs=[pl.BlockSpec(memory_space=pltpu.HBM)],
        out_specs=[pl.BlockSpec(memory_space=pltpu.VMEM)] * len(blocks),
        out_shape=[jax.ShapeDtypeStruct((count, size, rhs), density.dtype) for count in blocks],
        scratch_shapes=[pltpu.SemaphoreType.DMA((2 * gu + 2 * gv,))],
        cost_estimate=cost(2.5),
        compiler_params=pltpu.CompilerParams(vmem_limit_bytes=merge_vmem),
    )(in_hbm(density))


natural = ((1,), (0,))


def merge_kernel(has_path, last, mine_ref, other_ref, sketch_ref, *refs):
    if has_path:
        path_ref, *refs = refs
    left_ref, new_path_ref, w_k, w_e, z_ref = refs
    rank = mine_ref.shape[0]
    mine, my_key = decode(mine_ref)
    other, other_key = decode(other_ref)
    lead = my_key < other_key
    z_ref[:rank, :] = jnp.where(lead, mine, other)
    z_ref[rank:, :] = jnp.where(lead, other, mine)
    stacked = z_ref[...]
    sketch = sketch_ref[...]
    gram = split_dot(stacked, stacked, ((1,), (1,)))
    reduced = split_dot(sketch, gram, natural)
    w_k[...] = split_dot(reduced, sketch, ((1,), (1,)))
    rows = lax.broadcasted_iota(jnp.int32, (rank, rank), 0)
    cols = lax.broadcasted_iota(jnp.int32, (rank, rank), 1)
    w_e[...] = jnp.where(rows == cols, 1.0, 0.0)
    own = jnp.where(lead, reduced[:, :rank], reduced[:, rank:])
    if has_path:
        own = split_dot(own, path_ref[...], natural)
    eliminate(w_k, w_e)
    inverse = w_e[...]
    mixed = split_dot(inverse, sketch, natural)
    if last:
        count = left_ref.shape[1]
        part = z_ref[:, pl.ds(pl.multiple_of(lax.axis_index("pu") * count, 128), count)]
        left_ref[...] = split_dot(mixed, part, natural)
    else:
        encode(split_dot(mixed, z_ref[...], natural), jnp.minimum(my_key, other_key), left_ref)
    new_path_ref[...] = split_dot(inverse, own, natural)


def merge(level, mine, other, sketch, path, last_rows):
    rank, cols = mine.shape
    whole = pl.BlockSpec(memory_space=pltpu.VMEM)
    paths = () if path is None else (path,)
    if last_rows:
        left = jax.ShapeDtypeStruct((rank, last_rows), jnp.float32)
    else:
        left = jax.ShapeDtypeStruct(mine.shape, jnp.int16)
    return pl.pallas_call(
        functools.partial(merge_kernel, bool(paths), bool(last_rows)),
        in_specs=[whole, whole, whole] + [whole] * len(paths),
        out_specs=[whole, whole],
        out_shape=[left, jax.ShapeDtypeStruct((rank, rank), jnp.float32)],
        scratch_shapes=[
            pltpu.VMEM((rank, rank), jnp.float32),
            pltpu.VMEM((rank, rank), jnp.float32),
            pltpu.VMEM((2 * rank, cols - tail_lanes), jnp.float32),
        ],
        cost_estimate=cost((9, 1.5)[level] if level < 2 else 0.5),
        compiler_params=pltpu.CompilerParams(vmem_limit_bytes=merge_vmem),
    )(mine, other, sketch, *paths)


def from_partner(value, axis, mask):
    pairs = [(source, source ^ mask) for source in range(lax.axis_size(axis))]
    return lax.ppermute(value, axis, pairs)


def summed(values):
    return functools.reduce(lambda a, b: a + b, values)


def swapped(value, axis, far):
    count = lax.axis_size(axis)
    pairs = []
    for low in range(int(far), count - 1, 2):
        pairs += [(low, low + 1), (low + 1, low)]
    return lax.ppermute(value, axis, pairs)


def tied(*values):
    return lax.optimization_barrier(values)


def per_device(density, near_blocks, neighbours, far_right, far_left, sketch, patch_order):
    pu_count = lax.axis_size("pu")
    pv_count = lax.axis_size("pv")
    rhs = density.shape[3]
    pv_levels = pv_count.bit_length() - 1
    pu_levels = pu_count.bit_length() - 1
    levels = pv_levels + pu_levels

    def partner(value, level):
        if level < pv_levels:
            return from_partner(value, "pv", 1 << level)
        return from_partner(value, "pu", 1 << level - pv_levels)

    rows = far_left.shape[2]
    left, sketch = coded_leaf(far_left, sketch, patch_order, (pu_count, pv_count))
    other = partner(left, 0)
    density, left = tied(density, left)
    beside, ends, mids, pu_near, pu_far = patch_edges(density)
    beside = swapped(beside, "pv", False)
    pu_near = swapped(pu_near, "pu", False)
    pu_far = swapped(pu_far, "pu", True)

    coefs = []
    corrected = share = None
    pv_path = pu_path = None
    for level in range(levels):
        last = level == levels - 1
        coef = None
        if level:
            other = partner(left, level)
        if level in (1, 2) or last:
            links, left = tied(neighbours, left)
        if level == 1:
            corrected, coef = near_middle(density, near_blocks, far_right, links, corrected)
        elif level == 2:
            ends, mids, left = tied(ends, mids, left)
            ends = swapped(ends, "pv", True)
            mids = swapped(mids, "pv", True)
            corrected, coef = near_rows(density, pu_near, pu_far, near_blocks, far_right, links, corrected)
        elif last:
            corner_near, corner_far = patch_corners(beside, ends)
            corner_near = swapped(corner_near, "pu", False)
            corner_far = swapped(corner_far, "pu", True)
            halo = (density, pu_near, pu_far, corner_near, corner_far)
            corrected, coef = near_column(0, *halo, (beside,), near_blocks, far_right, links, corrected)
            coefs.append(coef)
            corrected, coef = near_column(1, *halo, (ends, mids), near_blocks, far_right, links, corrected)
        if coef is not None:
            other, coef = tied(other, coef)
            coefs.append(coef)
        if last:
            coef = summed(coefs)
            share = lax.dot_general(coef, pv_path, (((0,), (1,)), ((), ())), precision=high)
            share = share.reshape(pv_count, rhs // pv_count, -1)
            share, other = tied(share, other)
            share = lax.psum_scatter(share, "pv", scatter_dimension=0)
        path = pv_path if level < pv_levels else pu_path
        last_rows = rows // pu_count if last else 0
        left, path = merge(level, left, other, sketch, path, last_rows)
        if level < pv_levels:
            pv_path = path
        else:
            pu_path = path

    root_coef = lax.dot_general(share, pu_path, (((1,), (1,)), ((), ())), precision=high)
    root_coef = summed([root_coef] + [from_partner(root_coef, "pu", by) for by in range(1, pu_count)])
    far_field = lax.dot_general(left, root_coef, (((0,), (1,)), ((), ())), precision=high)
    return (corrected, far_field)


def solution(mesh):
    in_specs = (
        P("pu", "pv", None, None),
        P("pu", "pv", None, None, None),
        P("pu", "pv", None),
        P("pu", "pv", None, None),
        P("pu", "pv", None, None),
        P(),
        P(),
    )
    out_specs = (P("pu", "pv", None, None), P("pu", "pv"))
    return jax.shard_map(
        per_device, mesh=mesh, in_specs=in_specs, out_specs=out_specs, check_vma=False
    )
```
